32 devices in a mesh: dp: 32 (over z, y, x, core).
Axes of the slice: x: 2, y: 2, z: 4, core: 2. Of those that a mesh axis runs over, the one named last changes fastest.
Arguments:
- tokens: bfloat16 [32, 512, 640], P('dp'), may hold values from -27 to 27
- segment_ids: int32 [32, 512], P('dp'), may hold values from 0 to 3, never falling along the last dimension, each value on 1 to 256 neighbouring positions
- cotangent: bfloat16 [32, 512, 640], P('dp'), may hold values from -6 to 6
- query_weight: float32 [640, 1024], P('dp'), may hold values from -0.25 to 0.25
- keyval_weight: float32 [640, 512], P('dp'), may hold values from -0.25 to 0.25
- output_weight: float32 [1024, 640], P('dp'), may hold values from -0.1875 to 0.1875
- gateup_weight: float32 [640, 2, 2048], P('dp'), may hold values from -0.25 to 0.25
- down_weight: float32 [2048, 640], P('dp'), may hold values from -0.125 to 0.125
- norm_gains: float32 [4, 640], P(None, 'dp'), may hold values from -0.12 to 0.12
- qknorm_gains: float32 [2, 256], P(None, 'dp'), may hold values from -0.12 to 0.12
- query_mean: float32 [640, 1024], P('dp'), may hold values from -80 to 80
- keyval_mean: float32 [640, 512], P('dp'), may hold values from -80 to 80
- output_mean: float32 [1024, 640], P('dp'), may hold values from -80 to 80
- gateup_mean: float32 [640, 2, 2048], P('dp'), may hold values from -80 to 80
- down_mean: float32 [2048, 640], P('dp'), may hold values from -80 to 80
- norm_mean: float32 [4, 640], P(None, 'dp'), may hold values from -80 to 80
- qknorm_mean: float32 [2, 256], P(None, 'dp'), may hold values from -80 to 80
- query_square: float32 [640, 1024], P('dp'), may hold values from 16.384 to 65.536
- keyval_square: float32 [640, 512], P('dp'), may hold values from 16.384 to 65.536
- output_square: float32 [1024, 640], P('dp'), may hold values from 16.384 to 65.536
- gateup_square: float32 [640, 2, 2048], P('dp'), may hold values from 16.384 to 65.536
- down_square: float32 [2048, 640], P('dp'), may hold values from 16.384 to 65.536
- norm_square: float32 [4, 640], P(None, 'dp'), may hold values from 16.384 to 65.536
- qknorm_square: float32 [2, 256], P(None, 'dp'), may hold values from 16.384 to 65.536
Outputs:
- result: bfloat16 [32, 512, 640], P('dp')
- input_grad: float32 [32, 512, 640], P('dp')
- query_grad: float32 [640, 1024], P('dp')
- keyval_grad: float32 [640, 512], P('dp')
- output_grad: float32 [1024, 640], P('dp')
- gateup_grad: float32 [640, 2, 2048], P('dp')
- down_grad: float32 [2048, 640], P('dp')
- norm_grad: float32 [4, 640], P(None, 'dp')
- qknorm_grad: float32 [2, 256], P(None, 'dp')
- query_new: float32 [640, 1024], P('dp')
- keyval_new: float32 [640, 512], P('dp')
- output_new: float32 [1024, 640], P('dp')
- gateup_new: float32 [640, 2, 2048], P('dp')
- down_new: float32 [2048, 640], P('dp')
- norm_new: float32 [4, 640], P(None, 'dp')
- qknorm_new: float32 [2, 256], P(None, 'dp')
- query_mean_new: float32 [640, 1024], P('dp')
- keyval_mean_new: float32 [640, 512], P('dp')
- output_mean_new: float32 [1024, 640], P('dp')
- gateup_mean_new: float32 [640, 2, 2048], P('dp')
- down_mean_new: float32 [2048, 640], P('dp')
- norm_mean_new: float32 [4, 640], P(None, 'dp')
- qknorm_mean_new: float32 [2, 256], P(None, 'dp')
- query_square_new: float32 [640, 1024], P('dp')
- keyval_square_new: float32 [640, 512], P('dp')
- output_square_new: float32 [1024, 640], P('dp')
- gateup_square_new: float32 [640, 2, 2048], P('dp')
- down_square_new: float32 [2048, 640], P('dp')
- norm_square_new: float32 [4, 640], P(None, 'dp')
- qknorm_square_new: float32 [2, 256], P(None, 'dp')
The draws below stay inside these ranges and needn't reach their ends.
Inputs may be any that keep to these rules, and one draw needn't show every extreme that they name: `segment_ids`: segment numbers never fall along a sequence; a document holds 1 to 256 tokens.
All inputs are finite; a program needn't handle non-finite values.
Results may differ from the reference program's by a relative error of at most 0.025.
Values may be sent and summed in bfloat16 or wider, within the bound.
No kernel may reach another device: no remote copies, remote signals or barrier semaphores. Data moves between devices by JAX's collectives and lax.ppermute only.
A program may use at most 128 MiB of HBM per device.

```python
import math
import jax
import jax.numpy as jnp
import numpy as np
from jax import lax

D = 640
HEADS = 4
HEAD_DIM = 256
FF = 2048
LENGTH = 512
STEP = 3
SEQS = 32
DOCS = 4


def draw_tokens(key, part):
    base = jax.random.truncated_normal(jax.random.fold_in(key, 31), -3.0, 3.0, (SEQS, LENGTH, D), jnp.float32)
    low_end = jnp.log(0.3)
    high_end = jnp.log(3.0)
    row_scale = jnp.exp(jax.random.uniform(jax.random.fold_in(key, 32), (SEQS, LENGTH, 1), jnp.float32, low_end, high_end))
    column_scale = jnp.exp(jax.random.uniform(jax.random.fold_in(key, 33), (1, 1, D), jnp.float32, low_end, high_end))
    return (base * row_scale * column_scale).astype(jnp.bfloat16)


def block_levels(rng, extent, pieces, low, largest):
    def one(axis_at, parts):
        draws = jax.random.uniform(jax.random.fold_in(jax.random.fold_in(rng, 6), axis_at), (parts,), jnp.float32, low / len(pieces), largest / len(pieces))
        return jnp.repeat(jnp.exp(draws), extent[axis_at] // parts).reshape((-1,) + (1,) * (len(extent) - axis_at - 1))

    gain = one(*pieces[0])
    for cut in pieces[1:]:
        gain = gain * one(*cut)
    return gain


def split_up(count, total, reach, skew):
    portions = [(1 << 20) // math.isqrt(grade ** skew) + 1 for grade in range(2, count + 1)]
    surplus, given = total - reach - (count - 1), [1] * (count - 1)
    while surplus > 0:
        movable = [i for i in range(count - 1) if given[i] < reach]
        whole, left = sum([portions[i] for i in movable]), surplus
        for i in movable:
            addition = min(reach - given[i], max(1, left * portions[i] // whole), surplus)
            given[i] = given[i] + addition
            surplus = surplus - addition
    return np.array([reach] + given)


def uneven_parts(rng, count, total, reach, skew):
    if count == 2:
        one = jax.random.randint(rng, (), max(1, total - reach), min(reach, total - 1) + 1)
        return jnp.stack([one, total - one])
    lengths = jnp.asarray(split_up(count, total, reach, skew), jnp.int32)
    twos = (count - 1) // 2
    donor, sink = lengths[1:1 + 2 * twos:2], lengths[2:2 + 2 * twos:2]
    slack = jnp.minimum(donor - 1, reach - sink)
    shifted = jax.random.randint(jax.random.fold_in(rng, 1), (twos,), 0, 1 << 20) % (slack + 1)
    lengths = lengths.at[1:1 + 2 * twos:2].set(donor - shifted).at[2:2 + 2 * twos:2].set(sink + shifted)
    return lengths[jax.random.permutation(jax.random.fold_in(rng, 2), count)]


def bell_draw(stream_key, shape, deviation, limit, shards=(), kind=jnp.bfloat16):
    entries = deviation * jax.random.normal(stream_key, shape, jnp.float32)
    if shards:
        entries = entries * block_levels(stream_key, shape, shards, -0.22, 0.18)
    return jnp.clip(entries, -limit, limit).astype(kind)


def setup_inputs(seed: int = 0) -> dict:
    keys = jax.random.split(jax.random.key(seed), 25)
    return {
        "tokens": draw_tokens(jax.random.fold_in(keys[24], 71), 0),
        "segment_ids": jax.vmap(lambda own: jnp.searchsorted(jnp.cumsum(uneven_parts(own, DOCS, LENGTH, LENGTH // 2, 2)), jnp.arange(LENGTH), side="right"))(jax.random.split(keys[1], SEQS)).reshape((SEQS, LENGTH)).astype(jnp.int32),
        "cotangent": bell_draw(keys[2], (SEQS, LENGTH, D), 1.0, 6.0, ((0, 32),)),
        "query_weight": bell_draw(keys[3], (D, HEADS * HEAD_DIM), D ** -0.5, 0.25, ((0, 32),), jnp.float32),
        "keyval_weight": bell_draw(keys[4], (D, 2 * HEAD_DIM), D ** -0.5, 0.25, ((0, 32),), jnp.float32),
        "output_weight": bell_draw(keys[5], (HEADS * HEAD_DIM, D), (HEADS * HEAD_DIM) ** -0.5, 0.1875, ((0, 32),), jnp.float32),
        "gateup_weight": bell_draw(keys[6], (D, 2, FF), D ** -0.5, 0.25, ((0, 32),), jnp.float32),
        "down_weight": bell_draw(keys[7], (FF, D), FF ** -0.5, 0.125, ((0, 32),), jnp.float32),
        "norm_gains": jnp.clip(jax.random.uniform(keys[8], (4, D), jnp.float32, -0.12, 0.12) * block_levels(keys[8], (4, D), ((1, 32),), -0.4, 0.0), -0.12, 0.12),
        "qknorm_gains": jnp.clip(jax.random.uniform(keys[9], (2, HEAD_DIM), jnp.float32, -0.12, 0.12) * block_levels(keys[9], (2, HEAD_DIM), ((1, 32),), -0.4, 0.0), -0.12, 0.12),
        "query_mean": bell_draw(keys[10], (D, HEADS * HEAD_DIM), (0.1 * (SEQS * LENGTH) ** 0.5), 80.0, ((0, 32),), jnp.float32),
        "keyval_mean": bell_draw(keys[11], (D, 2 * HEAD_DIM), (0.1 * (SEQS * LENGTH) ** 0.5), 80.0, ((0, 32),), jnp.float32),
        "output_mean": bell_draw(keys[12], (HEADS * HEAD_DIM, D), (0.1 * (SEQS * LENGTH) ** 0.5), 80.0, ((0, 32),), jnp.float32),
        "gateup_mean": bell_draw(keys[13], (D, 2, FF), (0.1 * (SEQS * LENGTH) ** 0.5), 80.0, ((0, 32),), jnp.float32),
        "down_mean": bell_draw(keys[14], (FF, D), (0.1 * (SEQS * LENGTH) ** 0.5), 80.0, ((0, 32),), jnp.float32),
        "norm_mean": bell_draw(keys[15], (4, D), (0.1 * (SEQS * LENGTH) ** 0.5), 80.0, ((1, 32),), jnp.float32),
        "qknorm_mean": bell_draw(keys[16], (2, HEAD_DIM), (0.1 * (SEQS * LENGTH) ** 0.5), 80.0, ((1, 32),), jnp.float32),
        "query_square": jnp.clip(jnp.exp(math.log(65.536) - 1.3862944 * jax.random.uniform(keys[17], (D, HEADS * HEAD_DIM), jnp.float32) ** block_levels(keys[17], (D, HEADS * HEAD_DIM), ((0, 32),), -0.2, 0.2)), 16.384, 65.536),
        "keyval_square": jnp.clip(jnp.exp(math.log(65.536) - 1.3862944 * jax.random.uniform(keys[18], (D, 2 * HEAD_DIM), jnp.float32) ** block_levels(keys[18], (D, 2 * HEAD_DIM), ((0, 32),), -0.2, 0.2)), 16.384, 65.536),
        "output_square": jnp.clip(jnp.exp(math.log(65.536) - 1.3862944 * jax.random.uniform(keys[19], (HEADS * HEAD_DIM, D), jnp.float32) ** block_levels(keys[19], (HEADS * HEAD_DIM, D), ((0, 32),), -0.2, 0.2)), 16.384, 65.536),
        "gateup_square": jnp.clip(jnp.exp(math.log(65.536) - 1.3862944 * jax.random.uniform(keys[20], (D, 2, FF), jnp.float32) ** block_levels(keys[20], (D, 2, FF), ((0, 32),), -0.2, 0.2)), 16.384, 65.536),
        "down_square": jnp.clip(jnp.exp(math.log(65.536) - 1.3862944 * jax.random.uniform(keys[21], (FF, D), jnp.float32) ** block_levels(keys[21], (FF, D), ((0, 32),), -0.2, 0.2)), 16.384, 65.536),
        "norm_square": jnp.clip(jnp.exp(math.log(65.536) - 1.3862944 * jax.random.uniform(keys[22], (4, D), jnp.float32) ** block_levels(keys[22], (4, D), ((1, 32),), -0.2, 0.2)), 16.384, 65.536),
        "qknorm_square": jnp.clip(jnp.exp(math.log(65.536) - 1.3862944 * jax.random.uniform(keys[23], (2, HEAD_DIM), jnp.float32) ** block_levels(keys[23], (2, HEAD_DIM), ((1, 32),), -0.2, 0.2)), 16.384, 65.536),
    }


norm_epsilon = 1e-06
beta_one = 0.9
beta_two = 0.999
learn_rate = 0.03
decay_coef = 0.1
adam_epsilon = 1e-08

def norm_apply(values, gain_vector):
    inverse = lax.rsqrt(lax.optimization_barrier(jnp.mean(values * values, axis=-1, keepdims=True)) + norm_epsilon)
    return values * inverse * (1.0 + gain_vector)

def gelu_product(gate_part, up_part):
    return jax.nn.gelu(gate_part, approximate=True) * up_part

def layer_sequence(tokens, segments, cotangent, rounded):
    query_round, keyval_round, output_round, gateup_round, down_round, main_gains, head_gains = rounded
    length = tokens.shape[0]
    score_scale = HEAD_DIM ** (-0.5)
    gateup_flat = gateup_round.reshape(D, 2 * FF)
    inputs = tokens.astype(jnp.float32)
    normed_in = norm_apply(inputs, main_gains[0]).astype(jnp.bfloat16)
    queries = jnp.dot(normed_in, query_round, preferred_element_type=jnp.float32).reshape(length, HEADS, HEAD_DIM)
    keyvals = jnp.dot(normed_in, keyval_round, preferred_element_type=jnp.float32)
    key_rows = keyvals[:, :HEAD_DIM]
    value_rows = keyvals[:, HEAD_DIM:]
    query_normed = norm_apply(queries, head_gains[0]).astype(jnp.bfloat16)
    key_normed = norm_apply(key_rows, head_gains[1]).astype(jnp.bfloat16)
    value_round = value_rows.astype(jnp.bfloat16)
    positions = jnp.arange(length)
    allowed = ((segments[:, None] == segments[None, :]) & (positions[None, :] <= positions[:, None]))[None]
    scores = jnp.einsum('qhd,kd->hqk', query_normed.astype(jnp.float32), key_normed.astype(jnp.float32)) * score_scale
    masked = jnp.where(allowed, scores, -1e+30)
    row_max = lax.optimization_barrier(jnp.max(masked, axis=-1, keepdims=True))
    row_total = lax.optimization_barrier(jnp.sum(jnp.where(allowed, jnp.exp(masked - row_max), 0.0), axis=-1, keepdims=True))
    log_total = row_max + jnp.log(row_total)
    soft_weights = jnp.where(allowed, jnp.exp(masked - log_total), 0.0)
    soft_round = soft_weights.astype(jnp.bfloat16)
    attended = jnp.einsum('hqk,kd->qhd', soft_round.astype(jnp.float32), value_round.astype(jnp.float32)).astype(jnp.bfloat16)
    attended_flat = attended.reshape(length, HEADS * HEAD_DIM)
    branch = jnp.dot(attended_flat, output_round, preferred_element_type=jnp.float32)
    middle = inputs + norm_apply(branch, main_gains[1])
    normed_mid = norm_apply(middle, main_gains[2]).astype(jnp.bfloat16)
    gate_up = jnp.dot(normed_mid, gateup_flat, preferred_element_type=jnp.float32)
    gate_part = gate_up[:, :FF]
    up_part = gate_up[:, FF:]
    hidden = gelu_product(gate_part, up_part).astype(jnp.bfloat16)
    down_out = jnp.dot(hidden, down_round, preferred_element_type=jnp.float32)
    result = (middle + norm_apply(down_out, main_gains[3])).astype(jnp.bfloat16)
    grad_out = cotangent.astype(jnp.float32)
    _, pull_back = jax.vjp(norm_apply, down_out, main_gains[3])
    grad_down_out, grad_gain_three = pull_back(grad_out)
    grad_down_round = grad_down_out.astype(jnp.bfloat16)
    grad_down = jnp.dot(hidden.T, grad_down_round, preferred_element_type=jnp.float32)
    grad_hidden = jnp.dot(grad_down_round, down_round.T, preferred_element_type=jnp.float32)
    _, pull_back = jax.vjp(gelu_product, gate_part, up_part)
    grad_gate, grad_up = pull_back(grad_hidden)
    grad_gate_up = jnp.concatenate([grad_gate, grad_up], axis=1).astype(jnp.bfloat16)
    grad_gateup = jnp.dot(normed_mid.T, grad_gate_up, preferred_element_type=jnp.float32).reshape(D, 2, FF)
    grad_normed_mid = jnp.dot(grad_gate_up, gateup_flat.T, preferred_element_type=jnp.float32)
    _, pull_back = jax.vjp(norm_apply, middle, main_gains[2])
    grad_mid_norm, grad_gain_two = pull_back(grad_normed_mid)
    grad_middle = grad_out + grad_mid_norm
    _, pull_back = jax.vjp(norm_apply, branch, main_gains[1])
    grad_branch, grad_gain_one = pull_back(grad_middle)
    grad_branch_round = grad_branch.astype(jnp.bfloat16)
    grad_output = jnp.dot(attended_flat.T, grad_branch_round, preferred_element_type=jnp.float32)
    grad_attended = jnp.dot(grad_branch_round, output_round.T, preferred_element_type=jnp.float32).reshape(length, HEADS, HEAD_DIM).astype(jnp.bfloat16)
    row_delta = lax.optimization_barrier(jnp.sum(grad_attended.astype(jnp.float32) * attended.astype(jnp.float32), axis=-1))
    grad_values = jnp.einsum('hqk,qhd->kd', soft_round.astype(jnp.float32), grad_attended.astype(jnp.float32))
    grad_soft = jnp.einsum('qhd,kd->hqk', grad_attended.astype(jnp.float32), value_round.astype(jnp.float32))
    grad_scores = (soft_weights * (grad_soft - row_delta.T[:, :, None]) * score_scale).astype(jnp.bfloat16)
    grad_query_normed = jnp.einsum('hqk,kd->qhd', grad_scores.astype(jnp.float32), key_normed.astype(jnp.float32))
    grad_key_normed = jnp.einsum('hqk,qhd->kd', grad_scores.astype(jnp.float32), query_normed.astype(jnp.float32))
    _, pull_back = jax.vjp(norm_apply, queries, head_gains[0])
    grad_queries, grad_head_zero = pull_back(grad_query_normed)
    _, pull_back = jax.vjp(norm_apply, key_rows, head_gains[1])
    grad_keys, grad_head_one = pull_back(grad_key_normed)
    grad_query_round = grad_queries.reshape(length, HEADS * HEAD_DIM).astype(jnp.bfloat16)
    grad_keyval_round = jnp.concatenate([grad_keys, grad_values], axis=1).astype(jnp.bfloat16)
    grad_query = jnp.dot(normed_in.T, grad_query_round, preferred_element_type=jnp.float32)
    grad_keyval = jnp.dot(normed_in.T, grad_keyval_round, preferred_element_type=jnp.float32)
    grad_normed_in = jnp.dot(grad_query_round, query_round.T, preferred_element_type=jnp.float32) + jnp.dot(grad_keyval_round, keyval_round.T, preferred_element_type=jnp.float32)
    _, pull_back = jax.vjp(norm_apply, inputs, main_gains[0])
    grad_in_norm, grad_gain_zero = pull_back(grad_normed_in)
    input_grad = grad_middle + grad_in_norm
    grad_gains = jnp.stack([grad_gain_zero, grad_gain_one, grad_gain_two, grad_gain_three])
    grad_heads = jnp.stack([grad_head_zero, grad_head_one])
    all_grads = (grad_query, grad_keyval, grad_output, grad_gateup, grad_down, grad_gains, grad_heads)
    return (result, input_grad, all_grads)

def adam_update(parameter, gradient, first_moment, second_moment, decay_value):
    first_new = beta_one * first_moment + (1.0 - beta_one) * gradient
    second_new = beta_two * second_moment + (1.0 - beta_two) * gradient * gradient
    first_hat = first_new / (1.0 - beta_one ** STEP)
    second_hat = second_new / (1.0 - beta_two ** STEP)
    parameter_new = parameter - learn_rate * first_hat / (jnp.sqrt(second_hat) + adam_epsilon) - learn_rate * decay_value * parameter
    return (parameter_new, first_new, second_new)

def reference(tokens, segment_ids, cotangent, query_weight, keyval_weight, output_weight, gateup_weight, down_weight, norm_gains, qknorm_gains, query_mean, keyval_mean, output_mean, gateup_mean, down_mean, norm_mean, qknorm_mean, query_square, keyval_square, output_square, gateup_square, down_square, norm_square, qknorm_square):
    parameters = (query_weight, keyval_weight, output_weight, gateup_weight, down_weight, norm_gains, qknorm_gains)
    firsts = (query_mean, keyval_mean, output_mean, gateup_mean, down_mean, norm_mean, qknorm_mean)
    seconds = (query_square, keyval_square, output_square, gateup_square, down_square, norm_square, qknorm_square)
    rounded = (query_weight.astype(jnp.bfloat16), keyval_weight.astype(jnp.bfloat16), output_weight.astype(jnp.bfloat16), gateup_weight.astype(jnp.bfloat16), down_weight.astype(jnp.bfloat16), lax.optimization_barrier(norm_gains.astype(jnp.bfloat16)).astype(jnp.float32), lax.optimization_barrier(qknorm_gains.astype(jnp.bfloat16)).astype(jnp.float32))
    zero_grads = tuple((jnp.zeros(parameter.shape, jnp.float32) for parameter in parameters))

    def scan_step(carried, seq_item):
        result_seq, input_seq, grads_seq = layer_sequence(seq_item[0], seq_item[1], seq_item[2], rounded)
        summed = tuple((left + right for left, right in zip(carried, grads_seq)))
        return (summed, (result_seq, input_seq))
    gradients, (result, input_grad) = lax.scan(scan_step, zero_grads, (tokens, segment_ids, cotangent))
    decays = (decay_coef, decay_coef, decay_coef, decay_coef, decay_coef, 0.0, 0.0)
    updates = [adam_update(parameters[place], gradients[place], firsts[place], seconds[place], decays[place]) for place in range(7)]
    news = tuple((update[0] for update in updates))
    first_news = tuple((update[1] for update in updates))
    second_news = tuple((update[2] for update in updates))
    return (result, input_grad) + tuple(gradients) + news + first_news + second_news
```

```python
import jax
import jax.numpy as jnp
import numpy as np
from jax import lax
from jax.experimental import pallas as pl
from jax.experimental.pallas import tpu as pltpu
from jax.sharding import PartitionSpec as P

STEP = 3
DIMS = (4, 2, 2, 2)
BF = jnp.bfloat16


def shift_perm(axis, amount):
    pairs = []
    for place in range(int(np.prod(DIMS))):
        spot = list(np.unravel_index(place, DIMS))
        spot[axis] = (spot[axis] + amount) % DIMS[axis]
        pairs.append((place, int(np.ravel_multi_index(spot, DIMS))))
    return pairs


def shift(values, axis, amount):
    return lax.ppermute(values, "dp", shift_perm(axis, amount))


def own_coords():
    place = lax.axis_index("dp")
    return place // 8, (place // 4) % 2, (place // 2) % 2, place % 2


def gather_pieces(block):
    near = [block] + [shift(block, 0, -step) for step in (1, 2, 3)]
    first = jnp.stack([near[0], near[1]])
    second = jnp.stack([near[2], near[3]])
    pair_a = jnp.stack([first, shift(first, 2, 1)])
    pair_b = jnp.stack([second, shift(second, 1, 1)])
    across_a = shift(pair_a, 1, 1)
    across_b = shift(pair_b, 2, 1)
    mine = [pair_a, across_a, pair_b, across_b]
    return mine + [shift(piece, 3, 1) for piece in mine]


def piece_spots(coords_ref):
    for group in range(8):
        far_core, kind = group // 4, group % 4
        for one in range(2):
            for two in range(2):
                if kind < 2:
                    gap = (two, kind, one)
                else:
                    gap = (2 + two, one, kind - 2)
                along = lax.rem(coords_ref[0] + gap[0], 4)
                upward = lax.rem(coords_ref[1] + gap[1], 2)
                sideways = lax.rem(coords_ref[2] + gap[2], 2)
                core = lax.rem(coords_ref[3] + far_core, 2)
                yield group, one, two, (along * 2 + upward) * 2 + sideways, core


def fetch_pieces(coords_ref, piece_refs, room, arrived):
    copies = []
    for group, one, two, chip, core in piece_spots(coords_ref):
        copies.append(
            pltpu.make_async_copy(
                piece_refs[group].at[one, two], room.at[core, chip], arrived
            )
        )
    for copy in copies:
        copy.start()
    for copy in copies:
        copy.wait()


def assemble_attention(coords_ref, *refs):
    piece_refs, (query_ref, keyval_ref, output_ref, gains_ref), (room, arrived) = (
        refs[:8],
        refs[8:12],
        refs[12:],
    )
    fetch_pieces(coords_ref, piece_refs, room, arrived)
    gains = jnp.zeros((8, 640), jnp.float32)
    for core in range(2):
        for chip in range(16):
            rows = slice(40 * chip, 40 * chip + 40)
            query_ref[rows, 512 * core : 512 * core + 512] = room[core, chip, :, 0:512]
            keyval_ref[rows, 256 * core : 256 * core + 256] = room[core, chip, :, 512:768]
            spot = 32 * (2 * chip + core)
            output_ref[spot : spot + 32, :] = room[core, chip, 0:32, 768:1408]
            gains = gains + room[core, chip, 32:40, 768:1408].astype(jnp.float32)
    gains_ref[...] = gains


def assemble_gateup(coords_ref, *refs):
    piece_refs, gateup_ref, (room, arrived) = refs[:8], refs[8], refs[9:]
    fetch_pieces(coords_ref, piece_refs, room, arrived)
    for core in range(2):
        for chip in range(16):
            gateup_ref[40 * chip : 40 * chip + 40, 2048 * core : 2048 * core + 2048] = room[core, chip]


def assemble_down(coords_ref, *refs):
    piece_refs, down_ref, (room, arrived) = refs[:8], refs[8], refs[9:]
    fetch_pieces(coords_ref, piece_refs, room, arrived)
    for core in range(2):
        for chip in range(16):
            spot = 64 * (2 * chip + core)
            down_ref[spot : spot + 64, :] = room[core, chip]


def run_assemble(kernel, coords, pieces, outs):
    return pl.pallas_call(
        kernel,
        out_shape=outs,
        in_specs=[pl.BlockSpec(memory_space=pltpu.SMEM)] + [pl.BlockSpec(memory_space=pl.ANY)] * 8,
        out_specs=jax.tree.map(lambda _: pl.BlockSpec(memory_space=pltpu.VMEM), outs),
        scratch_shapes=[
            pltpu.VMEM((2, 16) + pieces[0].shape[2:], BF),
            pltpu.SemaphoreType.DMA,
        ],
        compiler_params=pltpu.CompilerParams(vmem_limit_bytes=48 * 1024 * 1024),
    )(coords, *pieces)


def send_spots(coords_ref):
    for far_core in range(2):
        core = lax.rem(coords_ref[3] + far_core, 2)
        for group in range(2):
            for one in range(2):
                for two in range(2):
                    for three in range(2):
                        gap = (three, one, two) if group == 0 else (2 + three, two, one)
                        along = lax.rem(coords_ref[0] + gap[0], 4)
                        upward = lax.rem(coords_ref[1] + gap[1], 2)
                        sideways = lax.rem(coords_ref[2] + gap[2], 2)
                        chip = (along * 2 + upward) * 2 + sideways
                        yield 2 * far_core + group, one, two, three, chip, core


def post_pieces(coords_ref, room, out_refs, posted):
    copies = []
    for which, one, two, three, chip, core in send_spots(coords_ref):
        copies.append(
            pltpu.make_async_copy(
                room.at[core, chip], out_refs[which].at[one, two, three], posted
            )
        )
    for copy in copies:
        copy.start()
    for copy in copies:
        copy.wait()


def split_attention(coords_ref, query_ref, keyval_ref, output_ref, gains_ref, *refs):
    out_refs, (room, posted) = refs[:4], refs[4:]
    gains = gains_ref[...].astype(BF)
    for core in range(2):
        for chip in range(16):
            rows = slice(40 * chip, 40 * chip + 40)
            room[core, chip, :, 0:512] = query_ref[rows, 512 * core : 512 * core + 512].astype(BF)
            room[core, chip, :, 512:768] = keyval_ref[rows, 256 * core : 256 * core + 256].astype(BF)
            spot = 32 * (2 * chip + core)
            room[core, chip, 0:32, 768:1408] = output_ref[spot : spot + 32, :].astype(BF)
            room[core, chip, 32:40, 768:1408] = gains
    post_pieces(coords_ref, room, out_refs, posted)


def split_gateup(coords_ref, gateup_ref, *refs):
    out_refs, (room, posted) = refs[:4], refs[4:]
    for core in range(2):
        for chip in range(16):
            room[core, chip] = gateup_ref[
                40 * chip : 40 * chip + 40, 2048 * core : 2048 * core + 2048
            ].astype(BF)
    post_pieces(coords_ref, room, out_refs, posted)


def split_down(coords_ref, down_ref, *refs):
    out_refs, (room, posted) = refs[:4], refs[4:]
    for core in range(2):
        for chip in range(16):
            spot = 64 * (2 * chip + core)
            room[core, chip] = down_ref[spot : spot + 64, :].astype(BF)
    post_pieces(coords_ref, room, out_refs, posted)


def run_split(kernel, coords, grads, rows, columns):
    outs = [jax.ShapeDtypeStruct((2, 2, 2, rows, columns), BF)] * 4
    return pl.pallas_call(
        kernel,
        out_shape=outs,
        in_specs=[pl.BlockSpec(memory_space=pltpu.SMEM)]
        + [pl.BlockSpec(memory_space=pltpu.VMEM)] * len(grads),
        out_specs=[pl.BlockSpec(memory_space=pl.ANY)] * 4,
        scratch_shapes=[pltpu.VMEM((2, 16, rows, columns), BF), pltpu.SemaphoreType.DMA],
        compiler_params=pltpu.CompilerParams(vmem_limit_bytes=48 * 1024 * 1024),
    )(coords, *grads)


def wide(values):
    return values.astype(jnp.float32)


def scatter_pieces(keep_a, keep_b, send_a, send_b):
    got_a, got_b = shift(send_a, 3, 1), shift(send_b, 3, 1)
    far_a = shift((wide(keep_a[1]) + wide(got_a[1])).astype(BF), 1, 1)
    far_b = shift((wide(keep_b[1]) + wide(got_b[1])).astype(BF), 2, 1)
    sum_a = wide(keep_a[0]) + wide(got_a[0]) + wide(far_a)
    sum_b = wide(keep_b[0]) + wide(got_b[0]) + wide(far_b)
    side_a = shift(sum_a[1].astype(BF), 2, 1)
    side_b = shift(sum_b[1].astype(BF), 1, 1)
    last_a = sum_a[0] + wide(side_a)
    last_b = sum_b[0] + wide(side_b)
    total = last_a[0]
    total = total + wide(shift(last_a[1].astype(BF), 0, 1))
    total = total + wide(shift(last_b[0].astype(BF), 0, 2))
    total = total + wide(shift(last_b[1].astype(BF), 0, 3))
    return total


def swap_halves(core, low, high):
    return jnp.where(core == 0, high, low), jnp.where(core == 0, low, high)


def gather_all(query_round, keyval_round, output_round, gateup_round, down_round, gains, heads):
    along, upward, sideways, core = own_coords()
    coords = jnp.stack([along, upward, sideways, core]).astype(jnp.int32)
    low = jnp.concatenate([query_round[:, :512], keyval_round[:, :256], gateup_round[:, 0]], axis=1)
    high = jnp.concatenate([query_round[:, 512:], keyval_round[:, 256:], gateup_round[:, 1]], axis=1)
    away, keep = swap_halves(core, low, high)
    got = shift(away, 3, 1)
    both = jnp.concatenate(
        [jnp.where(core == 0, keep, got), jnp.where(core == 0, got, keep)], axis=0
    )
    place = lax.axis_index("dp")
    spread = jnp.zeros((8, 640), BF)
    spread = lax.dynamic_update_slice(spread, gains, (0, place * gains.shape[1]))
    spread = lax.dynamic_update_slice(spread, heads, (4, place * heads.shape[1]))
    block_a = jnp.concatenate([both[:, :768], jnp.concatenate([output_round, spread], axis=0)], axis=1)
    block_g = both[:, 768:]
    pieces_a = gather_pieces(block_a)
    pieces_g = gather_pieces(block_g)
    pieces_w = gather_pieces(down_round)
    shape = jax.ShapeDtypeStruct
    query_full, keyval_full, output_full, gains_full = run_assemble(
        assemble_attention,
        coords,
        pieces_a,
        [shape((640, 1024), BF), shape((640, 512), BF), shape((1024, 640), BF), shape((8, 640), jnp.float32)],
    )
    gateup_full = run_assemble(assemble_gateup, coords, pieces_g, shape((640, 4096), BF))
    down_full = run_assemble(assemble_down, coords, pieces_w, shape((2048, 640), BF))
    return query_full, keyval_full, output_full, gateup_full, down_full, gains_full[:4], gains_full[4:6, :256]


def scatter_all(grad_query, grad_keyval, grad_output, grad_gateup, grad_down, grad_gains, grad_heads):
    along, upward, sideways, core = own_coords()
    place = lax.axis_index("dp")
    coords = jnp.stack([along, upward, sideways, core]).astype(jnp.int32)
    down_grad = scatter_pieces(*run_split(split_down, coords, [grad_down], 64, 640))
    gateup_sum = scatter_pieces(*run_split(split_gateup, coords, [grad_gateup], 40, 2048))
    small = jnp.concatenate(
        [grad_gains, jnp.pad(grad_heads, ((0, 2), (0, 640 - grad_heads.shape[1])))], axis=0
    )
    rest = scatter_pieces(*run_split(split_attention, coords, [grad_query, grad_keyval, grad_output, small], 40, 1408))
    output_grad = rest[:32, 768:]
    norm_grad = lax.dynamic_slice(rest[32:36, 768:], (0, place * 20), (4, 20))
    qknorm_grad = lax.dynamic_slice(rest[36:38, 768:], (0, place * 8), (2, 8))
    both = jnp.concatenate([rest[:, :768], gateup_sum], axis=1)
    away, keep = swap_halves(core, both[:20], both[20:])
    got = shift(away, 3, 1)
    low, high = jnp.where(core == 0, keep, got), jnp.where(core == 0, got, keep)
    query_grad = jnp.concatenate([low[:, :512], high[:, :512]], axis=1)
    keyval_grad = jnp.concatenate([low[:, 512:768], high[:, 512:768]], axis=1)
    gateup_grad = jnp.stack([low[:, 768:], high[:, 768:]], axis=1)
    return query_grad, keyval_grad, output_grad, gateup_grad, down_grad, norm_grad, qknorm_grad


def gather_plain(query_round, keyval_round, output_round, gateup_round, down_round, gains_round, headgain_round):
    gateup_full = lax.all_gather(gateup_round, "dp", axis=0, tiled=True)
    return (
        lax.all_gather(query_round, "dp", axis=0, tiled=True),
        lax.all_gather(keyval_round, "dp", axis=0, tiled=True),
        lax.all_gather(output_round, "dp", axis=0, tiled=True),
        gateup_full.reshape(gateup_full.shape[0], -1),
        lax.all_gather(down_round, "dp", axis=0, tiled=True),
        lax.all_gather(gains_round, "dp", axis=1, tiled=True).astype(jnp.float32),
        lax.all_gather(headgain_round, "dp", axis=1, tiled=True).astype(jnp.float32),
    )


def scatter_plain(grad_query, grad_keyval, grad_output, grad_gateup, grad_down, grad_gains, grad_heads):
    rows = grad_gateup.shape[0]
    return (
        lax.psum_scatter(grad_query, "dp", scatter_dimension=0, tiled=True),
        lax.psum_scatter(grad_keyval, "dp", scatter_dimension=0, tiled=True),
        lax.psum_scatter(grad_output, "dp", scatter_dimension=0, tiled=True),
        lax.psum_scatter(grad_gateup.reshape(rows, 2, -1), "dp", scatter_dimension=0, tiled=True),
        lax.psum_scatter(grad_down, "dp", scatter_dimension=0, tiled=True),
        lax.psum_scatter(grad_gains, "dp", scatter_dimension=1, tiled=True),
        lax.psum_scatter(grad_heads, "dp", scatter_dimension=1, tiled=True),
    )


norm_epsilon = 1e-06
beta_one = 0.9
beta_two = 0.999
learn_rate = 0.03
decay_coef = 0.1
adam_epsilon = 1e-08


def norm_apply(values, gain_vector):
    inverse = lax.rsqrt(jnp.mean(values * values, axis=-1, keepdims=True) + norm_epsilon)
    return values * inverse * (1.0 + gain_vector)


def gelu_product(gate_part, up_part):
    return jax.nn.gelu(gate_part, approximate=True) * up_part


def block_scores(query_normed, key_normed, segments, row_start, row_stop, score_scale):
    positions = jnp.arange(row_stop)
    same_doc = segments[row_start:row_stop, None] == segments[None, :row_stop]
    causal = positions[None, :] <= positions[row_start:row_stop, None]
    allowed = (same_doc & causal)[None]
    scores = (
        jnp.einsum("qhd,kd->hqk", query_normed, key_normed, preferred_element_type=jnp.float32)
        * score_scale
    )
    return (jnp.where(allowed, scores, -1e30), allowed)


def attend_forward(query_normed, key_normed, value_round, segments, score_scale):
    length = query_normed.shape[0]
    block_rows = min(512, length)
    masked, allowed = block_scores(query_normed, key_normed, segments, 0, block_rows, score_scale)
    row_max = jnp.max(masked, axis=-1, keepdims=True)
    row_total = jnp.sum(jnp.where(allowed, jnp.exp(masked - row_max), 0.0), axis=-1, keepdims=True)
    log_total = row_max + jnp.log(row_total)
    soft_round = jnp.where(allowed, jnp.exp(masked - log_total), 0.0).astype(jnp.bfloat16)
    attended_block = jnp.einsum(
        "hqk,kd->qhd", soft_round, value_round, preferred_element_type=jnp.float32
    )
    attended_parts = attended_block.astype(jnp.bfloat16)
    total_parts = log_total[:, :, 0]
    return (attended_parts, total_parts)


def attend_backward(
    query_normed,
    key_normed,
    value_round,
    segments,
    log_totals,
    attended,
    grad_attended,
    score_scale,
):
    length = query_normed.shape[0]
    head_dim = key_normed.shape[1]
    block_rows = min(512, length)
    row_delta = jnp.sum(grad_attended.astype(jnp.float32) * attended.astype(jnp.float32), axis=-1)
    grad_key_sum = jnp.zeros((length, head_dim), jnp.float32)
    grad_value_sum = jnp.zeros((length, head_dim), jnp.float32)
    masked, allowed = block_scores(query_normed, key_normed, segments, 0, block_rows, score_scale)
    soft_weights = jnp.where(allowed, jnp.exp(masked - log_totals[:, 0:block_rows, None]), 0.0)
    soft_round = soft_weights.astype(jnp.bfloat16)
    grad_value_sum = grad_value_sum.at[:block_rows].add(
        jnp.einsum("hqk,qhd->kd", soft_round, grad_attended, preferred_element_type=jnp.float32)
    )
    grad_soft = jnp.einsum(
        "qhd,kd->hqk", grad_attended, value_round, preferred_element_type=jnp.float32
    )
    delta_block = row_delta.T[:, :, None]
    grad_scores = (soft_weights * (grad_soft - delta_block) * score_scale).astype(jnp.bfloat16)
    grad_query_parts = jnp.einsum(
        "hqk,kd->qhd", grad_scores, key_normed, preferred_element_type=jnp.float32
    )
    grad_key_sum = grad_key_sum.at[:block_rows].add(
        jnp.einsum("hqk,qhd->kd", grad_scores, query_normed, preferred_element_type=jnp.float32)
    )
    return (grad_query_parts, grad_key_sum, grad_value_sum)


def adam_update(parameter, gradient, first_moment, second_moment, decay_value):
    first_new = beta_one * first_moment + (1.0 - beta_one) * gradient
    second_new = beta_two * second_moment + (1.0 - beta_two) * gradient * gradient
    first_hat = first_new / (1.0 - beta_one**STEP)
    second_hat = second_new / (1.0 - beta_two**STEP)
    parameter_new = (
        parameter
        - learn_rate * first_hat / (jnp.sqrt(second_hat) + adam_epsilon)
        - learn_rate * decay_value * parameter
    )
    return (parameter_new, first_new, second_new)


def per_device(
    tokens,
    segment_ids,
    cotangent,
    query_weight,
    keyval_weight,
    output_weight,
    gateup_weight,
    down_weight,
    norm_gains,
    qknorm_gains,
    query_mean,
    keyval_mean,
    output_mean,
    gateup_mean,
    down_mean,
    norm_mean,
    qknorm_mean,
    query_square,
    keyval_square,
    output_square,
    gateup_square,
    down_square,
    norm_square,
    qknorm_square,
):
    query_round = query_weight.astype(jnp.bfloat16)
    keyval_round = keyval_weight.astype(jnp.bfloat16)
    output_round = output_weight.astype(jnp.bfloat16)
    gateup_round = gateup_weight.astype(jnp.bfloat16)
    down_round = down_weight.astype(jnp.bfloat16)
    gains_round = norm_gains.astype(jnp.bfloat16)
    headgain_round = qknorm_gains.astype(jnp.bfloat16)
    fast = lax.axis_size("dp") == 32
    gather, scatter = (gather_all, scatter_all) if fast else (gather_plain, scatter_plain)
    query_full, keyval_full, output_full, gateup_full, down_full, main_gains, head_gains = gather(
        query_round,
        keyval_round,
        output_round,
        gateup_round,
        down_round,
        gains_round,
        headgain_round,
    )
    seq_count, length, model_width = tokens.shape
    row_count = seq_count * length
    head_dim = head_gains.shape[1]
    head_count = query_full.shape[1] // head_dim
    hidden_units = gateup_full.shape[1] // 2
    score_scale = head_dim ** (-0.5)
    inputs = tokens.reshape(row_count, model_width).astype(jnp.float32)
    normed_in = norm_apply(inputs, main_gains[0]).astype(jnp.bfloat16)
    queries = jnp.dot(normed_in, query_full, preferred_element_type=jnp.float32).reshape(
        row_count, head_count, head_dim
    )
    keyvals = jnp.dot(normed_in, keyval_full, preferred_element_type=jnp.float32)
    key_rows = keyvals[:, :head_dim]
    value_rows = keyvals[:, head_dim:]
    query_normed = norm_apply(queries, head_gains[0]).astype(jnp.bfloat16)
    key_normed = norm_apply(key_rows, head_gains[1]).astype(jnp.bfloat16)
    value_round = value_rows.astype(jnp.bfloat16)
    seq_index = 0
    attended_seq, totals_seq = attend_forward(
        query_normed, key_normed, value_round, segment_ids[seq_index], score_scale
    )
    total_parts = [totals_seq]
    attended_flat = attended_seq.reshape(row_count, head_count * head_dim)
    branch = jnp.dot(attended_flat, output_full, preferred_element_type=jnp.float32)
    middle = inputs + norm_apply(branch, main_gains[1])
    normed_mid = norm_apply(middle, main_gains[2]).astype(jnp.bfloat16)
    gate_up = jnp.dot(
        normed_mid,
        gateup_full,
        preferred_element_type=jnp.float32,
    )
    gate_part = gate_up[:, :hidden_units]
    up_part = gate_up[:, hidden_units:]
    hidden = gelu_product(gate_part, up_part).astype(jnp.bfloat16)
    down_out = jnp.dot(hidden, down_full, preferred_element_type=jnp.float32)
    result = (middle + norm_apply(down_out, main_gains[3])).astype(jnp.bfloat16)
    query_back, keyval_back, output_back, gateup_back, down_back = (
        query_full,
        keyval_full,
        output_full,
        gateup_full,
        down_full,
    )
    gateup_flat = gateup_back
    grad_out = cotangent.reshape(row_count, model_width).astype(jnp.float32)
    _, pull_back = jax.vjp(norm_apply, down_out, main_gains[3])
    grad_down_out, grad_gain_three = pull_back(grad_out)
    grad_down_round = grad_down_out.astype(jnp.bfloat16)
    grad_down = jnp.dot(hidden.T, grad_down_round, preferred_element_type=jnp.float32)
    grad_hidden = jnp.dot(grad_down_round, down_back.T, preferred_element_type=jnp.float32)
    _, pull_back = jax.vjp(gelu_product, gate_part, up_part)
    grad_gate, grad_up = pull_back(grad_hidden)
    grad_gate_up = jnp.concatenate([grad_gate, grad_up], axis=1).astype(jnp.bfloat16)
    grad_gateup = jnp.dot(normed_mid.T, grad_gate_up, preferred_element_type=jnp.float32)
    grad_normed_mid = jnp.dot(grad_gate_up, gateup_flat.T, preferred_element_type=jnp.float32)
    _, pull_back = jax.vjp(norm_apply, middle, main_gains[2])
    grad_mid_norm, grad_gain_two = pull_back(grad_normed_mid)
    grad_middle = grad_out + grad_mid_norm
    _, pull_back = jax.vjp(norm_apply, branch, main_gains[1])
    grad_branch, grad_gain_one = pull_back(grad_middle)
    grad_branch_round = grad_branch.astype(jnp.bfloat16)
    grad_output = jnp.dot(attended_flat.T, grad_branch_round, preferred_element_type=jnp.float32)
    grad_attended = (
        jnp.dot(grad_branch_round, output_back.T, preferred_element_type=jnp.float32)
        .reshape(row_count, head_count, head_dim)
        .astype(jnp.bfloat16)
    )
    seq_index = 0
    grad_query_seq, grad_key_seq, grad_value_seq = attend_backward(
        query_normed,
        key_normed,
        value_round,
        segment_ids[seq_index],
        total_parts[seq_index],
        attended_seq,
        grad_attended,
        score_scale,
    )
    _, pull_back = jax.vjp(norm_apply, queries, head_gains[0])
    grad_queries, grad_head_zero = pull_back(grad_query_seq)
    _, pull_back = jax.vjp(norm_apply, key_rows, head_gains[1])
    grad_keys, grad_head_one = pull_back(grad_key_seq)
    grad_query_round = grad_queries.reshape(row_count, head_count * head_dim).astype(jnp.bfloat16)
    grad_keyval_round = jnp.concatenate([grad_keys, grad_value_seq], axis=1).astype(jnp.bfloat16)
    grad_query = jnp.dot(normed_in.T, grad_query_round, preferred_element_type=jnp.float32)
    grad_keyval = jnp.dot(normed_in.T, grad_keyval_round, preferred_element_type=jnp.float32)
    grad_normed_in = jnp.dot(
        grad_query_round, query_back.T, preferred_element_type=jnp.float32
    ) + jnp.dot(grad_keyval_round, keyval_back.T, preferred_element_type=jnp.float32)
    _, pull_back = jax.vjp(norm_apply, inputs, main_gains[0])
    grad_in_norm, grad_gain_zero = pull_back(grad_normed_in)
    input_grad = grad_middle + grad_in_norm
    grad_gains = jnp.stack([grad_gain_zero, grad_gain_one, grad_gain_two, grad_gain_three])
    grad_heads = jnp.stack([grad_head_zero, grad_head_one])
    gradients = scatter(
        grad_query, grad_keyval, grad_output, grad_gateup, grad_down, grad_gains, grad_heads
    )
    parameters = (
        query_weight,
        keyval_weight,
        output_weight,
        gateup_weight,
        down_weight,
        norm_gains,
        qknorm_gains,
    )
    firsts = (query_mean, keyval_mean, output_mean, gateup_mean, down_mean, norm_mean, qknorm_mean)
    seconds = (
        query_square,
        keyval_square,
        output_square,
        gateup_square,
        down_square,
        norm_square,
        qknorm_square,
    )
    decays = (decay_coef, decay_coef, decay_coef, decay_coef, decay_coef, 0.0, 0.0)
    updates = [
        adam_update(
            parameters[place], gradients[place], firsts[place], seconds[place], decays[place]
        )
        for place in range(7)
    ]
    news = tuple((update[0] for update in updates))
    first_news = tuple((update[1] for update in updates))
    second_news = tuple((update[2] for update in updates))
    result_out = result.reshape(seq_count, length, model_width)
    input_out = input_grad.reshape(seq_count, length, model_width)
    return (result_out, input_out) + gradients + news + first_news + second_news


def solution(mesh):
    in_specs = (
        P("dp", None, None),
        P("dp", None),
        P("dp", None, None),
        P("dp", None),
        P("dp", None),
        P("dp", None),
        P("dp", None, None),
        P("dp", None),
        P(None, "dp"),
        P(None, "dp"),
        P("dp", None),
        P("dp", None),
        P("dp", None),
        P("dp", None, None),
        P("dp", None),
        P(None, "dp"),
        P(None, "dp"),
        P("dp", None),
        P("dp", None),
        P("dp", None),
        P("dp", None, None),
        P("dp", None),
        P(None, "dp"),
        P(None, "dp"),
    )
    out_specs = (
        P("dp", None, None),
        P("dp", None, None),
        P("dp", None),
        P("dp", None),
        P("dp", None),
        P("dp", None, None),
        P("dp", None),
        P(None, "dp"),
        P(None, "dp"),
        P("dp", None),
        P("dp", None),
        P("dp", None),
        P("dp", None, None),
        P("dp", None),
        P(None, "dp"),
        P(None, "dp"),
        P("dp", None),
        P("dp", None),
        P("dp", None),
        P("dp", None, None),
        P("dp", None),
        P(None, "dp"),
        P(None, "dp"),
        P("dp", None),
        P("dp", None),
        P("dp", None),
        P("dp", None, None),
        P("dp", None),
        P(None, "dp"),
        P(None, "dp"),
    )
    return jax.shard_map(
        per_device, mesh=mesh, in_specs=in_specs, out_specs=out_specs, check_vma=False
    )
```

```python
import jax
import jax.numpy as jnp
import numpy as np
from jax import lax
from jax.experimental import pallas as pl
from jax.experimental.pallas import tpu as pltpu
from jax.sharding import PartitionSpec as P

STEP = 3
norm_epsilon = 1e-06
beta_one = 0.9
beta_two = 0.999
learn_rate = 0.03
decay_coef = 0.1
adam_epsilon = 1e-08

DIMS = (4, 2, 2, 2)
BF = jnp.bfloat16


def shift_perm(axis, amount):
    pairs = []
    for place in range(int(np.prod(DIMS))):
        spot = list(np.unravel_index(place, DIMS))
        spot[axis] = (spot[axis] + amount) % DIMS[axis]
        pairs.append((place, int(np.ravel_multi_index(spot, DIMS))))
    return pairs


def shift(values, axis, amount):
    return lax.ppermute(values, "dp", shift_perm(axis, amount))


def own_coords():
    place = lax.axis_index("dp")
    return place // 8, (place // 4) % 2, (place // 2) % 2, place % 2


def after(values, *others):
    return lax.optimization_barrier((values, others))[0]


def gather_along(block):
    return [block] + [shift(block, 0, -step) for step in (1, 2, 3)]


def gather_pair(near):
    first = jnp.stack([near[0], near[1]])
    second = jnp.stack([near[2], near[3]])
    return jnp.stack([first, shift(first, 2, 1)]), jnp.stack([second, shift(second, 1, 1)])


def gather_across(pair_a, pair_b):
    return [pair_a, shift(pair_a, 1, 1), pair_b, shift(pair_b, 2, 1)]


def gather_core(mine):
    return mine + [shift(piece, 3, 1) for piece in mine]


def wide(values):
    return values.astype(jnp.float32)


def swap_halves(core, low, high):
    return jnp.where(core == 0, high, low), jnp.where(core == 0, low, high)


def gather_plain(query_round, keyval_round, output_round, gateup_round, down_round, gains_round, headgain_round):
    gateup_full = lax.all_gather(gateup_round, "dp", axis=0, tiled=True)
    return (
        lax.all_gather(query_round, "dp", axis=0, tiled=True),
        lax.all_gather(keyval_round, "dp", axis=0, tiled=True),
        lax.all_gather(output_round, "dp", axis=0, tiled=True),
        gateup_full.reshape(gateup_full.shape[0], -1),
        lax.all_gather(down_round, "dp", axis=0, tiled=True),
        lax.all_gather(gains_round, "dp", axis=1, tiled=True).astype(jnp.float32),
        lax.all_gather(headgain_round, "dp", axis=1, tiled=True).astype(jnp.float32),
    )


def scatter_plain(grad_query, grad_keyval, grad_output, grad_gateup, grad_down, grad_gains, grad_heads):
    rows = grad_gateup.shape[0]
    return (
        lax.psum_scatter(grad_query, "dp", scatter_dimension=0, tiled=True),
        lax.psum_scatter(grad_keyval, "dp", scatter_dimension=0, tiled=True),
        lax.psum_scatter(grad_output, "dp", scatter_dimension=0, tiled=True),
        lax.psum_scatter(grad_gateup.reshape(rows, 2, -1), "dp", scatter_dimension=0, tiled=True),
        lax.psum_scatter(grad_down, "dp", scatter_dimension=0, tiled=True),
        lax.psum_scatter(grad_gains, "dp", scatter_dimension=1, tiled=True),
        lax.psum_scatter(grad_heads, "dp", scatter_dimension=1, tiled=True),
    )


HALF = 1024 // 2
SCALE = 256 ** (-0.5)
KEY_SPANS = ((0, 128), (0, 256), (0, 384), (128, 512))
TANH_SLOPE = (2.0 / np.pi) ** 0.5
TANH_CUBE = 0.044715


def dot(left, right):
    return jnp.dot(left, right, preferred_element_type=jnp.float32)


def dot_right_t(left, right):
    return lax.dot_general(left, right, (((1,), (1,)), ((), ())), preferred_element_type=jnp.float32)


def dot_left_t(left, right):
    return lax.dot_general(left, right, (((0,), (0,)), ((), ())), preferred_element_type=jnp.float32)


def inverse_rms(values):
    return lax.rsqrt(jnp.mean(values * values, axis=-1, keepdims=True) + norm_epsilon)


def pull_norm(values, gain_plus, grad):
    inverse = inverse_rms(values)
    unit = values * inverse
    scaled = grad * gain_plus
    return inverse * (scaled - unit * jnp.mean(scaled * unit, axis=-1, keepdims=True)), grad * unit


def fold_rows(values):
    rows, columns = values.shape
    return jnp.sum(values.reshape(rows // 8, 8, columns), axis=0)


def chunks(count, size, body, carry):
    def step(index, carried):
        return body(pl.ds(pl.multiple_of(index * size, size), size), carried)

    return lax.fori_loop(0, count // size, step, carry)


def group_rows(piece_ref, low, high):
    return piece_ref[:, :, :, low:high].reshape(160, high - low)


def chip_at(coords_ref, gap):
    along = lax.rem(coords_ref[0] + gap[0], 4)
    upward = lax.rem(coords_ref[1] + gap[1], 2)
    sideways = lax.rem(coords_ref[2] + gap[2], 2)
    return (along * 2 + upward) * 2 + sideways


def gap_of(group, one, two):
    return (two, group, one) if group < 2 else (2 + two, one, group - 2)


def slots(coords_ref):
    for far in range(2):
        core = lax.rem(coords_ref[3] + far, 2)
        for group in range(4):
            for one in range(2):
                for two in range(2):
                    yield far, group, one, two, 2 * chip_at(coords_ref, gap_of(group, one, two)) + core


def project_forward(coords_ref, index_ref, tokens_ref, *refs):
    piece_refs, refs = refs[:8], refs[8:]
    (
        h1_ref, q_ref, kv_ref, qn_ref, kn_ref, vb_ref, wo_ref, gains_ref, perm_ref, plain_ref
    ) = refs
    for far, group, one, two, place in slots(coords_ref):
        wo_ref[place] = piece_refs[4 * far + group][one, two, 0:32, 768:1408]
    gains = jnp.zeros((8, 640), jnp.float32)
    for far in range(2):
        for group in range(4):
            for one in range(2):
                for two in range(2):
                    gains = gains + piece_refs[4 * far + group][one, two, 32:40, 768:1408].astype(jnp.float32)
    gains_ref[...] = gains
    core = coords_ref[3]

    def make_perm(rows, carry):
        place = lax.broadcasted_iota(jnp.int32, (64, 1024), 0) + rows.start
        perm_ref[rows, :] = jnp.where(place == index_ref[...], 1.0, 0.0).astype(BF)
        return carry

    chunks(640, 64, make_perm, 0)
    gain_zero = 1.0 + gains_ref[0:1, :]

    def norm_in(rows, carry):
        values = tokens_ref[rows, :].astype(jnp.float32)
        plain_ref[rows, :] = (values * inverse_rms(values) * gain_zero).astype(BF)
        return carry

    chunks(512, 32, norm_in, 0)
    h1_ref[...] = dot(plain_ref[...], perm_ref[...]).astype(BF)
    for far in range(2):
        side = lax.rem(core + far, 2)
        for part in range(3):
            total = jnp.zeros((512, 256), jnp.float32)
            for group in range(4):
                total = total + dot(
                    h1_ref[:, 256 * group : 256 * group + 160],
                    group_rows(piece_refs[4 * far + group], 256 * part, 256 * part + 256),
                )
            if part < 2:
                q_ref[2 * side + part] = total
            else:
                kv_ref[side] = total
    query_gain, key_gain = 1.0 + gains_ref[4:5, 0:256], 1.0 + gains_ref[5:6, 0:256]

    def norm_heads(rows, carry):
        for head in range(4):
            values = q_ref[head, rows, :]
            qn_ref[head, rows, :] = (values * inverse_rms(values) * query_gain).astype(BF)
        values = kv_ref[0, rows, :]
        kn_ref[rows, :] = (values * inverse_rms(values) * key_gain).astype(BF)
        vb_ref[rows, :] = kv_ref[1, rows, :].astype(BF)
        return carry

    chunks(512, 64, norm_heads, 0)


def attention_forward(
    coords_ref, tokens_ref, segrow_ref, segcol_ref, qn_ref, kn_ref, vb_ref, wo_ref, gains_ref, perm_ref,
    prob_ref, o_ref, branch_ref, mid_ref, h3_ref, plain_ref, bias_ref,
):
    for block, (low, high) in enumerate(KEY_SPANS):
        rows, span = slice(128 * block, 128 * block + 128), high - low
        row_at = lax.broadcasted_iota(jnp.int32, (128, span), 0) + 128 * block
        key_at = lax.broadcasted_iota(jnp.int32, (128, span), 1) + low
        allowed = (segcol_ref[rows, :] == segrow_ref[:, low:high]) & (key_at <= row_at)
        bias_ref[:, 0:span] = jnp.where(allowed, 0.0, -1e30)
        for head in range(4):
            scores = dot_right_t(qn_ref[head, rows, :], kn_ref[low:high, :]) * SCALE + bias_ref[:, 0:span]
            powers = jnp.exp(scores - jnp.max(scores, axis=-1, keepdims=True))
            weights = (powers * (1.0 / jnp.sum(powers, axis=-1, keepdims=True))).astype(BF)
            prob_ref[block, 128 * head : 128 * head + 128, 0:span] = weights
            o_ref[head, rows, :] = dot(weights, vb_ref[low:high, :]).astype(BF)
    total = jnp.zeros((512, 640), jnp.float32)
    for head in range(4):
        total = total + dot(o_ref[head], wo_ref[8 * head : 8 * head + 8].reshape(256, 640))
    branch_ref[...] = total
    gain_one, gain_two = 1.0 + gains_ref[1:2, :], 1.0 + gains_ref[2:3, :]

    def norm_mid(rows, carry):
        values = branch_ref[rows, :]
        middle = tokens_ref[rows, :].astype(jnp.float32) + values * inverse_rms(values) * gain_one
        mid_ref[rows, :] = middle
        plain_ref[rows, :] = (middle * inverse_rms(middle) * gain_two).astype(BF)
        return carry

    chunks(512, 32, norm_mid, 0)
    h3_ref[...] = dot(plain_ref[...], perm_ref[...]).astype(BF)


def gateup_forward(coords_ref, h3_ref, *refs):
    piece_refs, (slope_ref, gelu_ref, hidden_ref, both_ref) = refs[:8], refs[8:]
    core = coords_ref[3]
    for block in range(4):
        low = 512 * block
        for far in range(2):
            side = lax.rem(core + far, 2)
            total = jnp.zeros((512, 512), jnp.float32)
            for group in range(4):
                total = total + dot(
                    h3_ref[:, 256 * group : 256 * group + 160],
                    group_rows(piece_refs[4 * far + group], low, low + 512),
                )
            both_ref[side] = total

        def activate(rows, carry, low=low):
            gate, up = both_ref[0, rows, :], both_ref[1, rows, :]
            square = gate * gate
            bend = jnp.tanh(gate * (TANH_SLOPE + (TANH_SLOPE * TANH_CUBE) * square))
            weight = 0.5 + 0.5 * bend
            gelu = gate * weight
            slope = weight + (0.5 * gate) * (1.0 - bend * bend) * (
                TANH_SLOPE + (3.0 * TANH_SLOPE * TANH_CUBE) * square
            )
            slope_ref[rows, low : low + 512] = (slope * up).astype(BF)
            gelu_ref[rows, low : low + 512] = gelu.astype(BF)
            hidden_ref[rows, low : low + 512] = (gelu * up).astype(BF)
            return carry

        chunks(512, 16, activate, 0)


def down_both(coords_ref, hidden_ref, mid_ref, cot_ref, gains_ref, *refs):
    piece_refs, refs = refs[:8], refs[8:]
    (result_ref, dm_ref, gain_ref, wd_ref), refs = refs[:4], refs[4:]
    out_refs, (product_ref, natural_ref) = refs[:4], refs[4:]
    for far, group, one, two, place in slots(coords_ref):
        wd_ref[place] = piece_refs[4 * far + group][one, two]
    total = jnp.zeros((512, 640), jnp.float32)
    for block in range(8):
        total = total + dot(
            hidden_ref[:, 256 * block : 256 * block + 256],
            wd_ref[4 * block : 4 * block + 4].reshape(256, 640),
        )
    product_ref[...] = total
    gain_three = 1.0 + gains_ref[3:4, :]

    def finish(rows, carry):
        values = product_ref[rows, :]
        grad = cot_ref[rows, :].astype(jnp.float32)
        result_ref[rows, :] = (mid_ref[rows, :] + values * inverse_rms(values) * gain_three).astype(BF)
        pulled, term = pull_norm(values, gain_three, grad)
        dm_ref[rows, :] = pulled.astype(BF)
        return carry + fold_rows(term)

    gain_ref[...] = chunks(512, 32, finish, jnp.zeros((8, 640), jnp.float32))
    for block in range(8):
        grad = dot_left_t(hidden_ref[:, 256 * block : 256 * block + 256], dm_ref[...])
        natural_ref[4 * block : 4 * block + 4] = grad.astype(BF).reshape(4, 64, 640)
    for far, group, one, two, place in slots(coords_ref):
        out_refs[2 * far + group // 2][group % 2, one, two] = natural_ref[place]


def gateup_backward(coords_ref, dm_ref, wd_ref, slope_ref, gelu_ref, h3_ref, *refs):
    dgu_ref, out_refs, (dhid_ref, h3t_ref) = refs[0], refs[1:5], refs[5:]
    for block in range(4):
        low = 512 * block
        dhid_ref[...] = dot_right_t(dm_ref[...], wd_ref[8 * block : 8 * block + 8].reshape(512, 640))

        def spread(rows, carry, low=low):
            grad = dhid_ref[rows, :]
            dgu_ref[0, rows, low : low + 512] = (
                grad * slope_ref[rows, low : low + 512].astype(jnp.float32)
            ).astype(BF)
            dgu_ref[1, rows, low : low + 512] = (
                grad * gelu_ref[rows, low : low + 512].astype(jnp.float32)
            ).astype(BF)
            return carry

        chunks(512, 16, spread, 0)
    for group in range(4):
        h3t_ref[160 * group : 160 * group + 160, :] = h3_ref[:, 256 * group : 256 * group + 160].T
    for far in (1, 0):
        side = lax.rem(coords_ref[3] + far, 2)
        for block in range(4):
            low = 512 * block
            grad = dot(h3t_ref[...], dgu_ref[side, :, low : low + 512]).astype(BF)
            for spot in range(16):
                group, one, two = spot // 4, (spot // 2) % 2, spot % 2
                out_refs[2 * far + group // 2][group % 2, one, two, :, low : low + 512] = grad[
                    40 * spot : 40 * spot + 40
                ]


def to_plain(rel_ref, perm_ref, out_ref):
    high = rel_ref[...].astype(BF)
    low = (rel_ref[...] - high.astype(jnp.float32)).astype(BF)
    out_ref[...] = dot_right_t(high, perm_ref[...]) + dot_right_t(low, perm_ref[...])


def middle_backward(
    coords_ref, dgu_ref, mid_ref, branch_ref, cot_ref, gains_ref, perm_ref, *refs
):
    piece_refs, refs = refs[:8], refs[8:]
    dmid_ref, da_ref, gain_ref, rel_ref, plain_ref = refs
    core = coords_ref[3]
    rel_ref[...] = jnp.zeros_like(rel_ref)
    for group in range(4):
        total = jnp.zeros((512, 160), jnp.float32)
        for far in range(2):
            side = lax.rem(core + far, 2)
            total = total + dot_right_t(
                dgu_ref[side], group_rows(piece_refs[4 * far + group], 0, 2048)
            )
        rel_ref[:, 256 * group : 256 * group + 160] = total
    to_plain(rel_ref, perm_ref, plain_ref)
    gain_one, gain_two = 1.0 + gains_ref[1:2, :], 1.0 + gains_ref[2:3, :]

    def pull(rows, carry):
        pulled, term_two = pull_norm(mid_ref[rows, :], gain_two, plain_ref[rows, :])
        grad = cot_ref[rows, :].astype(jnp.float32) + pulled
        dmid_ref[rows, :] = grad
        pulled, term_one = pull_norm(branch_ref[rows, :], gain_one, grad)
        da_ref[rows, :] = pulled.astype(BF)
        return carry[0] + fold_rows(term_one), carry[1] + fold_rows(term_two)

    zero = jnp.zeros((8, 640), jnp.float32)
    gain_ref[0], gain_ref[1] = chunks(512, 32, pull, (zero, zero))


def attention_backward(
    coords_ref, da_ref, wo_ref, o_ref, prob_ref, qn_ref, kn_ref, vb_ref, q_ref, kv_ref, gains_ref,
    dqkv_ref, gain_ref, dwo_ref, do_ref, dqn_ref, dkn_ref, dv_ref, ds_ref,
):
    for head in range(4):
        block = wo_ref[8 * head : 8 * head + 8].reshape(256, 640)
        do_ref[head] = dot_right_t(da_ref[...], block).astype(BF)
        grad = dot_left_t(o_ref[head], da_ref[...])
        dwo_ref[8 * head : 8 * head + 8] = grad.astype(BF).reshape(8, 32, 640)
    dkn_ref[...] = jnp.zeros_like(dkn_ref)
    dv_ref[...] = jnp.zeros_like(dv_ref)
    for block, (low, high) in enumerate(KEY_SPANS):
        rows, span = slice(128 * block, 128 * block + 128), high - low
        for head in range(4):
            grad = do_ref[head, rows, :]
            delta = jnp.sum(
                grad.astype(jnp.float32) * o_ref[head, rows, :].astype(jnp.float32), axis=-1, keepdims=True
            )
            soft = prob_ref[block, 128 * head : 128 * head + 128, 0:span].astype(jnp.float32)
            lifted = dot_right_t(grad, vb_ref[low:high, :])
            ds_ref[128 * head : 128 * head + 128, 0:span] = (soft * (lifted - delta) * SCALE).astype(BF)
        all_ds = ds_ref[:, 0:span]
        all_rows = qn_ref[:, rows, :].reshape(512, 256)
        dqn_ref[:, rows, :] = dot(all_ds, kn_ref[low:high, :]).reshape(4, 128, 256)
        dkn_ref[low:high, :] += dot_left_t(all_ds, all_rows)
        dv_ref[low:high, :] += dot_left_t(
            prob_ref[block, :, 0:span], do_ref[:, rows, :].reshape(512, 256)
        )
    query_gain, key_gain = 1.0 + gains_ref[4:5, 0:256], 1.0 + gains_ref[5:6, 0:256]

    def pull(rows, carry):
        query_sum, key_sum = carry
        for head in range(4):
            pulled, term = pull_norm(q_ref[head, rows, :], query_gain, dqn_ref[head, rows, :])
            dqkv_ref[head // 2, rows, 256 * (head % 2) : 256 * (head % 2) + 256] = pulled.astype(BF)
            query_sum = query_sum + fold_rows(term)
        pulled, term = pull_norm(kv_ref[0, rows, :], key_gain, dkn_ref[rows, :])
        dqkv_ref[0, rows, 512:768] = pulled.astype(BF)
        dqkv_ref[1, rows, 512:768] = dv_ref[rows, :].astype(BF)
        return query_sum, key_sum + fold_rows(term)

    zero = jnp.zeros((8, 256), jnp.float32)
    gain_ref[0], gain_ref[1] = chunks(512, 32, pull, (zero, zero))


def input_backward(
    coords_ref, dqkv_ref, h1_ref, dwo_ref, tokens_ref, dmid_ref, perm_ref, gains_ref, gain_mid_ref,
    gain_head_ref, gain_down_ref, *refs
):
    piece_refs, refs = refs[:8], refs[8:]
    (input_ref, *out_refs), (rel_ref, plain_ref, h1t_ref) = refs[:5], refs[5:]
    core = coords_ref[3]
    rel_ref[...] = jnp.zeros_like(rel_ref)
    for group in range(4):
        total = jnp.zeros((512, 160), jnp.float32)
        for far in range(2):
            side = lax.rem(core + far, 2)
            total = total + dot_right_t(
                dqkv_ref[side], group_rows(piece_refs[4 * far + group], 0, 768)
            )
        rel_ref[:, 256 * group : 256 * group + 160] = total
        h1t_ref[160 * group : 160 * group + 160, :] = h1_ref[:, 256 * group : 256 * group + 160].T
    to_plain(rel_ref, perm_ref, plain_ref)
    gain_zero = 1.0 + gains_ref[0:1, :]

    def pull(rows, carry):
        pulled, term = pull_norm(tokens_ref[rows, :].astype(jnp.float32), gain_zero, plain_ref[rows, :])
        input_ref[rows, :] = dmid_ref[rows, :] + pulled
        return carry + fold_rows(term)

    sums = [chunks(512, 32, pull, jnp.zeros((8, 640), jnp.float32))]
    sums += [gain_mid_ref[0], gain_mid_ref[1], gain_down_ref[...]]
    lines = [jnp.sum(part, axis=0, keepdims=True) for part in sums]
    for part in range(2):
        line = jnp.sum(gain_head_ref[part], axis=0, keepdims=True)
        lines.append(jnp.concatenate([line, jnp.zeros((1, 384), jnp.float32)], axis=1))
    lines.append(jnp.zeros((2, 640), jnp.float32))
    gain_block = jnp.concatenate(lines, axis=0).astype(BF)
    for far, group, one, two, place in slots(coords_ref):
        out = out_refs[2 * far + group // 2]
        out[group % 2, one, two, 0:32, 768:1408] = dwo_ref[place]
        out[group % 2, one, two, 32:40, 768:1408] = gain_block
    for far in range(2):
        side = lax.rem(core + far, 2)
        for part in range(3):
            low = 256 * part
            grad = dot(h1t_ref[...], dqkv_ref[side, :, low : low + 256]).astype(BF)
            for spot in range(16):
                group, one, two = spot // 4, (spot // 2) % 2, spot % 2
                out_refs[2 * far + group // 2][group % 2, one, two, :, low : low + 256] = grad[
                    40 * spot : 40 * spot + 40
                ]


def call(kernel, coords, inputs, outs, scratch=(), megabytes=32, cost=(1, 1), anys=0):
    whole = pl.BlockSpec(memory_space=pltpu.VMEM)
    return pl.pallas_call(
        kernel,
        out_shape=outs,
        in_specs=[pl.BlockSpec(memory_space=pltpu.SMEM)] + [whole] * len(inputs),
        out_specs=jax.tree.map(lambda _: whole, outs),
        scratch_shapes=list(scratch),
        cost_estimate=pl.CostEstimate(
            flops=int(cost[0] * 1e9), bytes_accessed=int(cost[1] * 1e6), transcendentals=0
        ),
        compiler_params=pltpu.CompilerParams(vmem_limit_bytes=megabytes * 1024 * 1024),
    )(coords, *inputs)


def rel_table():
    table = np.full((32, 1, 1024), -1, np.int32)
    for place in range(32):
        z, y, x, _ = np.unravel_index(place, DIMS)
        for group in range(4):
            for one in range(2):
                for two in range(2):
                    gap = gap_of(group, one, two)
                    chip = (((z + gap[0]) % 4) * 2 + (y + gap[1]) % 2) * 2 + (x + gap[2]) % 2
                    low = 256 * group + 80 * one + 40 * two
                    table[place, 0, low : low + 40] = 40 * chip + np.arange(40)
    return table


def shape(*sizes, kind=BF):
    return jax.ShapeDtypeStruct(sizes, kind)


def scatter_core(keep_a, keep_b, send_a, send_b):
    return keep_a, keep_b, shift(send_a, 3, 1), shift(send_b, 3, 1)


def scatter_across(keep_a, keep_b, got_a, got_b):
    far_a = shift((wide(keep_a[1]) + wide(got_a[1])).astype(BF), 1, 1)
    far_b = shift((wide(keep_b[1]) + wide(got_b[1])).astype(BF), 2, 1)
    return keep_a[0], keep_b[0], got_a[0], got_b[0], far_a, far_b


def scatter_pair(keep_a, keep_b, got_a, got_b, far_a, far_b):
    sum_a = wide(keep_a) + wide(got_a) + wide(far_a)
    sum_b = wide(keep_b) + wide(got_b) + wide(far_b)
    return sum_a[0], sum_b[0], shift(sum_a[1].astype(BF), 2, 1), shift(sum_b[1].astype(BF), 1, 1)


def scatter_along(sum_a, sum_b, side_a, side_b):
    last_a = sum_a + wide(side_a)
    last_b = sum_b + wide(side_b)
    return (
        last_a[0],
        shift(last_a[1].astype(BF), 0, 1),
        shift(last_b[0].astype(BF), 0, 2),
        shift(last_b[1].astype(BF), 0, 3),
    )


def scatter_end(own, *others):
    for other in others:
        own = own + wide(other)
    return own


def block_fast(tokens, segment_ids, cotangent, weights):
    query_round, keyval_round, output_round, gateup_round, down_round, gains, heads = weights
    f32 = jnp.float32
    along, upward, sideways, core = own_coords()
    place = lax.axis_index("dp")
    coords = jnp.stack([along, upward, sideways, core]).astype(jnp.int32)
    index = lax.dynamic_index_in_dim(jnp.asarray(rel_table()), place, keepdims=False)
    tokens, cotangent = tokens.reshape(512, 640), cotangent.reshape(512, 640)
    segcol = segment_ids.reshape(512, 1)

    low = jnp.concatenate([query_round[:, :512], keyval_round[:, :256], gateup_round[:, 0]], axis=1)
    high = jnp.concatenate([query_round[:, 512:], keyval_round[:, 256:], gateup_round[:, 1]], axis=1)
    away, keep = swap_halves(core, low, high)
    got = shift(away, 3, 1)
    both = jnp.concatenate([jnp.where(core == 0, keep, got), jnp.where(core == 0, got, keep)], axis=0)
    spread = jnp.zeros((8, 640), BF)
    spread = lax.dynamic_update_slice(spread, gains, (0, place * gains.shape[1]))
    spread = lax.dynamic_update_slice(spread, heads, (4, place * heads.shape[1]))
    block_a = jnp.concatenate([both[:, :768], jnp.concatenate([output_round, spread], axis=0)], axis=1)
    block_g = both[:, 768:]

    near_w = gather_along(down_round)
    near_a = gather_along(block_a)
    pairs_w = gather_pair(near_w)
    mine_w = gather_across(*pairs_w)
    pieces_w = gather_core(mine_w)
    near_g = gather_along(after(block_g, *near_a))
    pairs_a = gather_pair(after(near_a, *pairs_w))
    mine_a = gather_across(*pairs_a)
    pieces_a = gather_core(mine_a)
    pairs_g = gather_pair(after(near_g, *pairs_a))
    mine_g = gather_across(*after(pairs_g, *mine_a))
    pieces_g = gather_core(mine_g)

    h1, q, kv, qn, kn, vb, wo, gains_full, perm = call(
        project_forward,
        coords,
        [index, tokens, *after(pieces_a, *pairs_g)],
        [
            shape(512, 1024), shape(4, 512, 256, kind=f32), shape(2, 512, 256, kind=f32),
            shape(4, 512, 256), shape(512, 256), shape(512, 256),
            shape(32, 32, 640), shape(8, 640, kind=f32), shape(640, 1024),
        ],
        [pltpu.VMEM((512, 640), BF)],
        12,
        (5, 20),
    )
    prob, o, branch, mid, h3 = call(
        attention_forward,
        coords,
        [tokens, segment_ids, segcol, qn, kn, vb, wo, gains_full, perm],
        [
            shape(4, 512, 384), shape(4, 512, 256), shape(512, 640, kind=f32),
            shape(512, 640, kind=f32), shape(512, 1024),
        ],
        [pltpu.VMEM((512, 640), BF), pltpu.VMEM((128, 384), f32)],
        12,
        (5, 20),
    )
    slope, gelu, hidden = call(
        gateup_forward,
        coords,
        [h3, *pieces_g],
        [shape(512, 2048)] * 3,
        [pltpu.VMEM((2, 512, 512), f32)],
        12,
        (6, 20),
    )
    result, dm, gain_down, wd, *parts_w = call(
        down_both,
        coords,
        [hidden, mid, cotangent, gains_full, *pieces_w],
        [shape(512, 640), shape(512, 640), shape(8, 640, kind=f32), shape(32, 64, 640)]
        + [shape(2, 2, 2, 64, 640)] * 4,
        [pltpu.VMEM((512, 640), f32), pltpu.VMEM((32, 64, 640), BF)],
        12,
        (6, 20),
    )
    dgu, *parts_g = call(
        gateup_backward,
        coords,
        [dm, wd, slope, gelu, h3],
        [shape(2, 512, 2048)] + [shape(2, 2, 2, 40, 2048)] * 4,
        [pltpu.VMEM((512, 512), f32), pltpu.VMEM((640, 512), BF)],
        12,
        (8, 20),
    )
    got_w = scatter_core(*parts_w)
    dmid, da, gain_mid = call(
        middle_backward,
        coords,
        [after(dgu, *got_w), mid, branch, cotangent, gains_full, perm, *pieces_g],
        [shape(512, 640, kind=f32), shape(512, 640), shape(2, 8, 640, kind=f32)],
        [pltpu.VMEM((512, 1024), f32), pltpu.VMEM((512, 640), f32)],
        12,
        (8, 20),
    )
    far_w = scatter_across(*got_w)
    got_g = scatter_core(*parts_g)
    dqkv, gain_head, dwo = call(
        attention_backward,
        coords,
        [after(da, *far_w, *got_g), wo, o, prob, qn, kn, vb, q, kv, gains_full],
        [shape(2, 512, 768), shape(2, 8, 256, kind=f32), shape(32, 32, 640)],
        [
            pltpu.VMEM((4, 512, 256), BF),
            pltpu.VMEM((4, 512, 256), f32), pltpu.VMEM((512, 256), f32), pltpu.VMEM((512, 256), f32),
            pltpu.VMEM((512, 384), BF),
        ],
        12,
        (6, 20),
    )
    side_w = scatter_pair(*far_w)
    far_g = scatter_across(*got_g)
    input_grad, *parts_a = call(
        input_backward,
        coords,
        [after(dqkv, *side_w), h1, dwo, tokens, dmid, perm, gains_full, gain_mid, gain_head, gain_down, *pieces_a],
        [shape(512, 640, kind=f32)] + [shape(2, 2, 2, 40, 1408)] * 4,
        [pltpu.VMEM((512, 1024), f32), pltpu.VMEM((512, 640), f32), pltpu.VMEM((640, 512), BF)],
        12,
        (6, 20),
    )
    down_grad = scatter_end(*scatter_along(*side_w))
    side_g = scatter_pair(*far_g)
    got_a = scatter_core(*after(parts_a, *far_g))
    far_a = scatter_across(*after(got_a, *side_g))
    gateup_sum = scatter_end(*scatter_along(*side_g))
    rest = scatter_end(*scatter_along(*scatter_pair(*far_a)))
    output_grad = rest[:32, 768:]
    norm_grad = lax.dynamic_slice(rest[32:36, 768:], (0, place * 20), (4, 20))
    qknorm_grad = lax.dynamic_slice(rest[36:38, 768:], (0, place * 8), (2, 8))

    def own_rows(both):
        away, keep = swap_halves(core, both[:20], both[20:])
        got = shift(away, 3, 1)
        return jnp.where(core == 0, keep, got), jnp.where(core == 0, got, keep)

    low, high = own_rows(gateup_sum)
    gateup_grad = jnp.stack([low, high], axis=1)
    low, high = own_rows(rest[:, :768])
    query_grad = jnp.concatenate([low[:, :512], high[:, :512]], axis=1)
    keyval_grad = jnp.concatenate([low[:, 512:], high[:, 512:]], axis=1)
    grads = (query_grad, keyval_grad, output_grad, gateup_grad, down_grad, norm_grad, qknorm_grad)
    return result[None], input_grad[None], grads


def norm_apply(values, gain_vector):
    inverse = lax.rsqrt(jnp.mean(values * values, axis=-1, keepdims=True) + norm_epsilon)
    return values * inverse * (1.0 + gain_vector)


def gelu_product(gate_part, up_part):
    return jax.nn.gelu(gate_part, approximate=True) * up_part


def block_scores(query_normed, key_normed, segments, row_start, row_stop, score_scale):
    positions = jnp.arange(row_stop)
    same_doc = segments[row_start:row_stop, None] == segments[None, :row_stop]
    causal = positions[None, :] <= positions[row_start:row_stop, None]
    allowed = (same_doc & causal)[None]
    scores = (
        jnp.einsum("qhd,kd->hqk", query_normed, key_normed, preferred_element_type=jnp.float32)
        * score_scale
    )
    return (jnp.where(allowed, scores, -1e30), allowed)


def attend_forward(query_normed, key_normed, value_round, segments, score_scale):
    length = query_normed.shape[0]
    block_rows = min(512, length)
    masked, allowed = block_scores(query_normed, key_normed, segments, 0, block_rows, score_scale)
    row_max = jnp.max(masked, axis=-1, keepdims=True)
    row_total = jnp.sum(jnp.where(allowed, jnp.exp(masked - row_max), 0.0), axis=-1, keepdims=True)
    log_total = row_max + jnp.log(row_total)
    soft_round = jnp.where(allowed, jnp.exp(masked - log_total), 0.0).astype(jnp.bfloat16)
    attended_block = jnp.einsum(
        "hqk,kd->qhd", soft_round, value_round, preferred_element_type=jnp.float32
    )
    attended_parts = attended_block.astype(jnp.bfloat16)
    total_parts = log_total[:, :, 0]
    return (attended_parts, total_parts)


def attend_backward(
    query_normed,
    key_normed,
    value_round,
    segments,
    log_totals,
    attended,
    grad_attended,
    score_scale,
):
    length = query_normed.shape[0]
    head_dim = key_normed.shape[1]
    block_rows = min(512, length)
    row_delta = jnp.sum(grad_attended.astype(jnp.float32) * attended.astype(jnp.float32), axis=-1)
    grad_key_sum = jnp.zeros((length, head_dim), jnp.float32)
    grad_value_sum = jnp.zeros((length, head_dim), jnp.float32)
    masked, allowed = block_scores(query_normed, key_normed, segments, 0, block_rows, score_scale)
    soft_weights = jnp.where(allowed, jnp.exp(masked - log_totals[:, 0:block_rows, None]), 0.0)
    soft_round = soft_weights.astype(jnp.bfloat16)
    grad_value_sum = grad_value_sum.at[:block_rows].add(
        jnp.einsum("hqk,qhd->kd", soft_round, grad_attended, preferred_element_type=jnp.float32)
    )
    grad_soft = jnp.einsum(
        "qhd,kd->hqk", grad_attended, value_round, preferred_element_type=jnp.float32
    )
    delta_block = row_delta.T[:, :, None]
    grad_scores = (soft_weights * (grad_soft - delta_block) * score_scale).astype(jnp.bfloat16)
    grad_query_parts = jnp.einsum(
        "hqk,kd->qhd", grad_scores, key_normed, preferred_element_type=jnp.float32
    )
    grad_key_sum = grad_key_sum.at[:block_rows].add(
        jnp.einsum("hqk,qhd->kd", grad_scores, query_normed, preferred_element_type=jnp.float32)
    )
    return (grad_query_parts, grad_key_sum, grad_value_sum)


def adam_update(parameter, gradient, first_moment, second_moment, decay_value):
    first_new = beta_one * first_moment + (1.0 - beta_one) * gradient
    second_new = beta_two * second_moment + (1.0 - beta_two) * gradient * gradient
    first_hat = first_new / (1.0 - beta_one**STEP)
    second_hat = second_new / (1.0 - beta_two**STEP)
    parameter_new = (
        parameter
        - learn_rate * first_hat / (jnp.sqrt(second_hat) + adam_epsilon)
        - learn_rate * decay_value * parameter
    )
    return (parameter_new, first_new, second_new)


def block_plain(tokens, segment_ids, cotangent, weights):
    query_full, keyval_full, output_full, gateup_full, down_full, main_gains, head_gains = gather_plain(*weights)
    seq_count, length, model_width = tokens.shape
    row_count = seq_count * length
    head_dim = head_gains.shape[1]
    head_count = query_full.shape[1] // head_dim
    hidden_units = gateup_full.shape[1] // 2
    score_scale = head_dim ** (-0.5)
    inputs = tokens.reshape(row_count, model_width).astype(jnp.float32)
    normed_in = norm_apply(inputs, main_gains[0]).astype(jnp.bfloat16)
    queries = jnp.dot(normed_in, query_full, preferred_element_type=jnp.float32).reshape(
        row_count, head_count, head_dim
    )
    keyvals = jnp.dot(normed_in, keyval_full, preferred_element_type=jnp.float32)
    key_rows = keyvals[:, :head_dim]
    value_rows = keyvals[:, head_dim:]
    query_normed = norm_apply(queries, head_gains[0]).astype(jnp.bfloat16)
    key_normed = norm_apply(key_rows, head_gains[1]).astype(jnp.bfloat16)
    value_round = value_rows.astype(jnp.bfloat16)
    seq_index = 0
    attended_seq, totals_seq = attend_forward(
        query_normed, key_normed, value_round, segment_ids[seq_index], score_scale
    )
    total_parts = [totals_seq]
    attended_flat = attended_seq.reshape(row_count, head_count * head_dim)
    branch = jnp.dot(attended_flat, output_full, preferred_element_type=jnp.float32)
    middle = inputs + norm_apply(branch, main_gains[1])
    normed_mid = norm_apply(middle, main_gains[2]).astype(jnp.bfloat16)
    gate_up = jnp.dot(
        normed_mid,
        gateup_full,
        preferred_element_type=jnp.float32,
    )
    gate_part = gate_up[:, :hidden_units]
    up_part = gate_up[:, hidden_units:]
    hidden = gelu_product(gate_part, up_part).astype(jnp.bfloat16)
    down_out = jnp.dot(hidden, down_full, preferred_element_type=jnp.float32)
    result = (middle + norm_apply(down_out, main_gains[3])).astype(jnp.bfloat16)
    query_back, keyval_back, output_back, gateup_back, down_back = (
        query_full,
        keyval_full,
        output_full,
        gateup_full,
        down_full,
    )
    gateup_flat = gateup_back
    grad_out = cotangent.reshape(row_count, model_width).astype(jnp.float32)
    _, pull_back = jax.vjp(norm_apply, down_out, main_gains[3])
    grad_down_out, grad_gain_three = pull_back(grad_out)
    grad_down_round = grad_down_out.astype(jnp.bfloat16)
    grad_down = jnp.dot(hidden.T, grad_down_round, preferred_element_type=jnp.float32)
    grad_hidden = jnp.dot(grad_down_round, down_back.T, preferred_element_type=jnp.float32)
    _, pull_back = jax.vjp(gelu_product, gate_part, up_part)
    grad_gate, grad_up = pull_back(grad_hidden)
    grad_gate_up = jnp.concatenate([grad_gate, grad_up], axis=1).astype(jnp.bfloat16)
    grad_gateup = jnp.dot(normed_mid.T, grad_gate_up, preferred_element_type=jnp.float32)
    grad_normed_mid = jnp.dot(grad_gate_up, gateup_flat.T, preferred_element_type=jnp.float32)
    _, pull_back = jax.vjp(norm_apply, middle, main_gains[2])
    grad_mid_norm, grad_gain_two = pull_back(grad_normed_mid)
    grad_middle = grad_out + grad_mid_norm
    _, pull_back = jax.vjp(norm_apply, branch, main_gains[1])
    grad_branch, grad_gain_one = pull_back(grad_middle)
    grad_branch_round = grad_branch.astype(jnp.bfloat16)
    grad_output = jnp.dot(attended_flat.T, grad_branch_round, preferred_element_type=jnp.float32)
    grad_attended = (
        jnp.dot(grad_branch_round, output_back.T, preferred_element_type=jnp.float32)
        .reshape(row_count, head_count, head_dim)
        .astype(jnp.bfloat16)
    )
    seq_index = 0
    grad_query_seq, grad_key_seq, grad_value_seq = attend_backward(
        query_normed,
        key_normed,
        value_round,
        segment_ids[seq_index],
        total_parts[seq_index],
        attended_seq,
        grad_attended,
        score_scale,
    )
    _, pull_back = jax.vjp(norm_apply, queries, head_gains[0])
    grad_queries, grad_head_zero = pull_back(grad_query_seq)
    _, pull_back = jax.vjp(norm_apply, key_rows, head_gains[1])
    grad_keys, grad_head_one = pull_back(grad_key_seq)
    grad_query_round = grad_queries.reshape(row_count, head_count * head_dim).astype(jnp.bfloat16)
    grad_keyval_round = jnp.concatenate([grad_keys, grad_value_seq], axis=1).astype(jnp.bfloat16)
    grad_query = jnp.dot(normed_in.T, grad_query_round, preferred_element_type=jnp.float32)
    grad_keyval = jnp.dot(normed_in.T, grad_keyval_round, preferred_element_type=jnp.float32)
    grad_normed_in = jnp.dot(
        grad_query_round, query_back.T, preferred_element_type=jnp.float32
    ) + jnp.dot(grad_keyval_round, keyval_back.T, preferred_element_type=jnp.float32)
    _, pull_back = jax.vjp(norm_apply, inputs, main_gains[0])
    grad_in_norm, grad_gain_zero = pull_back(grad_normed_in)
    input_grad = grad_middle + grad_in_norm
    grad_gains = jnp.stack([grad_gain_zero, grad_gain_one, grad_gain_two, grad_gain_three])
    grad_heads = jnp.stack([grad_head_zero, grad_head_one])
    gradients = scatter_plain(
        grad_query, grad_keyval, grad_output, grad_gateup, grad_down, grad_gains, grad_heads
    )
    result_out = result.reshape(seq_count, length, model_width)
    input_out = input_grad.reshape(seq_count, length, model_width)
    return result_out, input_out, gradients


def per_device(
    tokens,
    segment_ids,
    cotangent,
    query_weight,
    keyval_weight,
    output_weight,
    gateup_weight,
    down_weight,
    norm_gains,
    qknorm_gains,
    query_mean,
    keyval_mean,
    output_mean,
    gateup_mean,
    down_mean,
    norm_mean,
    qknorm_mean,
    query_square,
    keyval_square,
    output_square,
    gateup_square,
    down_square,
    norm_square,
    qknorm_square,
):
    query_round = query_weight.astype(jnp.bfloat16)
    keyval_round = keyval_weight.astype(jnp.bfloat16)
    output_round = output_weight.astype(jnp.bfloat16)
    gateup_round = gateup_weight.astype(jnp.bfloat16)
    down_round = down_weight.astype(jnp.bfloat16)
    gains_round = norm_gains.astype(jnp.bfloat16)
    headgain_round = qknorm_gains.astype(jnp.bfloat16)
    weights = (
        query_round, keyval_round, output_round, gateup_round, down_round, gains_round, headgain_round
    )
    block = block_fast if lax.axis_size("dp") == 32 else block_plain
    result_out, input_out, gradients = block(tokens, segment_ids, cotangent, weights)
    parameters = (
        query_weight,
        keyval_weight,
        output_weight,
        gateup_weight,
        down_weight,
        norm_gains,
        qknorm_gains,
    )
    firsts = (query_mean, keyval_mean, output_mean, gateup_mean, down_mean, norm_mean, qknorm_mean)
    seconds = (
        query_square,
        keyval_square,
        output_square,
        gateup_square,
        down_square,
        norm_square,
        qknorm_square,
    )
    decays = (decay_coef, decay_coef, decay_coef, decay_coef, decay_coef, 0.0, 0.0)
    updates = [
        adam_update(
            parameters[place], gradients[place], firsts[place], seconds[place], decays[place]
        )
        for place in range(7)
    ]
    news = tuple((update[0] for update in updates))
    first_news = tuple((update[1] for update in updates))
    second_news = tuple((update[2] for update in updates))
    return (result_out, input_out) + gradients + news + first_news + second_news


def solution(mesh):
    in_specs = (
        P("dp", None, None),
        P("dp", None),
        P("dp", None, None),
        P("dp", None),
        P("dp", None),
        P("dp", None),
        P("dp", None, None),
        P("dp", None),
        P(None, "dp"),
        P(None, "dp"),
        P("dp", None),
        P("dp", None),
        P("dp", None),
        P("dp", None, None),
        P("dp", None),
        P(None, "dp"),
        P(None, "dp"),
        P("dp", None),
        P("dp", None),
        P("dp", None),
        P("dp", None, None),
        P("dp", None),
        P(None, "dp"),
        P(None, "dp"),
    )
    out_specs = (
        P("dp", None, None),
        P("dp", None, None),
        P("dp", None),
        P("dp", None),
        P("dp", None),
        P("dp", None, None),
        P("dp", None),
        P(None, "dp"),
        P(None, "dp"),
        P("dp", None),
        P("dp", None),
        P("dp", None),
        P("dp", None, None),
        P("dp", None),
        P(None, "dp"),
        P(None, "dp"),
        P("dp", None),
        P("dp", None),
        P("dp", None),
        P("dp", None, None),
        P("dp", None),
        P(None, "dp"),
        P(None, "dp"),
        P("dp", None),
        P("dp", None),
        P("dp", None),
        P("dp", None, None),
        P("dp", None),
        P(None, "dp"),
        P(None, "dp"),
    )
    return jax.shard_map(
        per_device, mesh=mesh, in_specs=in_specs, out_specs=out_specs, check_vma=False
    )
```

```python
import jax
import jax.numpy as jnp
import numpy as np
from jax import lax
from jax.experimental import pallas as pl
from jax.experimental.layout import Layout, with_layout_constraint
from jax.experimental.pallas import tpu as pltpu
from jax.sharding import PartitionSpec as P

STEP = 3
norm_epsilon = 1e-06
beta_one = 0.9
beta_two = 0.999
learn_rate = 0.03
decay_coef = 0.1
adam_epsilon = 1e-08

DIMS = (4, 2, 2, 2)
BF = jnp.bfloat16


def shift_perm(axis, amount):
    pairs = []
    for place in range(int(np.prod(DIMS))):
        spot = list(np.unravel_index(place, DIMS))
        spot[axis] = (spot[axis] + amount) % DIMS[axis]
        pairs.append((place, int(np.ravel_multi_index(spot, DIMS))))
    return pairs


def shift(values, axis, amount):
    with jax.named_scope("zyxc"[axis] + str(amount % DIMS[axis])):
        return lax.ppermute(values, "dp", shift_perm(axis, amount))


def own_coords():
    place = lax.axis_index("dp")
    return place // 8, (place // 4) % 2, (place // 2) % 2, place % 2


def after(values, *others):
    return lax.optimization_barrier((values, others))[0]


def gather_along(block):
    return [block] + [shift(block, 0, -step) for step in (1, 2, 3)]


def gather_pair(near):
    first = jnp.stack([near[0], near[1]])
    second = jnp.stack([near[2], near[3]])
    return jnp.stack([first, shift(first, 2, 1)]), jnp.stack([second, shift(second, 1, 1)])


def gather_across(pair_a, pair_b):
    return [pair_a, shift(pair_a, 1, 1), pair_b, shift(pair_b, 2, 1)]


def gather_core(mine):
    return mine + [shift(piece, 3, 1) for piece in mine]


def wide(values):
    return values.astype(jnp.float32)


def swap_halves(core, low, high):
    return jnp.where(core == 0, high, low), jnp.where(core == 0, low, high)


def gather_plain(query_round, keyval_round, output_round, gateup_round, down_round, gains_round, headgain_round):
    gateup_full = lax.all_gather(gateup_round, "dp", axis=0, tiled=True)
    return (
        lax.all_gather(query_round, "dp", axis=0, tiled=True),
        lax.all_gather(keyval_round, "dp", axis=0, tiled=True),
        lax.all_gather(output_round, "dp", axis=0, tiled=True),
        gateup_full.reshape(gateup_full.shape[0], -1),
        lax.all_gather(down_round, "dp", axis=0, tiled=True),
        lax.all_gather(gains_round, "dp", axis=1, tiled=True).astype(jnp.float32),
        lax.all_gather(headgain_round, "dp", axis=1, tiled=True).astype(jnp.float32),
    )


def scatter_plain(grad_query, grad_keyval, grad_output, grad_gateup, grad_down, grad_gains, grad_heads):
    rows = grad_gateup.shape[0]
    return (
        lax.psum_scatter(grad_query, "dp", scatter_dimension=0, tiled=True),
        lax.psum_scatter(grad_keyval, "dp", scatter_dimension=0, tiled=True),
        lax.psum_scatter(grad_output, "dp", scatter_dimension=0, tiled=True),
        lax.psum_scatter(grad_gateup.reshape(rows, 2, -1), "dp", scatter_dimension=0, tiled=True),
        lax.psum_scatter(grad_down, "dp", scatter_dimension=0, tiled=True),
        lax.psum_scatter(grad_gains, "dp", scatter_dimension=1, tiled=True),
        lax.psum_scatter(grad_heads, "dp", scatter_dimension=1, tiled=True),
    )


BYTES = 1e6
COST = 1.0
HALF = 1024 // 2
SCALE = 256 ** (-0.5)
KEY_SPANS = ((0, 128), (0, 256), (0, 384), (128, 512))
TANH_SLOPE = (2.0 / np.pi) ** 0.5
TANH_CUBE = 0.044715


def dot(left, right):
    return jnp.dot(left, right, preferred_element_type=jnp.float32)


def dot_right_t(left, right):
    return lax.dot_general(left, right, (((1,), (1,)), ((), ())), preferred_element_type=jnp.float32)


def dot_left_t(left, right):
    return lax.dot_general(left, right, (((0,), (0,)), ((), ())), preferred_element_type=jnp.float32)


def inverse_rms(values):
    return lax.rsqrt(jnp.mean(values * values, axis=-1, keepdims=True) + norm_epsilon)


def pull_norm(values, gain_plus, grad):
    inverse = inverse_rms(values)
    unit = values * inverse
    scaled = grad * gain_plus
    return inverse * (scaled - unit * jnp.mean(scaled * unit, axis=-1, keepdims=True)), grad * unit


def fold_rows(values):
    rows, columns = values.shape
    return jnp.sum(values.reshape(rows // 8, 8, columns), axis=0)


def chunks(count, size, body, carry):
    for low in range(0, count, size):
        carry = body(slice(low, low + size), carry)
    return carry


def looped(count, size, body, unroll):
    def step(index, carried):
        body(pl.ds(pl.multiple_of(index * size, size), size))
        return carried

    lax.fori_loop(0, count // size, step, 0, unroll=unroll)


def group_rows(piece_ref, low, high):
    return piece_ref[:, :, :, low:high].reshape(160, high - low)


def chip_at(coords_ref, gap):
    along = lax.rem(coords_ref[0] + gap[0], 4)
    upward = lax.rem(coords_ref[1] + gap[1], 2)
    sideways = lax.rem(coords_ref[2] + gap[2], 2)
    return (along * 2 + upward) * 2 + sideways


def gap_of(group, one, two):
    return (two, group, one) if group < 2 else (2 + two, one, group - 2)


def slots(coords_ref):
    for far in range(2):
        core = lax.rem(coords_ref[3] + far, 2)
        for group in range(4):
            for one in range(2):
                for two in range(2):
                    yield far, group, one, two, 2 * chip_at(coords_ref, gap_of(group, one, two)) + core


def place_rows(out_ref, piece_refs, low, high):
    for group in range(4):
        for one in range(2):
            for two in range(2):
                row = 160 * group + 80 * one + 40 * two
                out_ref[row : row + 40, :] = piece_refs[group][one, two, :, low:high]


def project_forward(coords_ref, index_ref, tokens_ref, *refs):
    piece_refs, refs = refs[:8], refs[8:]
    (
        h1_ref, q_ref, kv_ref, qn_ref, kn_ref, vb_ref, wo_ref, gains_ref, perm_ref, own_ref, far_ref, plain_ref
    ) = refs
    for far, group, one, two, place in slots(coords_ref):
        wo_ref[place] = piece_refs[4 * far + group][one, two, 0:32, 768:1408]
    gains = jnp.zeros((8, 640), jnp.float32)
    for far in range(2):
        for group in range(4):
            for one in range(2):
                for two in range(2):
                    gains = gains + piece_refs[4 * far + group][one, two, 32:40, 768:1408].astype(jnp.float32)
    gains_ref[...] = gains
    core = coords_ref[3]

    def make_perm(rows, carry):
        place = lax.broadcasted_iota(jnp.int32, (64, 640), 0) + rows.start
        perm_ref[rows, :] = jnp.where(place == index_ref[...], 1.0, 0.0).astype(BF)
        return carry

    chunks(640, 64, make_perm, 0)
    gain_zero = 1.0 + gains_ref[0:1, :]

    def norm_in(rows, carry):
        values = tokens_ref[rows, :].astype(jnp.float32)
        plain_ref[rows, :] = (values * inverse_rms(values) * gain_zero).astype(BF)
        return carry

    chunks(512, 32, norm_in, 0)
    h1_ref[...] = dot(plain_ref[...], perm_ref[...]).astype(BF)
    for far, weight_ref in enumerate((own_ref, far_ref)):
        place_rows(weight_ref, piece_refs[4 * far : 4 * far + 4], 0, 768)
        side = lax.rem(core + far, 2)
        for part in range(3):
            total = dot(h1_ref[...], weight_ref[:, 256 * part : 256 * part + 256])
            if part < 2:
                q_ref[2 * side + part] = total
            else:
                kv_ref[side] = total
    query_gain, key_gain = 1.0 + gains_ref[4:5, 0:256], 1.0 + gains_ref[5:6, 0:256]

    def norm_heads(rows, carry):
        for head in range(4):
            values = q_ref[head, rows, :]
            qn_ref[head, rows, :] = (values * inverse_rms(values) * query_gain).astype(BF)
        values = kv_ref[0, rows, :]
        kn_ref[rows, :] = (values * inverse_rms(values) * key_gain).astype(BF)
        vb_ref[rows, :] = kv_ref[1, rows, :].astype(BF)
        return carry

    chunks(512, 64, norm_heads, 0)


def attention_forward(
    coords_ref, tokens_ref, segrow_ref, segcol_ref, qn_ref, kn_ref, vb_ref, wo_ref, gains_ref, perm_ref,
    prob_ref, o_ref, branch_ref, mid_ref, h3_ref, plain_ref, bias_ref, score_ref,
):
    for block, (low, high) in enumerate(KEY_SPANS):
        rows, span = slice(128 * block, 128 * block + 128), high - low
        row_at = lax.broadcasted_iota(jnp.int32, (128, span), 0) + 128 * block
        key_at = lax.broadcasted_iota(jnp.int32, (128, span), 1) + low
        allowed = (segcol_ref[rows, :] == segrow_ref[:, low:high]) & (key_at <= row_at)
        bias_ref[:, 0:span] = jnp.where(allowed, 0.0, -1e30)
        score_ref[:, 0:span] = dot_right_t(qn_ref[:, rows, :].reshape(512, 256), kn_ref[low:high, :])

        def soften(part, carry, block=block, span=span):
            near = slice(part.start % 128, part.start % 128 + 32)
            scores = score_ref[part, 0:span] * SCALE + bias_ref[near, 0:span]
            powers = jnp.exp(scores - jnp.max(scores, axis=-1, keepdims=True))
            inverse = 1.0 / jnp.sum(powers, axis=-1, keepdims=True)
            prob_ref[block, part, 0:span] = (powers * inverse).astype(BF)
            return carry

        chunks(512, 32, soften, 0)
        mixed = dot(prob_ref[block, :, 0:span], vb_ref[low:high, :])
        o_ref[:, rows, :] = mixed.astype(BF).reshape(4, 128, 256)
    total = jnp.zeros((512, 640), jnp.float32)
    for head in range(4):
        total = total + dot(o_ref[head], wo_ref[8 * head : 8 * head + 8].reshape(256, 640))
    branch_ref[...] = total
    gain_one, gain_two = 1.0 + gains_ref[1:2, :], 1.0 + gains_ref[2:3, :]

    def norm_mid(rows, carry):
        values = branch_ref[rows, :]
        middle = tokens_ref[rows, :].astype(jnp.float32) + values * inverse_rms(values) * gain_one
        mid_ref[rows, :] = middle
        plain_ref[rows, :] = (middle * inverse_rms(middle) * gain_two).astype(BF)
        return carry

    chunks(512, 32, norm_mid, 0)
    h3_ref[...] = dot(plain_ref[...], perm_ref[...]).astype(BF)


def gateup_own(coords_ref, h3_ref, *refs):
    piece_refs, (own_ref, weight_ref) = refs[:4], refs[4:]
    place_rows(weight_ref, piece_refs, 0, 2048)
    for block in range(4):
        low = 512 * block
        own_ref[:, low : low + 512] = dot(h3_ref[...], weight_ref[:, low : low + 512])


def gateup_forward(coords_ref, h3_ref, own_ref, *refs):
    piece_refs, (slope_ref, gelu_ref, hidden_ref, weight_ref, far_ref) = refs[:4], refs[4:]
    core = coords_ref[3]
    place_rows(weight_ref, piece_refs, 0, 2048)
    for block in range(4):
        low = 512 * block
        far_ref[...] = dot(h3_ref[...], weight_ref[:, low : low + 512])

        def activate(rows, low=low):
            own, far = own_ref[rows, low : low + 512], far_ref[rows, :]
            gate, up = jnp.where(core == 0, own, far), jnp.where(core == 0, far, own)
            square = gate * gate
            bend = jnp.tanh(gate * (TANH_SLOPE + (TANH_SLOPE * TANH_CUBE) * square))
            weight = 0.5 + 0.5 * bend
            gelu = gate * weight
            slope = weight + (0.5 * gate) * (1.0 - bend * bend) * (
                TANH_SLOPE + (3.0 * TANH_SLOPE * TANH_CUBE) * square
            )
            slope_ref[rows, low : low + 512] = (slope * up).astype(BF)
            gelu_ref[rows, low : low + 512] = gelu.astype(BF)
            hidden_ref[rows, low : low + 512] = (gelu * up).astype(BF)

        looped(512, 16, activate, 4)


def down_both(coords_ref, hidden_ref, mid_ref, cot_ref, gains_ref, *refs):
    piece_refs, refs = refs[:8], refs[8:]
    (result_ref, dm_ref, gain_ref, wd_ref), refs = refs[:4], refs[4:]
    out_refs, (product_ref, natural_ref) = refs[:2], refs[2:]
    for far, group, one, two, place in slots(coords_ref):
        wd_ref[place] = piece_refs[4 * far + group][one, two]
    total = jnp.zeros((512, 640), jnp.float32)
    for block in range(8):
        total = total + dot(
            hidden_ref[:, 256 * block : 256 * block + 256],
            wd_ref[4 * block : 4 * block + 4].reshape(256, 640),
        )
    product_ref[...] = total
    gain_three = 1.0 + gains_ref[3:4, :]

    def finish(rows, carry):
        values = product_ref[rows, :]
        grad = cot_ref[rows, :].astype(jnp.float32)
        result_ref[rows, :] = (mid_ref[rows, :] + values * inverse_rms(values) * gain_three).astype(BF)
        pulled, term = pull_norm(values, gain_three, grad)
        dm_ref[rows, :] = pulled.astype(BF)
        return carry + fold_rows(term)

    gain_ref[...] = chunks(512, 32, finish, jnp.zeros((8, 640), jnp.float32))
    for block in range(8):
        grad = dot_left_t(hidden_ref[:, 256 * block : 256 * block + 256], dm_ref[...])
        natural_ref[4 * block : 4 * block + 4] = grad.astype(BF).reshape(4, 64, 640)
    for far, group, one, two, place in slots(coords_ref):
        out_refs[far][group, one, two] = natural_ref[place]


def gateup_backward(coords_ref, dm_ref, wd_ref, slope_ref, gelu_ref, h3_ref, *refs):
    dgu_ref, out_refs, (dhid_ref, h3t_ref) = refs[0], refs[1:3], refs[3:]
    for block in range(4):
        low = 512 * block
        dhid_ref[...] = dot_right_t(dm_ref[...], wd_ref[8 * block : 8 * block + 8].reshape(512, 640))

        def spread(rows, low=low):
            grad = dhid_ref[rows, :]
            dgu_ref[0, rows, low : low + 512] = (
                grad * slope_ref[rows, low : low + 512].astype(jnp.float32)
            ).astype(BF)
            dgu_ref[1, rows, low : low + 512] = (
                grad * gelu_ref[rows, low : low + 512].astype(jnp.float32)
            ).astype(BF)

        looped(512, 16, spread, 4)
    h3t_ref[...] = h3_ref[...].T
    for far in (1, 0):
        side = lax.rem(coords_ref[3] + far, 2)
        for block in range(4):
            low = 512 * block
            grad = dot(h3t_ref[...], dgu_ref[side, :, low : low + 512]).astype(BF)
            for spot in range(16):
                group, one, two = spot // 4, (spot // 2) % 2, spot % 2
                out_refs[far][group, one, two, :, low : low + 512] = grad[
                    40 * spot : 40 * spot + 40
                ]


def middle_backward(
    coords_ref, dgu_ref, mid_ref, branch_ref, cot_ref, gains_ref, perm_ref, own_ref, far_ref,
    dmid_ref, da_ref, gain_ref, rel_ref, plain_ref,
):
    core = coords_ref[3]
    for low in (0, 256):
        rows = slice(low, low + 256)
        total = dot_right_t(dgu_ref[core, rows, :], own_ref[...])
        total = total + dot_right_t(dgu_ref[1 - core, rows, :], far_ref[...])
        rel_ref[rows, :] = total.astype(BF)
    plain_ref[...] = dot_right_t(rel_ref[...], perm_ref[...])
    gain_one, gain_two = 1.0 + gains_ref[1:2, :], 1.0 + gains_ref[2:3, :]

    def pull(rows, carry):
        pulled, term_two = pull_norm(mid_ref[rows, :], gain_two, plain_ref[rows, :])
        grad = cot_ref[rows, :].astype(jnp.float32) + pulled
        dmid_ref[rows, :] = grad
        pulled, term_one = pull_norm(branch_ref[rows, :], gain_one, grad)
        da_ref[rows, :] = pulled.astype(BF)
        return carry[0] + fold_rows(term_one), carry[1] + fold_rows(term_two)

    zero = jnp.zeros((8, 640), jnp.float32)
    gain_ref[0], gain_ref[1] = chunks(512, 32, pull, (zero, zero))


def attention_backward(
    coords_ref, da_ref, wo_ref, o_ref, prob_ref, qn_ref, kn_ref, vb_ref, q_ref, kv_ref, gains_ref,
    dqkv_ref, gain_ref, dwo_ref, do_ref, dqn_ref, dkn_ref, dv_ref, ds_ref, lifted_ref,
):
    for head in range(4):
        block = wo_ref[8 * head : 8 * head + 8].reshape(256, 640)
        do_ref[head] = dot_right_t(da_ref[...], block).astype(BF)
        grad = dot_left_t(o_ref[head], da_ref[...])
        dwo_ref[8 * head : 8 * head + 8] = grad.astype(BF).reshape(8, 32, 640)
    dkn_ref[...] = jnp.zeros_like(dkn_ref)
    dv_ref[...] = jnp.zeros_like(dv_ref)
    for block, (low, high) in enumerate(KEY_SPANS):
        rows, span = slice(128 * block, 128 * block + 128), high - low
        lifted_ref[:, 0:span] = dot_right_t(do_ref[:, rows, :].reshape(512, 256), vb_ref[low:high, :])

        def soften(part, carry, block=block, span=span):
            head, near = part.start // 128, 128 * block + part.start % 128
            near = slice(near, near + 32)
            delta = jnp.sum(
                do_ref[head, near, :].astype(jnp.float32) * o_ref[head, near, :].astype(jnp.float32),
                axis=-1,
                keepdims=True,
            )
            soft = prob_ref[block, part, 0:span].astype(jnp.float32)
            ds_ref[part, 0:span] = (soft * (lifted_ref[part, 0:span] - delta) * SCALE).astype(BF)
            return carry

        chunks(512, 32, soften, 0)
        all_ds = ds_ref[:, 0:span]
        all_rows = qn_ref[:, rows, :].reshape(512, 256)
        dqn_ref[:, rows, :] = dot(all_ds, kn_ref[low:high, :]).reshape(4, 128, 256)
        dkn_ref[low:high, :] += dot_left_t(all_ds, all_rows)
        dv_ref[low:high, :] += dot_left_t(
            prob_ref[block, :, 0:span], do_ref[:, rows, :].reshape(512, 256)
        )
    query_gain, key_gain = 1.0 + gains_ref[4:5, 0:256], 1.0 + gains_ref[5:6, 0:256]

    def pull(rows, carry):
        query_sum, key_sum = carry
        for head in range(4):
            pulled, term = pull_norm(q_ref[head, rows, :], query_gain, dqn_ref[head, rows, :])
            dqkv_ref[head // 2, rows, 256 * (head % 2) : 256 * (head % 2) + 256] = pulled.astype(BF)
            query_sum = query_sum + fold_rows(term)
        pulled, term = pull_norm(kv_ref[0, rows, :], key_gain, dkn_ref[rows, :])
        dqkv_ref[0, rows, 512:768] = pulled.astype(BF)
        dqkv_ref[1, rows, 512:768] = dv_ref[rows, :].astype(BF)
        return query_sum, key_sum + fold_rows(term)

    zero = jnp.zeros((8, 256), jnp.float32)
    gain_ref[0], gain_ref[1] = chunks(512, 32, pull, (zero, zero))


def input_backward(
    coords_ref, dqkv_ref, h1_ref, dwo_ref, tokens_ref, dmid_ref, perm_ref, gains_ref, gain_mid_ref,
    gain_head_ref, gain_down_ref, own_ref, far_ref, input_ref, *refs
):
    out_refs, (rel_ref, plain_ref, h1t_ref) = refs[:2], refs[2:]
    core = coords_ref[3]
    total = dot_right_t(dqkv_ref[core], own_ref[...]) + dot_right_t(dqkv_ref[1 - core], far_ref[...])
    rel_ref[...] = total.astype(BF)
    h1t_ref[...] = h1_ref[...].T
    plain_ref[...] = dot_right_t(rel_ref[...], perm_ref[...])
    gain_zero = 1.0 + gains_ref[0:1, :]

    def pull(rows, carry):
        pulled, term = pull_norm(tokens_ref[rows, :].astype(jnp.float32), gain_zero, plain_ref[rows, :])
        input_ref[rows, :] = dmid_ref[rows, :] + pulled
        return carry + fold_rows(term)

    sums = [chunks(512, 32, pull, jnp.zeros((8, 640), jnp.float32))]
    sums += [gain_mid_ref[0], gain_mid_ref[1], gain_down_ref[...]]
    lines = [jnp.sum(part, axis=0, keepdims=True) for part in sums]
    for part in range(2):
        line = jnp.sum(gain_head_ref[part], axis=0, keepdims=True)
        lines.append(jnp.concatenate([line, jnp.zeros((1, 384), jnp.float32)], axis=1))
    lines.append(jnp.zeros((2, 640), jnp.float32))
    gain_block = jnp.concatenate(lines, axis=0).astype(BF)
    for far, group, one, two, place in slots(coords_ref):
        out_refs[far][group, one, two, 0:32, 768:1408] = dwo_ref[place]
        out_refs[far][group, one, two, 32:40, 768:1408] = gain_block
    for far in range(2):
        side = lax.rem(core + far, 2)
        for part in range(3):
            low = 256 * part
            grad = dot(h1t_ref[...], dqkv_ref[side, :, low : low + 256]).astype(BF)
            for spot in range(16):
                group, one, two = spot // 4, (spot // 2) % 2, spot % 2
                out_refs[far][group, one, two, :, low : low + 256] = grad[
                    40 * spot : 40 * spot + 40
                ]


def call(kernel, coords, inputs, outs, scratch=(), megabytes=32, cost=(1, 1), anys=0):
    whole = pl.BlockSpec(memory_space=pltpu.VMEM)
    return pl.pallas_call(
        kernel,
        out_shape=outs,
        in_specs=[pl.BlockSpec(memory_space=pltpu.SMEM)] + [whole] * len(inputs),
        out_specs=jax.tree.map(lambda _: whole, outs),
        scratch_shapes=list(scratch),
        cost_estimate=pl.CostEstimate(
            flops=int(cost[0] * COST * 1e9), bytes_accessed=int(cost[1] * BYTES), transcendentals=0
        ),
        compiler_params=pltpu.CompilerParams(vmem_limit_bytes=megabytes * 1024 * 1024),
    )(coords, *inputs)


def rel_table():
    table = np.zeros((32, 1, 640), np.int32)
    for place in range(32):
        z, y, x, _ = np.unravel_index(place, DIMS)
        for group in range(4):
            for one in range(2):
                for two in range(2):
                    gap = gap_of(group, one, two)
                    chip = (((z + gap[0]) % 4) * 2 + (y + gap[1]) % 2) * 2 + (x + gap[2]) % 2
                    low = 160 * group + 80 * one + 40 * two
                    table[place, 0, low : low + 40] = 40 * chip + np.arange(40)
    return table


def shape(*sizes, kind=BF):
    return jax.ShapeDtypeStruct(sizes, kind)


def join(*values):
    return lax.optimization_barrier(values)


def narrow(left, right):
    return (wide(left) + wide(right)).astype(BF)


def scatter_across(keep, got):
    return shift(narrow(keep[1], got[1]), 1, 1), shift(narrow(keep[3], got[3]), 2, 1)


def scatter_sums(keep, got, far_a, far_b):
    sum_a = wide(keep[0]) + wide(got[0]) + wide(far_a)
    sum_b = wide(keep[2]) + wide(got[2]) + wide(far_b)
    return sum_a[0], sum_b[0], sum_a[1].astype(BF), sum_b[1].astype(BF)


def scatter_pair(keep, got, far_a, far_b):
    first, second, side_a, side_b = scatter_sums(keep, got, far_a, far_b)
    return first, second, shift(side_a, 2, 1), shift(side_b, 1, 1)


def scatter_along(sum_a, sum_b, side_a, side_b):
    last_a = sum_a + wide(side_a)
    last_b = sum_b + wide(side_b)
    return last_a[0], [last_a[1].astype(BF), last_b[0].astype(BF), last_b[1].astype(BF)]


def scatter_end(own, *others):
    for other in others:
        own = own + wide(other)
    return own


def block_fast(tokens, segment_ids, cotangent, weights, update_gateup):
    query_round, keyval_round, output_round, gateup_round, down_round, gains, heads = weights
    f32 = jnp.float32
    along, upward, sideways, core = own_coords()
    place = lax.axis_index("dp")
    coords = jnp.stack([along, upward, sideways, core]).astype(jnp.int32)
    index = lax.dynamic_index_in_dim(jnp.asarray(rel_table()), place, keepdims=False)
    tokens, cotangent = tokens.reshape(512, 640), cotangent.reshape(512, 640)
    segcol = segment_ids.reshape(512, 1)

    low = jnp.concatenate([query_round[:, :512], keyval_round[:, :256], gateup_round[:, 0]], axis=1)
    high = jnp.concatenate([query_round[:, 512:], keyval_round[:, 256:], gateup_round[:, 1]], axis=1)
    away, keep = swap_halves(core, low, high)
    got = shift(away, 3, 1)
    both = jnp.concatenate([jnp.where(core == 0, keep, got), jnp.where(core == 0, got, keep)], axis=0)
    spread = jnp.zeros((8, 640), BF)
    spread = lax.dynamic_update_slice(spread, gains, (0, place * gains.shape[1]))
    spread = lax.dynamic_update_slice(spread, heads, (4, place * heads.shape[1]))
    block_a = jnp.concatenate([both[:, :768], jnp.concatenate([output_round, spread], axis=0)], axis=1)
    block_g = both[:, 768:]

    near_a = gather_along(block_a)
    near_a, block_w, block_g = join(near_a, down_round, block_g)
    first, second = jnp.stack([near_a[0], near_a[1]]), jnp.stack([near_a[2], near_a[3]])
    first, second, block_w, block_g = join(first, second, block_w, block_g)
    pairs_a = [jnp.stack([first, shift(first, 2, 1)]), jnp.stack([second, shift(second, 1, 1)])]
    near_w = gather_along(block_w)
    pairs_a, near_w, block_g = join(pairs_a, near_w, block_g)
    mine_a = gather_across(*pairs_a)
    near_g = gather_along(block_g)
    pairs_w = gather_pair(near_w)
    mine_a, near_g = join(mine_a, near_g)
    pieces_a = gather_core(mine_a)
    pairs_g = gather_pair(near_g)
    pairs_g, pairs_w = join(pairs_g, pairs_w)
    mine_g = gather_across(*pairs_g)
    early_g = [shift(pair, 3, 1) for pair in pairs_g]
    h1, q, kv, qn, kn, vb, wo, gains_full, perm, own_qkv, far_qkv = call(
        project_forward,
        coords,
        [index, tokens, *pieces_a],
        [
            shape(512, 640), shape(4, 512, 256, kind=f32), shape(2, 512, 256, kind=f32),
            shape(4, 512, 256), shape(512, 256), shape(512, 256),
            shape(32, 32, 640), shape(8, 640, kind=f32), shape(640, 640), shape(640, 768), shape(640, 768),
        ],
        [pltpu.VMEM((512, 640), BF)],
        12,
        (5, 20),
    )
    qn, pairs_w = join(qn, pairs_w)
    mine_w = gather_across(*pairs_w)
    early_w = [shift(pair, 3, 1) for pair in pairs_w]
    prob, o, branch, mid, h3 = call(
        attention_forward,
        coords,
        [tokens, segment_ids, segcol, qn, kn, vb, wo, gains_full, perm],
        [
            shape(4, 512, 384), shape(4, 512, 256), shape(512, 640, kind=f32),
            shape(512, 640, kind=f32), shape(512, 640),
        ],
        [pltpu.VMEM((512, 640), BF), pltpu.VMEM((128, 384), f32), pltpu.VMEM((512, 384), f32)],
        12,
        (5, 20),
    )
    mine_g, h3, early_g = join(mine_g, h3, early_g)
    far_g = [early_g[0], shift(mine_g[1], 3, 1), early_g[1], shift(mine_g[3], 3, 1)]
    own, own_gu = call(
        gateup_own,
        coords,
        [h3, *mine_g],
        [shape(512, 2048, kind=f32), shape(640, 2048)],
        [],
        12,
        (6, 20),
    )
    far_g, own = join(far_g, own)
    slope, gelu, hidden, far_gu = call(
        gateup_forward,
        coords,
        [h3, own, *far_g],
        [shape(512, 2048)] * 3 + [shape(640, 2048)],
        [pltpu.VMEM((512, 512), f32)],
        12,
        (6, 20),
    )
    hidden, mine_w = join(hidden, mine_w)
    pieces_w = mine_w + [early_w[0], shift(mine_w[1], 3, 1), early_w[1], shift(mine_w[3], 3, 1)]
    result, dm, gain_down, wd, keep_w, send_w = call(
        down_both,
        coords,
        [hidden, mid, cotangent, gains_full, *pieces_w],
        [shape(512, 640), shape(512, 640), shape(8, 640, kind=f32), shape(32, 64, 640)]
        + [shape(4, 2, 2, 64, 640)] * 2,
        [pltpu.VMEM((512, 640), f32), pltpu.VMEM((32, 64, 640), BF)],
        12,
        (6, 20),
    )
    got_w = shift(send_w, 3, 1)
    dgu, keep_g, send_g = call(
        gateup_backward,
        coords,
        [dm, wd, slope, gelu, h3],
        [shape(2, 512, 2048)] + [shape(4, 2, 2, 40, 2048)] * 2,
        [pltpu.VMEM((512, 512), f32), pltpu.VMEM((640, 512), BF)],
        12,
        (8, 20),
    )
    dgu, got_w, send_g = join(dgu, got_w, send_g)
    far_w = scatter_across(keep_w, got_w)
    got_g = shift(send_g, 3, 1)
    dmid, da, gain_mid = call(
        middle_backward,
        coords,
        [dgu, mid, branch, cotangent, gains_full, perm, own_gu, far_gu],
        [shape(512, 640, kind=f32), shape(512, 640), shape(2, 8, 640, kind=f32)],
        [pltpu.VMEM((512, 640), BF), pltpu.VMEM((512, 640), f32)],
        12,
        (8, 20),
    )
    da, got_g, far_w = join(da, got_g, far_w)
    side_w = scatter_pair(keep_w, got_w, *far_w)
    far_g = scatter_across(keep_g, got_g)
    dqkv, gain_head, dwo = call(
        attention_backward,
        coords,
        [da, wo, o, prob, qn, kn, vb, q, kv, gains_full],
        [shape(2, 512, 768), shape(2, 8, 256, kind=f32), shape(32, 32, 640)],
        [
            pltpu.VMEM((4, 512, 256), BF),
            pltpu.VMEM((4, 512, 256), f32), pltpu.VMEM((512, 256), f32), pltpu.VMEM((512, 256), f32),
            pltpu.VMEM((512, 384), BF), pltpu.VMEM((512, 384), f32),
        ],
        12,
        (6, 20),
    )
    dqkv, side_w = join(dqkv, side_w)
    own_w, along_w = scatter_along(*side_w)
    along_w = [shift(part, 0, step + 1) for step, part in enumerate(along_w)]
    input_grad, keep_a, send_a = call(
        input_backward,
        coords,
        [dqkv, h1, dwo, tokens, dmid, perm, gains_full, gain_mid, gain_head, gain_down, own_qkv, far_qkv],
        [shape(512, 640, kind=f32)] + [shape(4, 2, 2, 40, 1408)] * 2,
        [pltpu.VMEM((512, 640), BF), pltpu.VMEM((512, 640), f32), pltpu.VMEM((640, 512), BF)],
        12,
        (6, 20),
    )
    send_a, far_g, along_w = join(send_a, far_g, along_w)
    down_grad = scatter_end(own_w, *along_w)
    got_a = shift(send_a, 3, 1)
    side_g = scatter_pair(keep_g, got_g, *far_g)
    got_a, side_g = join(got_a, side_g)
    first, second = narrow(keep_a[1], got_a[1]), narrow(keep_a[3], got_a[3])
    first, second, side_g = join(first, second, side_g)
    far_a = shift(first, 1, 1), shift(second, 2, 1)
    own_g, along_g = scatter_along(*side_g)
    ends_g = [shift(along_g[0], 0, 1), shift(along_g[2], 0, 3)]
    far_a, ends_g, across_g = join(far_a, ends_g, along_g[1])
    first, second, *side_a = scatter_sums(keep_a, got_a, *far_a)
    side_a, across_g = join(side_a, across_g)
    side_a = shift(side_a[0], 2, 1), shift(side_a[1], 1, 1)
    across_g = shift(across_g, 0, 2)
    side_a, across_g = join(side_a, across_g)
    own_a, along_a = scatter_along(first, second, *side_a)
    along_a = [shift(part, 0, step + 1) for step, part in enumerate(along_a)]
    gateup_sum = scatter_end(own_g, across_g, *ends_g)

    def own_rows(both):
        away, keep = swap_halves(core, both[:20], both[20:])
        got = shift(away, 3, 1)
        return jnp.where(core == 0, keep, got), jnp.where(core == 0, got, keep)

    low, high = own_rows(gateup_sum)
    gateup_grad = with_layout_constraint(jnp.stack([low, high], axis=1), Layout((0, 1, 2)))
    gateup_done = (gateup_grad, *update_gateup(gateup_grad))
    along_a, gateup_done = join(along_a, gateup_done)
    rest = scatter_end(own_a, *along_a)
    output_grad = rest[:32, 768:]
    norm_grad = lax.dynamic_slice(rest[32:36, 768:], (0, place * 20), (4, 20))
    qknorm_grad = lax.dynamic_slice(rest[36:38, 768:], (0, place * 8), (2, 8))

    low, high = own_rows(rest[:, :768])
    query_grad = jnp.concatenate([low[:, :512], high[:, :512]], axis=1)
    keyval_grad = jnp.concatenate([low[:, 512:], high[:, 512:]], axis=1)
    grads = (query_grad, keyval_grad, output_grad, gateup_done[0], down_grad, norm_grad, qknorm_grad)
    return result[None], input_grad[None], grads, gateup_done[1:]


def norm_apply(values, gain_vector):
    inverse = lax.rsqrt(jnp.mean(values * values, axis=-1, keepdims=True) + norm_epsilon)
    return values * inverse * (1.0 + gain_vector)


def gelu_product(gate_part, up_part):
    return jax.nn.gelu(gate_part, approximate=True) * up_part


def block_scores(query_normed, key_normed, segments, row_start, row_stop, score_scale):
    positions = jnp.arange(row_stop)
    same_doc = segments[row_start:row_stop, None] == segments[None, :row_stop]
    causal = positions[None, :] <= positions[row_start:row_stop, None]
    allowed = (same_doc & causal)[None]
    scores = (
        jnp.einsum("qhd,kd->hqk", query_normed, key_normed, preferred_element_type=jnp.float32)
        * score_scale
    )
    return (jnp.where(allowed, scores, -1e30), allowed)


def attend_forward(query_normed, key_normed, value_round, segments, score_scale):
    length = query_normed.shape[0]
    block_rows = min(512, length)
    masked, allowed = block_scores(query_normed, key_normed, segments, 0, block_rows, score_scale)
    row_max = jnp.max(masked, axis=-1, keepdims=True)
    row_total = jnp.sum(jnp.where(allowed, jnp.exp(masked - row_max), 0.0), axis=-1, keepdims=True)
    log_total = row_max + jnp.log(row_total)
    soft_round = jnp.where(allowed, jnp.exp(masked - log_total), 0.0).astype(jnp.bfloat16)
    attended_block = jnp.einsum(
        "hqk,kd->qhd", soft_round, value_round, preferred_element_type=jnp.float32
    )
    attended_parts = attended_block.astype(jnp.bfloat16)
    total_parts = log_total[:, :, 0]
    return (attended_parts, total_parts)


def attend_backward(
    query_normed,
    key_normed,
    value_round,
    segments,
    log_totals,
    attended,
    grad_attended,
    score_scale,
):
    length = query_normed.shape[0]
    head_dim = key_normed.shape[1]
    block_rows = min(512, length)
    row_delta = jnp.sum(grad_attended.astype(jnp.float32) * attended.astype(jnp.float32), axis=-1)
    grad_key_sum = jnp.zeros((length, head_dim), jnp.float32)
    grad_value_sum = jnp.zeros((length, head_dim), jnp.float32)
    masked, allowed = block_scores(query_normed, key_normed, segments, 0, block_rows, score_scale)
    soft_weights = jnp.where(allowed, jnp.exp(masked - log_totals[:, 0:block_rows, None]), 0.0)
    soft_round = soft_weights.astype(jnp.bfloat16)
    grad_value_sum = grad_value_sum.at[:block_rows].add(
        jnp.einsum("hqk,qhd->kd", soft_round, grad_attended, preferred_element_type=jnp.float32)
    )
    grad_soft = jnp.einsum(
        "qhd,kd->hqk", grad_attended, value_round, preferred_element_type=jnp.float32
    )
    delta_block = row_delta.T[:, :, None]
    grad_scores = (soft_weights * (grad_soft - delta_block) * score_scale).astype(jnp.bfloat16)
    grad_query_parts = jnp.einsum(
        "hqk,kd->qhd", grad_scores, key_normed, preferred_element_type=jnp.float32
    )
    grad_key_sum = grad_key_sum.at[:block_rows].add(
        jnp.einsum("hqk,qhd->kd", grad_scores, query_normed, preferred_element_type=jnp.float32)
    )
    return (grad_query_parts, grad_key_sum, grad_value_sum)


def adam_update(parameter, gradient, first_moment, second_moment, decay_value):
    first_new = beta_one * first_moment + (1.0 - beta_one) * gradient
    second_new = beta_two * second_moment + (1.0 - beta_two) * gradient * gradient
    first_hat = first_new / (1.0 - beta_one**STEP)
    second_hat = second_new / (1.0 - beta_two**STEP)
    parameter_new = (
        parameter
        - learn_rate * first_hat / (jnp.sqrt(second_hat) + adam_epsilon)
        - learn_rate * decay_value * parameter
    )
    return (parameter_new, first_new, second_new)


def block_plain(tokens, segment_ids, cotangent, weights, update_gateup):
    query_full, keyval_full, output_full, gateup_full, down_full, main_gains, head_gains = gather_plain(*weights)
    seq_count, length, model_width = tokens.shape
    row_count = seq_count * length
    head_dim = head_gains.shape[1]
    head_count = query_full.shape[1] // head_dim
    hidden_units = gateup_full.shape[1] // 2
    score_scale = head_dim ** (-0.5)
    inputs = tokens.reshape(row_count, model_width).astype(jnp.float32)
    normed_in = norm_apply(inputs, main_gains[0]).astype(jnp.bfloat16)
    queries = jnp.dot(normed_in, query_full, preferred_element_type=jnp.float32).reshape(
        row_count, head_count, head_dim
    )
    keyvals = jnp.dot(normed_in, keyval_full, preferred_element_type=jnp.float32)
    key_rows = keyvals[:, :head_dim]
    value_rows = keyvals[:, head_dim:]
    query_normed = norm_apply(queries, head_gains[0]).astype(jnp.bfloat16)
    key_normed = norm_apply(key_rows, head_gains[1]).astype(jnp.bfloat16)
    value_round = value_rows.astype(jnp.bfloat16)
    seq_index = 0
    attended_seq, totals_seq = attend_forward(
        query_normed, key_normed, value_round, segment_ids[seq_index], score_scale
    )
    total_parts = [totals_seq]
    attended_flat = attended_seq.reshape(row_count, head_count * head_dim)
    branch = jnp.dot(attended_flat, output_full, preferred_element_type=jnp.float32)
    middle = inputs + norm_apply(branch, main_gains[1])
    normed_mid = norm_apply(middle, main_gains[2]).astype(jnp.bfloat16)
    gate_up = jnp.dot(
        normed_mid,
        gateup_full,
        preferred_element_type=jnp.float32,
    )
    gate_part = gate_up[:, :hidden_units]
    up_part = gate_up[:, hidden_units:]
    hidden = gelu_product(gate_part, up_part).astype(jnp.bfloat16)
    down_out = jnp.dot(hidden, down_full, preferred_element_type=jnp.float32)
    result = (middle + norm_apply(down_out, main_gains[3])).astype(jnp.bfloat16)
    query_back, keyval_back, output_back, gateup_back, down_back = (
        query_full,
        keyval_full,
        output_full,
        gateup_full,
        down_full,
    )
    gateup_flat = gateup_back
    grad_out = cotangent.reshape(row_count, model_width).astype(jnp.float32)
    _, pull_back = jax.vjp(norm_apply, down_out, main_gains[3])
    grad_down_out, grad_gain_three = pull_back(grad_out)
    grad_down_round = grad_down_out.astype(jnp.bfloat16)
    grad_down = jnp.dot(hidden.T, grad_down_round, preferred_element_type=jnp.float32)
    grad_hidden = jnp.dot(grad_down_round, down_back.T, preferred_element_type=jnp.float32)
    _, pull_back = jax.vjp(gelu_product, gate_part, up_part)
    grad_gate, grad_up = pull_back(grad_hidden)
    grad_gate_up = jnp.concatenate([grad_gate, grad_up], axis=1).astype(jnp.bfloat16)
    grad_gateup = jnp.dot(normed_mid.T, grad_gate_up, preferred_element_type=jnp.float32)
    grad_normed_mid = jnp.dot(grad_gate_up, gateup_flat.T, preferred_element_type=jnp.float32)
    _, pull_back = jax.vjp(norm_apply, middle, main_gains[2])
    grad_mid_norm, grad_gain_two = pull_back(grad_normed_mid)
    grad_middle = grad_out + grad_mid_norm
    _, pull_back = jax.vjp(norm_apply, branch, main_gains[1])
    grad_branch, grad_gain_one = pull_back(grad_middle)
    grad_branch_round = grad_branch.astype(jnp.bfloat16)
    grad_output = jnp.dot(attended_flat.T, grad_branch_round, preferred_element_type=jnp.float32)
    grad_attended = (
        jnp.dot(grad_branch_round, output_back.T, preferred_element_type=jnp.float32)
        .reshape(row_count, head_count, head_dim)
        .astype(jnp.bfloat16)
    )
    seq_index = 0
    grad_query_seq, grad_key_seq, grad_value_seq = attend_backward(
        query_normed,
        key_normed,
        value_round,
        segment_ids[seq_index],
        total_parts[seq_index],
        attended_seq,
        grad_attended,
        score_scale,
    )
    _, pull_back = jax.vjp(norm_apply, queries, head_gains[0])
    grad_queries, grad_head_zero = pull_back(grad_query_seq)
    _, pull_back = jax.vjp(norm_apply, key_rows, head_gains[1])
    grad_keys, grad_head_one = pull_back(grad_key_seq)
    grad_query_round = grad_queries.reshape(row_count, head_count * head_dim).astype(jnp.bfloat16)
    grad_keyval_round = jnp.concatenate([grad_keys, grad_value_seq], axis=1).astype(jnp.bfloat16)
    grad_query = jnp.dot(normed_in.T, grad_query_round, preferred_element_type=jnp.float32)
    grad_keyval = jnp.dot(normed_in.T, grad_keyval_round, preferred_element_type=jnp.float32)
    grad_normed_in = jnp.dot(
        grad_query_round, query_back.T, preferred_element_type=jnp.float32
    ) + jnp.dot(grad_keyval_round, keyval_back.T, preferred_element_type=jnp.float32)
    _, pull_back = jax.vjp(norm_apply, inputs, main_gains[0])
    grad_in_norm, grad_gain_zero = pull_back(grad_normed_in)
    input_grad = grad_middle + grad_in_norm
    grad_gains = jnp.stack([grad_gain_zero, grad_gain_one, grad_gain_two, grad_gain_three])
    grad_heads = jnp.stack([grad_head_zero, grad_head_one])
    gradients = scatter_plain(
        grad_query, grad_keyval, grad_output, grad_gateup, grad_down, grad_gains, grad_heads
    )
    result_out = result.reshape(seq_count, length, model_width)
    input_out = input_grad.reshape(seq_count, length, model_width)
    return result_out, input_out, gradients, update_gateup(gradients[3])


def per_device(
    tokens,
    segment_ids,
    cotangent,
    query_weight,
    keyval_weight,
    output_weight,
    gateup_weight,
    down_weight,
    norm_gains,
    qknorm_gains,
    query_mean,
    keyval_mean,
    output_mean,
    gateup_mean,
    down_mean,
    norm_mean,
    qknorm_mean,
    query_square,
    keyval_square,
    output_square,
    gateup_square,
    down_square,
    norm_square,
    qknorm_square,
):
    query_round = query_weight.astype(jnp.bfloat16)
    keyval_round = keyval_weight.astype(jnp.bfloat16)
    output_round = output_weight.astype(jnp.bfloat16)
    gateup_round = gateup_weight.astype(jnp.bfloat16)
    down_round = down_weight.astype(jnp.bfloat16)
    gains_round = norm_gains.astype(jnp.bfloat16)
    headgain_round = qknorm_gains.astype(jnp.bfloat16)
    weights = (
        query_round, keyval_round, output_round, gateup_round, down_round, gains_round, headgain_round
    )

    def update_gateup(gradient):
        return adam_update(gateup_weight, gradient, gateup_mean, gateup_square, decay_coef)

    block = block_fast if lax.axis_size("dp") == 32 else block_plain
    result_out, input_out, gradients, gateup_done = block(
        tokens, segment_ids, cotangent, weights, update_gateup
    )
    parameters = (
        query_weight,
        keyval_weight,
        output_weight,
        gateup_weight,
        down_weight,
        norm_gains,
        qknorm_gains,
    )
    firsts = (query_mean, keyval_mean, output_mean, gateup_mean, down_mean, norm_mean, qknorm_mean)
    seconds = (
        query_square,
        keyval_square,
        output_square,
        gateup_square,
        down_square,
        norm_square,
        qknorm_square,
    )
    decays = (decay_coef, decay_coef, decay_coef, decay_coef, decay_coef, 0.0, 0.0)
    updates = [
        adam_update(
            parameters[place], gradients[place], firsts[place], seconds[place], decays[place]
        )
        if place != 3
        else gateup_done
        for place in range(7)
    ]
    news = tuple((update[0] for update in updates))
    first_news = tuple((update[1] for update in updates))
    second_news = tuple((update[2] for update in updates))
    return (result_out, input_out) + gradients + news + first_news + second_news


def solution(mesh):
    in_specs = (
        P("dp", None, None),
        P("dp", None),
        P("dp", None, None),
        P("dp", None),
        P("dp", None),
        P("dp", None),
        P("dp", None, None),
        P("dp", None),
        P(None, "dp"),
        P(None, "dp"),
        P("dp", None),
        P("dp", None),
        P("dp", None),
        P("dp", None, None),
        P("dp", None),
        P(None, "dp"),
        P(None, "dp"),
        P("dp", None),
        P("dp", None),
        P("dp", None),
        P("dp", None, None),
        P("dp", None),
        P(None, "dp"),
        P(None, "dp"),
    )
    out_specs = (
        P("dp", None, None),
        P("dp", None, None),
        P("dp", None),
        P("dp", None),
        P("dp", None),
        P("dp", None, None),
        P("dp", None),
        P(None, "dp"),
        P(None, "dp"),
        P("dp", None),
        P("dp", None),
        P("dp", None),
        P("dp", None, None),
        P("dp", None),
        P(None, "dp"),
        P(None, "dp"),
        P("dp", None),
        P("dp", None),
        P("dp", None),
        P("dp", None, None),
        P("dp", None),
        P(None, "dp"),
        P(None, "dp"),
        P("dp", None),
        P("dp", None),
        P("dp", None),
        P("dp", None, None),
        P("dp", None),
        P(None, "dp"),
        P(None, "dp"),
    )
    return jax.shard_map(
        per_device, mesh=mesh, in_specs=in_specs, out_specs=out_specs, check_vma=False
    )
```

```python
import jax
import jax.numpy as jnp
import numpy as np
from jax import lax
from jax.experimental import pallas as pl
from jax.experimental.layout import Layout, with_layout_constraint
from jax.experimental.pallas import tpu as pltpu
from jax.sharding import PartitionSpec as P

STEP = 3
norm_epsilon = 1e-06
beta_one = 0.9
beta_two = 0.999
learn_rate = 0.03
decay_coef = 0.1
adam_epsilon = 1e-08

DIMS = (4, 2, 2, 2)
BF = jnp.bfloat16


def shift_perm(axis, amount):
    pairs = []
    for place in range(int(np.prod(DIMS))):
        spot = list(np.unravel_index(place, DIMS))
        spot[axis] = (spot[axis] + amount) % DIMS[axis]
        pairs.append((place, int(np.ravel_multi_index(spot, DIMS))))
    return pairs


def shift(values, axis, amount):
    with jax.named_scope("zyxc"[axis] + str(amount % DIMS[axis])):
        return lax.ppermute(values, "dp", shift_perm(axis, amount))


def own_coords():
    place = lax.axis_index("dp")
    return place // 8, (place // 4) % 2, (place // 2) % 2, place % 2


def after(values, *others):
    return lax.optimization_barrier((values, others))[0]


def gather_along(block):
    return [block] + [shift(block, 0, -step) for step in (1, 2, 3)]


def gather_pair(near):
    first = jnp.stack([near[0], near[1]])
    second = jnp.stack([near[2], near[3]])
    return jnp.stack([first, shift(first, 2, 1)]), jnp.stack([second, shift(second, 1, 1)])


def gather_across(pair_a, pair_b):
    return [pair_a, shift(pair_a, 1, 1), pair_b, shift(pair_b, 2, 1)]


def gather_core(mine):
    return mine + [shift(piece, 3, 1) for piece in mine]


def wide(values):
    return values.astype(jnp.float32)


def swap_halves(core, low, high):
    return jnp.where(core == 0, high, low), jnp.where(core == 0, low, high)


def gather_plain(query_round, keyval_round, output_round, gateup_round, down_round, gains_round, headgain_round):
    gateup_full = lax.all_gather(gateup_round, "dp", axis=0, tiled=True)
    return (
        lax.all_gather(query_round, "dp", axis=0, tiled=True),
        lax.all_gather(keyval_round, "dp", axis=0, tiled=True),
        lax.all_gather(output_round, "dp", axis=0, tiled=True),
        gateup_full.reshape(gateup_full.shape[0], -1),
        lax.all_gather(down_round, "dp", axis=0, tiled=True),
        lax.all_gather(gains_round, "dp", axis=1, tiled=True).astype(jnp.float32),
        lax.all_gather(headgain_round, "dp", axis=1, tiled=True).astype(jnp.float32),
    )


def scatter_plain(grad_query, grad_keyval, grad_output, grad_gateup, grad_down, grad_gains, grad_heads):
    rows = grad_gateup.shape[0]
    return (
        lax.psum_scatter(grad_query, "dp", scatter_dimension=0, tiled=True),
        lax.psum_scatter(grad_keyval, "dp", scatter_dimension=0, tiled=True),
        lax.psum_scatter(grad_output, "dp", scatter_dimension=0, tiled=True),
        lax.psum_scatter(grad_gateup.reshape(rows, 2, -1), "dp", scatter_dimension=0, tiled=True),
        lax.psum_scatter(grad_down, "dp", scatter_dimension=0, tiled=True),
        lax.psum_scatter(grad_gains, "dp", scatter_dimension=1, tiled=True),
        lax.psum_scatter(grad_heads, "dp", scatter_dimension=1, tiled=True),
    )


BYTES = 1e6
COST = 1.0
HALF = 1024 // 2
SCALE = 256 ** (-0.5)
KEY_SPANS = ((0, 128), (0, 256), (0, 384), (128, 512))
TANH_SLOPE = (2.0 / np.pi) ** 0.5
TANH_CUBE = 0.044715


def dot(left, right):
    return jnp.dot(left, right, preferred_element_type=jnp.float32)


def dot_right_t(left, right):
    return lax.dot_general(left, right, (((1,), (1,)), ((), ())), preferred_element_type=jnp.float32)


def dot_left_t(left, right):
    return lax.dot_general(left, right, (((0,), (0,)), ((), ())), preferred_element_type=jnp.float32)


def inverse_rms(values):
    return lax.rsqrt(jnp.mean(values * values, axis=-1, keepdims=True) + norm_epsilon)


def pull_norm(values, gain_plus, grad):
    inverse = inverse_rms(values)
    unit = values * inverse
    scaled = grad * gain_plus
    return inverse * (scaled - unit * jnp.mean(scaled * unit, axis=-1, keepdims=True)), grad * unit


def fold_rows(values):
    rows, columns = values.shape
    return jnp.sum(values.reshape(rows // 8, 8, columns), axis=0)


def chunks(count, size, body, carry):
    for low in range(0, count, size):
        carry = body(slice(low, low + size), carry)
    return carry


def group_rows(piece_ref, low, high):
    return piece_ref[:, :, :, low:high].reshape(160, high - low)


def chip_at(coords_ref, gap):
    along = lax.rem(coords_ref[0] + gap[0], 4)
    upward = lax.rem(coords_ref[1] + gap[1], 2)
    sideways = lax.rem(coords_ref[2] + gap[2], 2)
    return (along * 2 + upward) * 2 + sideways


def gap_of(group, one, two):
    return (two, group, one) if group < 2 else (2 + two, one, group - 2)


def slots(coords_ref):
    for far in range(2):
        core = lax.rem(coords_ref[3] + far, 2)
        for group in range(4):
            for one in range(2):
                for two in range(2):
                    yield far, group, one, two, 2 * chip_at(coords_ref, gap_of(group, one, two)) + core


def place_rows(out_ref, piece_refs, low, high):
    for group in range(4):
        for one in range(2):
            for two in range(2):
                row = 160 * group + 80 * one + 40 * two
                out_ref[row : row + 40, :] = piece_refs[group][one, two, :, low:high]


def project_forward(coords_ref, index_ref, tokens_ref, *refs):
    piece_refs, refs = refs[:8], refs[8:]
    (
        h1_ref, q_ref, kv_ref, qn_ref, kn_ref, vb_ref, wo_ref, gains_ref, perm_ref, own_ref, far_ref, plain_ref
    ) = refs
    for far, group, one, two, place in slots(coords_ref):
        wo_ref[place] = piece_refs[4 * far + group][one, two, 0:32, 768:1408]
    gains = jnp.zeros((8, 640), jnp.float32)
    for far in range(2):
        for group in range(4):
            for one in range(2):
                for two in range(2):
                    gains = gains + piece_refs[4 * far + group][one, two, 32:40, 768:1408].astype(jnp.float32)
    gains_ref[...] = gains
    core = coords_ref[3]

    def make_perm(rows, carry):
        place = lax.broadcasted_iota(jnp.int32, (64, 640), 0) + rows.start
        perm_ref[rows, :] = jnp.where(place == index_ref[...], 1.0, 0.0).astype(BF)
        return carry

    chunks(640, 64, make_perm, 0)
    gain_zero = 1.0 + gains_ref[0:1, :]

    def norm_in(rows, carry):
        values = tokens_ref[rows, :].astype(jnp.float32)
        plain_ref[rows, :] = (values * inverse_rms(values) * gain_zero).astype(BF)
        return carry

    chunks(512, 32, norm_in, 0)
    h1_ref[...] = dot(plain_ref[...], perm_ref[...]).astype(BF)
    for far, weight_ref in enumerate((own_ref, far_ref)):
        place_rows(weight_ref, piece_refs[4 * far : 4 * far + 4], 0, 768)
        side = lax.rem(core + far, 2)
        for part in range(3):
            total = dot(h1_ref[...], weight_ref[:, 256 * part : 256 * part + 256])
            if part < 2:
                q_ref[2 * side + part] = total
            else:
                kv_ref[side] = total
    query_gain, key_gain = 1.0 + gains_ref[4:5, 0:256], 1.0 + gains_ref[5:6, 0:256]

    def norm_heads(rows, carry):
        for head in range(4):
            values = q_ref[head, rows, :]
            qn_ref[head, rows, :] = (values * inverse_rms(values) * query_gain).astype(BF)
        values = kv_ref[0, rows, :]
        kn_ref[rows, :] = (values * inverse_rms(values) * key_gain).astype(BF)
        vb_ref[rows, :] = kv_ref[1, rows, :].astype(BF)
        return carry

    chunks(512, 64, norm_heads, 0)


def attention_forward(
    coords_ref, tokens_ref, segrow_ref, segcol_ref, qn_ref, kn_ref, vb_ref, wo_ref, gains_ref, perm_ref,
    prob_ref, o_ref, branch_ref, mid_ref, h3_ref, plain_ref, bias_ref, score_ref,
):
    for block, (low, high) in enumerate(KEY_SPANS):
        rows, span = slice(128 * block, 128 * block + 128), high - low
        row_at = lax.broadcasted_iota(jnp.int32, (128, span), 0) + 128 * block
        key_at = lax.broadcasted_iota(jnp.int32, (128, span), 1) + low
        allowed = (segcol_ref[rows, :] == segrow_ref[:, low:high]) & (key_at <= row_at)
        bias_ref[:, 0:span] = jnp.where(allowed, 0.0, -1e30)
        score_ref[:, 0:span] = dot_right_t(qn_ref[:, rows, :].reshape(512, 256), kn_ref[low:high, :])

        def soften(part, carry, block=block, span=span):
            near = slice(part.start % 128, part.start % 128 + 32)
            scores = score_ref[part, 0:span] * SCALE + bias_ref[near, 0:span]
            powers = jnp.exp(scores - jnp.max(scores, axis=-1, keepdims=True))
            inverse = 1.0 / jnp.sum(powers, axis=-1, keepdims=True)
            prob_ref[block, part, 0:span] = (powers * inverse).astype(BF)
            return carry

        chunks(512, 32, soften, 0)
        mixed = dot(prob_ref[block, :, 0:span], vb_ref[low:high, :])
        o_ref[:, rows, :] = mixed.astype(BF).reshape(4, 128, 256)
    total = jnp.zeros((512, 640), jnp.float32)
    for head in range(4):
        total = total + dot(o_ref[head], wo_ref[8 * head : 8 * head + 8].reshape(256, 640))
    branch_ref[...] = total
    gain_one, gain_two = 1.0 + gains_ref[1:2, :], 1.0 + gains_ref[2:3, :]

    def norm_mid(rows, carry):
        values = branch_ref[rows, :]
        middle = tokens_ref[rows, :].astype(jnp.float32) + values * inverse_rms(values) * gain_one
        mid_ref[rows, :] = middle
        plain_ref[rows, :] = (middle * inverse_rms(middle) * gain_two).astype(BF)
        return carry

    chunks(512, 32, norm_mid, 0)
    h3_ref[...] = dot(plain_ref[...], perm_ref[...]).astype(BF)


def gateup_own(coords_ref, h3_ref, *refs):
    piece_refs, (own_ref, weight_ref) = refs[:4], refs[4:]
    place_rows(weight_ref, piece_refs, 0, 2048)
    for block in range(4):
        low = 512 * block
        own_ref[:, low : low + 512] = dot(h3_ref[...], weight_ref[:, low : low + 512])


def gateup_forward(coords_ref, h3_ref, own_ref, *refs):
    piece_refs, (slope_ref, gelu_ref, hidden_ref, weight_ref, far_ref) = refs[:4], refs[4:]
    first = jnp.full((16, 512), coords_ref[3]) == 0
    place_rows(weight_ref, piece_refs, 0, 2048)
    for block in range(4):
        low = 512 * block
        spot = block % 2
        far_ref[spot] = dot(h3_ref[...], weight_ref[:, low : low + 512])

        def activate(rows, low=low, spot=spot):
            own, far = own_ref[rows, low : low + 512], far_ref[spot, rows, :]
            gate, up = jnp.where(first, own, far), jnp.where(first, far, own)
            square = gate * gate
            bend = jnp.tanh(gate * (TANH_SLOPE + (TANH_SLOPE * TANH_CUBE) * square))
            weight = 0.5 + 0.5 * bend
            rise = gate * (2.0 * TANH_SLOPE + (6.0 * TANH_SLOPE * TANH_CUBE) * square)
            gelu = gate * weight
            slope = weight + (weight * rise) * (1.0 - weight)
            slope_ref[rows, low : low + 512] = (slope * up).astype(BF)
            gelu_ref[rows, low : low + 512] = gelu.astype(BF)
            hidden_ref[rows, low : low + 512] = (gelu * up).astype(BF)

        for start in range(0, 512, 16):
            activate(slice(start, start + 16))


def down_both(coords_ref, hidden_ref, mid_ref, cot_ref, gains_ref, *refs):
    piece_refs, refs = refs[:8], refs[8:]
    (result_ref, dm_ref, gain_ref, wd_ref), refs = refs[:4], refs[4:]
    out_refs, (product_ref, natural_ref) = refs[:2], refs[2:]
    for far, group, one, two, place in slots(coords_ref):
        wd_ref[place] = piece_refs[4 * far + group][one, two]
    weights = wd_ref[...].reshape(2048, 640)
    for low in (0, 256):
        product_ref[low : low + 256, :] = dot(hidden_ref[low : low + 256, :], weights)
    gain_three = 1.0 + gains_ref[3:4, :]

    def finish(rows, carry):
        values = product_ref[rows, :]
        grad = cot_ref[rows, :].astype(jnp.float32)
        result_ref[rows, :] = (mid_ref[rows, :] + values * inverse_rms(values) * gain_three).astype(BF)
        pulled, term = pull_norm(values, gain_three, grad)
        dm_ref[rows, :] = pulled.astype(BF)
        return carry + fold_rows(term)

    gain_ref[...] = chunks(512, 32, finish, jnp.zeros((8, 640), jnp.float32))
    for block in range(8):
        grad = dot_left_t(hidden_ref[:, 256 * block : 256 * block + 256], dm_ref[...])
        natural_ref[4 * block : 4 * block + 4] = grad.astype(BF).reshape(4, 64, 640)
    for far, group, one, two, place in slots(coords_ref):
        out_refs[far][group, one, two] = natural_ref[place]


def gateup_backward(coords_ref, dm_ref, wd_ref, slope_ref, gelu_ref, h3_ref, *refs):
    dgu_ref, out_refs, (dhid_ref, h3t_ref) = refs[0], refs[1:3], refs[3:]
    for block in range(4):
        low = 512 * block
        spot = block % 2
        dhid_ref[spot] = dot_right_t(dm_ref[...], wd_ref[8 * block : 8 * block + 8].reshape(512, 640))

        def spread(rows, low=low, spot=spot):
            grad = dhid_ref[spot, rows, :]
            dgu_ref[0, rows, low : low + 512] = (
                grad * slope_ref[rows, low : low + 512].astype(jnp.float32)
            ).astype(BF)
            dgu_ref[1, rows, low : low + 512] = (
                grad * gelu_ref[rows, low : low + 512].astype(jnp.float32)
            ).astype(BF)

        for start in range(0, 512, 16):
            spread(slice(start, start + 16))
    h3t_ref[...] = h3_ref[...].T
    for far in (1, 0):
        side = lax.rem(coords_ref[3] + far, 2)
        for block in range(4):
            low = 512 * block
            grad = dot(h3t_ref[...], dgu_ref[side, :, low : low + 512]).astype(BF)
            for spot in range(16):
                group, one, two = spot // 4, (spot // 2) % 2, spot % 2
                out_refs[far][group, one, two, :, low : low + 512] = grad[
                    40 * spot : 40 * spot + 40
                ]


def middle_backward(
    coords_ref, dgu_ref, mid_ref, branch_ref, cot_ref, gains_ref, perm_ref, own_ref, far_ref,
    dmid_ref, da_ref, gain_ref, rel_ref, plain_ref,
):
    core = coords_ref[3]
    for low in (0, 256):
        rows = slice(low, low + 256)
        total = dot_right_t(dgu_ref[core, rows, :], own_ref[...])
        total = total + dot_right_t(dgu_ref[1 - core, rows, :], far_ref[...])
        rel_ref[rows, :] = total.astype(BF)
    plain_ref[...] = dot_right_t(rel_ref[...], perm_ref[...])
    gain_one, gain_two = 1.0 + gains_ref[1:2, :], 1.0 + gains_ref[2:3, :]

    def pull(rows, carry):
        pulled, term_two = pull_norm(mid_ref[rows, :], gain_two, plain_ref[rows, :])
        grad = cot_ref[rows, :].astype(jnp.float32) + pulled
        dmid_ref[rows, :] = grad
        pulled, term_one = pull_norm(branch_ref[rows, :], gain_one, grad)
        da_ref[rows, :] = pulled.astype(BF)
        return carry[0] + fold_rows(term_one), carry[1] + fold_rows(term_two)

    zero = jnp.zeros((8, 640), jnp.float32)
    gain_ref[0], gain_ref[1] = chunks(512, 32, pull, (zero, zero))


def attention_backward(
    coords_ref, da_ref, wo_ref, o_ref, prob_ref, qn_ref, kn_ref, vb_ref, q_ref, kv_ref, gains_ref,
    dqkv_ref, gain_ref, dwo_ref, do_ref, dqn_ref, dkn_ref, dv_ref, ds_ref, lifted_ref,
):
    for head in range(4):
        block = wo_ref[8 * head : 8 * head + 8].reshape(256, 640)
        do_ref[head] = dot_right_t(da_ref[...], block).astype(BF)
        grad = dot_left_t(o_ref[head], da_ref[...])
        dwo_ref[8 * head : 8 * head + 8] = grad.astype(BF).reshape(8, 32, 640)
    dkn_ref[...] = jnp.zeros_like(dkn_ref)
    dv_ref[...] = jnp.zeros_like(dv_ref)
    for block, (low, high) in enumerate(KEY_SPANS):
        rows, span = slice(128 * block, 128 * block + 128), high - low
        lifted_ref[:, 0:span] = dot_right_t(do_ref[:, rows, :].reshape(512, 256), vb_ref[low:high, :])

        def soften(part, carry, block=block, span=span):
            head, near = part.start // 128, 128 * block + part.start % 128
            near = slice(near, near + 32)
            delta = jnp.sum(
                do_ref[head, near, :].astype(jnp.float32) * o_ref[head, near, :].astype(jnp.float32),
                axis=-1,
                keepdims=True,
            )
            soft = prob_ref[block, part, 0:span].astype(jnp.float32)
            ds_ref[part, 0:span] = (soft * (lifted_ref[part, 0:span] - delta) * SCALE).astype(BF)
            return carry

        chunks(512, 32, soften, 0)
        all_ds = ds_ref[:, 0:span]
        all_rows = qn_ref[:, rows, :].reshape(512, 256)
        dqn_ref[:, rows, :] = dot(all_ds, kn_ref[low:high, :]).reshape(4, 128, 256)
        dkn_ref[low:high, :] += dot_left_t(all_ds, all_rows)
        dv_ref[low:high, :] += dot_left_t(
            prob_ref[block, :, 0:span], do_ref[:, rows, :].reshape(512, 256)
        )
    query_gain, key_gain = 1.0 + gains_ref[4:5, 0:256], 1.0 + gains_ref[5:6, 0:256]

    def pull(rows, carry):
        query_sum, key_sum = carry
        for head in range(4):
            pulled, term = pull_norm(q_ref[head, rows, :], query_gain, dqn_ref[head, rows, :])
            dqkv_ref[head // 2, rows, 256 * (head % 2) : 256 * (head % 2) + 256] = pulled.astype(BF)
            query_sum = query_sum + fold_rows(term)
        pulled, term = pull_norm(kv_ref[0, rows, :], key_gain, dkn_ref[rows, :])
        dqkv_ref[0, rows, 512:768] = pulled.astype(BF)
        dqkv_ref[1, rows, 512:768] = dv_ref[rows, :].astype(BF)
        return query_sum, key_sum + fold_rows(term)

    zero = jnp.zeros((8, 256), jnp.float32)
    gain_ref[0], gain_ref[1] = chunks(512, 32, pull, (zero, zero))


def input_backward(
    coords_ref, dqkv_ref, h1_ref, dwo_ref, tokens_ref, dmid_ref, perm_ref, gains_ref, gain_mid_ref,
    gain_head_ref, gain_down_ref, own_ref, far_ref, input_ref, *refs
):
    out_refs, (rel_ref, plain_ref, h1t_ref) = refs[:2], refs[2:]
    core = coords_ref[3]
    total = dot_right_t(dqkv_ref[core], own_ref[...]) + dot_right_t(dqkv_ref[1 - core], far_ref[...])
    rel_ref[...] = total.astype(BF)
    h1t_ref[...] = h1_ref[...].T
    plain_ref[...] = dot_right_t(rel_ref[...], perm_ref[...])
    gain_zero = 1.0 + gains_ref[0:1, :]

    def pull(rows, carry):
        pulled, term = pull_norm(tokens_ref[rows, :].astype(jnp.float32), gain_zero, plain_ref[rows, :])
        input_ref[rows, :] = dmid_ref[rows, :] + pulled
        return carry + fold_rows(term)

    sums = [chunks(512, 32, pull, jnp.zeros((8, 640), jnp.float32))]
    sums += [gain_mid_ref[0], gain_mid_ref[1], gain_down_ref[...]]
    lines = [jnp.sum(part, axis=0, keepdims=True) for part in sums]
    for part in range(2):
        line = jnp.sum(gain_head_ref[part], axis=0, keepdims=True)
        lines.append(jnp.concatenate([line, jnp.zeros((1, 384), jnp.float32)], axis=1))
    lines.append(jnp.zeros((2, 640), jnp.float32))
    gain_block = jnp.concatenate(lines, axis=0).astype(BF)
    for far, group, one, two, place in slots(coords_ref):
        out_refs[far][group, one, two, 0:32, 768:1408] = dwo_ref[place]
        out_refs[far][group, one, two, 32:40, 768:1408] = gain_block
    for far in range(2):
        side = lax.rem(core + far, 2)
        for part in range(3):
            low = 256 * part
            grad = dot(h1t_ref[...], dqkv_ref[side, :, low : low + 256]).astype(BF)
            for spot in range(16):
                group, one, two = spot // 4, (spot // 2) % 2, spot % 2
                out_refs[far][group, one, two, :, low : low + 256] = grad[
                    40 * spot : 40 * spot + 40
                ]


def call(kernel, coords, inputs, outs, scratch=(), megabytes=32, cost=(1, 1), anys=0):
    whole = pl.BlockSpec(memory_space=pltpu.VMEM)
    return pl.pallas_call(
        kernel,
        out_shape=outs,
        in_specs=[pl.BlockSpec(memory_space=pltpu.SMEM)] + [whole] * len(inputs),
        out_specs=jax.tree.map(lambda _: whole, outs),
        scratch_shapes=list(scratch),
        cost_estimate=pl.CostEstimate(
            flops=int(cost[0] * COST * 1e9), bytes_accessed=int(cost[1] * BYTES), transcendentals=0
        ),
        compiler_params=pltpu.CompilerParams(vmem_limit_bytes=megabytes * 1024 * 1024),
    )(coords, *inputs)


def rel_table():
    table = np.zeros((32, 1, 640), np.int32)
    for place in range(32):
        z, y, x, _ = np.unravel_index(place, DIMS)
        for group in range(4):
            for one in range(2):
                for two in range(2):
                    gap = gap_of(group, one, two)
                    chip = (((z + gap[0]) % 4) * 2 + (y + gap[1]) % 2) * 2 + (x + gap[2]) % 2
                    low = 160 * group + 80 * one + 40 * two
                    table[place, 0, low : low + 40] = 40 * chip + np.arange(40)
    return table


def shape(*sizes, kind=BF):
    return jax.ShapeDtypeStruct(sizes, kind)


def join(*values):
    return lax.optimization_barrier(values)


def narrow(left, right):
    return (wide(left) + wide(right)).astype(BF)


def scatter_across(keep, got):
    return shift(narrow(keep[1], got[1]), 1, 1), shift(narrow(keep[3], got[3]), 2, 1)


def scatter_sums(keep, got, far_a, far_b):
    sum_a = wide(keep[0]) + wide(got[0]) + wide(far_a)
    sum_b = wide(keep[2]) + wide(got[2]) + wide(far_b)
    return sum_a[0], sum_b[0], sum_a[1].astype(BF), sum_b[1].astype(BF)


def scatter_pair(keep, got, far_a, far_b):
    first, second, side_a, side_b = scatter_sums(keep, got, far_a, far_b)
    return first, second, shift(side_a, 2, 1), shift(side_b, 1, 1)


def scatter_along(sum_a, sum_b, side_a, side_b):
    last_a = sum_a + wide(side_a)
    last_b = sum_b + wide(side_b)
    return last_a[0], [last_a[1].astype(BF), last_b[0].astype(BF), last_b[1].astype(BF)]


def scatter_end(own, *others):
    for other in others:
        own = own + wide(other)
    return own


def block_fast(tokens, segment_ids, cotangent, weights, update_gateup):
    query_round, keyval_round, output_round, gateup_round, down_round, gains, heads = weights
    f32 = jnp.float32
    along, upward, sideways, core = own_coords()
    place = lax.axis_index("dp")
    coords = jnp.stack([along, upward, sideways, core]).astype(jnp.int32)
    index = lax.dynamic_index_in_dim(jnp.asarray(rel_table()), place, keepdims=False)
    tokens, cotangent = tokens.reshape(512, 640), cotangent.reshape(512, 640)
    segcol = segment_ids.reshape(512, 1)

    low = jnp.concatenate([query_round[:, :512], keyval_round[:, :256], gateup_round[:, 0]], axis=1)
    high = jnp.concatenate([query_round[:, 512:], keyval_round[:, 256:], gateup_round[:, 1]], axis=1)
    away, keep = swap_halves(core, low, high)
    got = shift(away, 3, 1)
    both = jnp.concatenate([jnp.where(core == 0, keep, got), jnp.where(core == 0, got, keep)], axis=0)
    spread = jnp.zeros((8, 640), BF)
    spread = lax.dynamic_update_slice(spread, gains, (0, place * gains.shape[1]))
    spread = lax.dynamic_update_slice(spread, heads, (4, place * heads.shape[1]))
    block_a = jnp.concatenate([both[:, :768], jnp.concatenate([output_round, spread], axis=0)], axis=1)
    block_g = both[:, 768:]

    near_a = gather_along(block_a)
    near_a, block_w, block_g = join(near_a, down_round, block_g)
    first, second = jnp.stack([near_a[0], near_a[1]]), jnp.stack([near_a[2], near_a[3]])
    first, second, block_w, block_g = join(first, second, block_w, block_g)
    pairs_a = [jnp.stack([first, shift(first, 2, 1)]), jnp.stack([second, shift(second, 1, 1)])]
    near_w = gather_along(block_w)
    pairs_a, near_w, block_g = join(pairs_a, near_w, block_g)
    mine_a = gather_across(*pairs_a)
    near_g = gather_along(block_g)
    pairs_w = gather_pair(near_w)
    mine_a, near_g = join(mine_a, near_g)
    pieces_a = gather_core(mine_a)
    pairs_g = gather_pair(near_g)
    pairs_g, pairs_w = join(pairs_g, pairs_w)
    mine_g = gather_across(*pairs_g)
    early_g = [shift(pair, 3, 1) for pair in pairs_g]
    h1, q, kv, qn, kn, vb, wo, gains_full, perm, own_qkv, far_qkv = call(
        project_forward,
        coords,
        [index, tokens, *pieces_a],
        [
            shape(512, 640), shape(4, 512, 256, kind=f32), shape(2, 512, 256, kind=f32),
            shape(4, 512, 256), shape(512, 256), shape(512, 256),
            shape(32, 32, 640), shape(8, 640, kind=f32), shape(640, 640), shape(640, 768), shape(640, 768),
        ],
        [pltpu.VMEM((512, 640), BF)],
        12,
        (5, 20),
    )
    qn, pairs_w = join(qn, pairs_w)
    mine_w = gather_across(*pairs_w)
    early_w = [shift(pair, 3, 1) for pair in pairs_w]
    prob, o, branch, mid, h3 = call(
        attention_forward,
        coords,
        [tokens, segment_ids, segcol, qn, kn, vb, wo, gains_full, perm],
        [
            shape(4, 512, 384), shape(4, 512, 256), shape(512, 640, kind=f32),
            shape(512, 640, kind=f32), shape(512, 640),
        ],
        [pltpu.VMEM((512, 640), BF), pltpu.VMEM((128, 384), f32), pltpu.VMEM((512, 384), f32)],
        12,
        (5, 20),
    )
    mine_g, h3, early_g = join(mine_g, h3, early_g)
    far_g = [early_g[0], shift(mine_g[1], 3, 1), early_g[1], shift(mine_g[3], 3, 1)]
    own, own_gu = call(
        gateup_own,
        coords,
        [h3, *mine_g],
        [shape(512, 2048, kind=f32), shape(640, 2048)],
        [],
        12,
        (6, 20),
    )
    far_g, own = join(far_g, own)
    slope, gelu, hidden, far_gu = call(
        gateup_forward,
        coords,
        [h3, own, *far_g],
        [shape(512, 2048)] * 3 + [shape(640, 2048)],
        [pltpu.VMEM((2, 512, 512), f32)],
        12,
        (3, 10),
    )
    hidden, mine_w = join(hidden, mine_w)
    pieces_w = mine_w + [early_w[0], shift(mine_w[1], 3, 1), early_w[1], shift(mine_w[3], 3, 1)]
    result, dm, gain_down, wd, keep_w, send_w = call(
        down_both,
        coords,
        [hidden, mid, cotangent, gains_full, *pieces_w],
        [shape(512, 640), shape(512, 640), shape(8, 640, kind=f32), shape(32, 64, 640)]
        + [shape(4, 2, 2, 64, 640)] * 2,
        [pltpu.VMEM((512, 640), f32), pltpu.VMEM((32, 64, 640), BF)],
        12,
        (6, 20),
    )
    got_w = shift(send_w, 3, 1)
    dgu, keep_g, send_g = call(
        gateup_backward,
        coords,
        [dm, wd, slope, gelu, h3],
        [shape(2, 512, 2048)] + [shape(4, 2, 2, 40, 2048)] * 2,
        [pltpu.VMEM((2, 512, 512), f32), pltpu.VMEM((640, 512), BF)],
        12,
        (8, 20),
    )
    dgu, got_w, send_g = join(dgu, got_w, send_g)
    far_w = scatter_across(keep_w, got_w)
    got_g = shift(send_g, 3, 1)
    dmid, da, gain_mid = call(
        middle_backward,
        coords,
        [dgu, mid, branch, cotangent, gains_full, perm, own_gu, far_gu],
        [shape(512, 640, kind=f32), shape(512, 640), shape(2, 8, 640, kind=f32)],
        [pltpu.VMEM((512, 640), BF), pltpu.VMEM((512, 640), f32)],
        12,
        (8, 20),
    )
    da, got_g, far_w = join(da, got_g, far_w)
    side_w = scatter_pair(keep_w, got_w, *far_w)
    far_g = scatter_across(keep_g, got_g)
    dqkv, gain_head, dwo = call(
        attention_backward,
        coords,
        [da, wo, o, prob, qn, kn, vb, q, kv, gains_full],
        [shape(2, 512, 768), shape(2, 8, 256, kind=f32), shape(32, 32, 640)],
        [
            pltpu.VMEM((4, 512, 256), BF),
            pltpu.VMEM((4, 512, 256), f32), pltpu.VMEM((512, 256), f32), pltpu.VMEM((512, 256), f32),
            pltpu.VMEM((512, 384), BF), pltpu.VMEM((512, 384), f32),
        ],
        12,
        (6, 20),
    )
    dqkv, side_w = join(dqkv, side_w)
    own_w, along_w = scatter_along(*side_w)
    along_w = [shift(part, 0, step + 1) for step, part in enumerate(along_w)]
    input_grad, keep_a, send_a = call(
        input_backward,
        coords,
        [dqkv, h1, dwo, tokens, dmid, perm, gains_full, gain_mid, gain_head, gain_down, own_qkv, far_qkv],
        [shape(512, 640, kind=f32)] + [shape(4, 2, 2, 40, 1408)] * 2,
        [pltpu.VMEM((512, 640), BF), pltpu.VMEM((512, 640), f32), pltpu.VMEM((640, 512), BF)],
        12,
        (6, 20),
    )
    send_a, far_g, along_w = join(send_a, far_g, along_w)
    down_grad = scatter_end(own_w, *along_w)
    got_a = shift(send_a, 3, 1)
    side_g = scatter_pair(keep_g, got_g, *far_g)
    got_a, side_g = join(got_a, side_g)
    first, second = narrow(keep_a[1], got_a[1]), narrow(keep_a[3], got_a[3])
    first, second, side_g = join(first, second, side_g)
    far_a = shift(first, 1, 1), shift(second, 2, 1)
    own_g, along_g = scatter_along(*side_g)
    ends_g = [shift(along_g[0], 0, 1), shift(along_g[2], 0, 3)]
    far_a, ends_g, across_g = join(far_a, ends_g, along_g[1])
    first, second, *side_a = scatter_sums(keep_a, got_a, *far_a)
    side_a, across_g = join(side_a, across_g)
    side_a = shift(side_a[0], 2, 1), shift(side_a[1], 1, 1)
    across_g = shift(across_g, 0, 2)
    side_a, across_g = join(side_a, across_g)
    own_a, along_a = scatter_along(first, second, *side_a)
    along_a = [shift(part, 0, step + 1) for step, part in enumerate(along_a)]
    gateup_sum = scatter_end(own_g, across_g, *ends_g)

    def own_rows(both):
        away, keep = swap_halves(core, both[:20], both[20:])
        got = shift(away, 3, 1)
        return jnp.where(core == 0, keep, got), jnp.where(core == 0, got, keep)

    low, high = own_rows(gateup_sum)
    gateup_grad = with_layout_constraint(jnp.stack([low, high], axis=1), Layout((0, 1, 2)))
    gateup_done = (gateup_grad, *update_gateup(gateup_grad))
    along_a, gateup_done = join(along_a, gateup_done)
    rest = scatter_end(own_a, *along_a)
    output_grad = rest[:32, 768:]
    norm_grad = lax.dynamic_slice(rest[32:36, 768:], (0, place * 20), (4, 20))
    qknorm_grad = lax.dynamic_slice(rest[36:38, 768:], (0, place * 8), (2, 8))

    low, high = own_rows(rest[:, :768])
    query_grad = jnp.concatenate([low[:, :512], high[:, :512]], axis=1)
    keyval_grad = jnp.concatenate([low[:, 512:], high[:, 512:]], axis=1)
    grads = (query_grad, keyval_grad, output_grad, gateup_done[0], down_grad, norm_grad, qknorm_grad)
    return result[None], input_grad[None], grads, gateup_done[1:]


def norm_apply(values, gain_vector):
    inverse = lax.rsqrt(jnp.mean(values * values, axis=-1, keepdims=True) + norm_epsilon)
    return values * inverse * (1.0 + gain_vector)


def gelu_product(gate_part, up_part):
    return jax.nn.gelu(gate_part, approximate=True) * up_part


def block_scores(query_normed, key_normed, segments, row_start, row_stop, score_scale):
    positions = jnp.arange(row_stop)
    same_doc = segments[row_start:row_stop, None] == segments[None, :row_stop]
    causal = positions[None, :] <= positions[row_start:row_stop, None]
    allowed = (same_doc & causal)[None]
    scores = (
        jnp.einsum("qhd,kd->hqk", query_normed, key_normed, preferred_element_type=jnp.float32)
        * score_scale
    )
    return (jnp.where(allowed, scores, -1e30), allowed)


def attend_forward(query_normed, key_normed, value_round, segments, score_scale):
    length = query_normed.shape[0]
    block_rows = min(512, length)
    masked, allowed = block_scores(query_normed, key_normed, segments, 0, block_rows, score_scale)
    row_max = jnp.max(masked, axis=-1, keepdims=True)
    row_total = jnp.sum(jnp.where(allowed, jnp.exp(masked - row_max), 0.0), axis=-1, keepdims=True)
    log_total = row_max + jnp.log(row_total)
    soft_round = jnp.where(allowed, jnp.exp(masked - log_total), 0.0).astype(jnp.bfloat16)
    attended_block = jnp.einsum(
        "hqk,kd->qhd", soft_round, value_round, preferred_element_type=jnp.float32
    )
    attended_parts = attended_block.astype(jnp.bfloat16)
    total_parts = log_total[:, :, 0]
    return (attended_parts, total_parts)


def attend_backward(
    query_normed,
    key_normed,
    value_round,
    segments,
    log_totals,
    attended,
    grad_attended,
    score_scale,
):
    length = query_normed.shape[0]
    head_dim = key_normed.shape[1]
    block_rows = min(512, length)
    row_delta = jnp.sum(grad_attended.astype(jnp.float32) * attended.astype(jnp.float32), axis=-1)
    grad_key_sum = jnp.zeros((length, head_dim), jnp.float32)
    grad_value_sum = jnp.zeros((length, head_dim), jnp.float32)
    masked, allowed = block_scores(query_normed, key_normed, segments, 0, block_rows, score_scale)
    soft_weights = jnp.where(allowed, jnp.exp(masked - log_totals[:, 0:block_rows, None]), 0.0)
    soft_round = soft_weights.astype(jnp.bfloat16)
    grad_value_sum = grad_value_sum.at[:block_rows].add(
        jnp.einsum("hqk,qhd->kd", soft_round, grad_attended, preferred_element_type=jnp.float32)
    )
    grad_soft = jnp.einsum(
        "qhd,kd->hqk", grad_attended, value_round, preferred_element_type=jnp.float32
    )
    delta_block = row_delta.T[:, :, None]
    grad_scores = (soft_weights * (grad_soft - delta_block) * score_scale).astype(jnp.bfloat16)
    grad_query_parts = jnp.einsum(
        "hqk,kd->qhd", grad_scores, key_normed, preferred_element_type=jnp.float32
    )
    grad_key_sum = grad_key_sum.at[:block_rows].add(
        jnp.einsum("hqk,qhd->kd", grad_scores, query_normed, preferred_element_type=jnp.float32)
    )
    return (grad_query_parts, grad_key_sum, grad_value_sum)


def adam_update(parameter, gradient, first_moment, second_moment, decay_value):
    first_new = beta_one * first_moment + (1.0 - beta_one) * gradient
    second_new = beta_two * second_moment + (1.0 - beta_two) * gradient * gradient
    first_hat = first_new / (1.0 - beta_one**STEP)
    second_hat = second_new / (1.0 - beta_two**STEP)
    parameter_new = (
        parameter
        - learn_rate * first_hat / (jnp.sqrt(second_hat) + adam_epsilon)
        - learn_rate * decay_value * parameter
    )
    return (parameter_new, first_new, second_new)


def block_plain(tokens, segment_ids, cotangent, weights, update_gateup):
    query_full, keyval_full, output_full, gateup_full, down_full, main_gains, head_gains = gather_plain(*weights)
    seq_count, length, model_width = tokens.shape
    row_count = seq_count * length
    head_dim = head_gains.shape[1]
    head_count = query_full.shape[1] // head_dim
    hidden_units = gateup_full.shape[1] // 2
    score_scale = head_dim ** (-0.5)
    inputs = tokens.reshape(row_count, model_width).astype(jnp.float32)
    normed_in = norm_apply(inputs, main_gains[0]).astype(jnp.bfloat16)
    queries = jnp.dot(normed_in, query_full, preferred_element_type=jnp.float32).reshape(
        row_count, head_count, head_dim
    )
    keyvals = jnp.dot(normed_in, keyval_full, preferred_element_type=jnp.float32)
    key_rows = keyvals[:, :head_dim]
    value_rows = keyvals[:, head_dim:]
    query_normed = norm_apply(queries, head_gains[0]).astype(jnp.bfloat16)
    key_normed = norm_apply(key_rows, head_gains[1]).astype(jnp.bfloat16)
    value_round = value_rows.astype(jnp.bfloat16)
    seq_index = 0
    attended_seq, totals_seq = attend_forward(
        query_normed, key_normed, value_round, segment_ids[seq_index], score_scale
    )
    total_parts = [totals_seq]
    attended_flat = attended_seq.reshape(row_count, head_count * head_dim)
    branch = jnp.dot(attended_flat, output_full, preferred_element_type=jnp.float32)
    middle = inputs + norm_apply(branch, main_gains[1])
    normed_mid = norm_apply(middle, main_gains[2]).astype(jnp.bfloat16)
    gate_up = jnp.dot(
        normed_mid,
        gateup_full,
        preferred_element_type=jnp.float32,
    )
    gate_part = gate_up[:, :hidden_units]
    up_part = gate_up[:, hidden_units:]
    hidden = gelu_product(gate_part, up_part).astype(jnp.bfloat16)
    down_out = jnp.dot(hidden, down_full, preferred_element_type=jnp.float32)
    result = (middle + norm_apply(down_out, main_gains[3])).astype(jnp.bfloat16)
    query_back, keyval_back, output_back, gateup_back, down_back = (
        query_full,
        keyval_full,
        output_full,
        gateup_full,
        down_full,
    )
    gateup_flat = gateup_back
    grad_out = cotangent.reshape(row_count, model_width).astype(jnp.float32)
    _, pull_back = jax.vjp(norm_apply, down_out, main_gains[3])
    grad_down_out, grad_gain_three = pull_back(grad_out)
    grad_down_round = grad_down_out.astype(jnp.bfloat16)
    grad_down = jnp.dot(hidden.T, grad_down_round, preferred_element_type=jnp.float32)
    grad_hidden = jnp.dot(grad_down_round, down_back.T, preferred_element_type=jnp.float32)
    _, pull_back = jax.vjp(gelu_product, gate_part, up_part)
    grad_gate, grad_up = pull_back(grad_hidden)
    grad_gate_up = jnp.concatenate([grad_gate, grad_up], axis=1).astype(jnp.bfloat16)
    grad_gateup = jnp.dot(normed_mid.T, grad_gate_up, preferred_element_type=jnp.float32)
    grad_normed_mid = jnp.dot(grad_gate_up, gateup_flat.T, preferred_element_type=jnp.float32)
    _, pull_back = jax.vjp(norm_apply, middle, main_gains[2])
    grad_mid_norm, grad_gain_two = pull_back(grad_normed_mid)
    grad_middle = grad_out + grad_mid_norm
    _, pull_back = jax.vjp(norm_apply, branch, main_gains[1])
    grad_branch, grad_gain_one = pull_back(grad_middle)
    grad_branch_round = grad_branch.astype(jnp.bfloat16)
    grad_output = jnp.dot(attended_flat.T, grad_branch_round, preferred_element_type=jnp.float32)
    grad_attended = (
        jnp.dot(grad_branch_round, output_back.T, preferred_element_type=jnp.float32)
        .reshape(row_count, head_count, head_dim)
        .astype(jnp.bfloat16)
    )
    seq_index = 0
    grad_query_seq, grad_key_seq, grad_value_seq = attend_backward(
        query_normed,
        key_normed,
        value_round,
        segment_ids[seq_index],
        total_parts[seq_index],
        attended_seq,
        grad_attended,
        score_scale,
    )
    _, pull_back = jax.vjp(norm_apply, queries, head_gains[0])
    grad_queries, grad_head_zero = pull_back(grad_query_seq)
    _, pull_back = jax.vjp(norm_apply, key_rows, head_gains[1])
    grad_keys, grad_head_one = pull_back(grad_key_seq)
    grad_query_round = grad_queries.reshape(row_count, head_count * head_dim).astype(jnp.bfloat16)
    grad_keyval_round = jnp.concatenate([grad_keys, grad_value_seq], axis=1).astype(jnp.bfloat16)
    grad_query = jnp.dot(normed_in.T, grad_query_round, preferred_element_type=jnp.float32)
    grad_keyval = jnp.dot(normed_in.T, grad_keyval_round, preferred_element_type=jnp.float32)
    grad_normed_in = jnp.dot(
        grad_query_round, query_back.T, preferred_element_type=jnp.float32
    ) + jnp.dot(grad_keyval_round, keyval_back.T, preferred_element_type=jnp.float32)
    _, pull_back = jax.vjp(norm_apply, inputs, main_gains[0])
    grad_in_norm, grad_gain_zero = pull_back(grad_normed_in)
    input_grad = grad_middle + grad_in_norm
    grad_gains = jnp.stack([grad_gain_zero, grad_gain_one, grad_gain_two, grad_gain_three])
    grad_heads = jnp.stack([grad_head_zero, grad_head_one])
    gradients = scatter_plain(
        grad_query, grad_keyval, grad_output, grad_gateup, grad_down, grad_gains, grad_heads
    )
    result_out = result.reshape(seq_count, length, model_width)
    input_out = input_grad.reshape(seq_count, length, model_width)
    return result_out, input_out, gradients, update_gateup(gradients[3])


def per_device(
    tokens,
    segment_ids,
    cotangent,
    query_weight,
    keyval_weight,
    output_weight,
    gateup_weight,
    down_weight,
    norm_gains,
    qknorm_gains,
    query_mean,
    keyval_mean,
    output_mean,
    gateup_mean,
    down_mean,
    norm_mean,
    qknorm_mean,
    query_square,
    keyval_square,
    output_square,
    gateup_square,
    down_square,
    norm_square,
    qknorm_square,
):
    query_round = query_weight.astype(jnp.bfloat16)
    keyval_round = keyval_weight.astype(jnp.bfloat16)
    output_round = output_weight.astype(jnp.bfloat16)
    gateup_round = gateup_weight.astype(jnp.bfloat16)
    down_round = down_weight.astype(jnp.bfloat16)
    gains_round = norm_gains.astype(jnp.bfloat16)
    headgain_round = qknorm_gains.astype(jnp.bfloat16)
    weights = (
        query_round, keyval_round, output_round, gateup_round, down_round, gains_round, headgain_round
    )

    def update_gateup(gradient):
        return adam_update(gateup_weight, gradient, gateup_mean, gateup_square, decay_coef)

    block = block_fast if lax.axis_size("dp") == 32 else block_plain
    result_out, input_out, gradients, gateup_done = block(
        tokens, segment_ids, cotangent, weights, update_gateup
    )
    parameters = (
        query_weight,
        keyval_weight,
        output_weight,
        gateup_weight,
        down_weight,
        norm_gains,
        qknorm_gains,
    )
    firsts = (query_mean, keyval_mean, output_mean, gateup_mean, down_mean, norm_mean, qknorm_mean)
    seconds = (
        query_square,
        keyval_square,
        output_square,
        gateup_square,
        down_square,
        norm_square,
        qknorm_square,
    )
    decays = (decay_coef, decay_coef, decay_coef, decay_coef, decay_coef, 0.0, 0.0)
    updates = [
        adam_update(
            parameters[place], gradients[place], firsts[place], seconds[place], decays[place]
        )
        if place != 3
        else gateup_done
        for place in range(7)
    ]
    news = tuple((update[0] for update in updates))
    first_news = tuple((update[1] for update in updates))
    second_news = tuple((update[2] for update in updates))
    return (result_out, input_out) + gradients + news + first_news + second_news


def solution(mesh):
    in_specs = (
        P("dp", None, None),
        P("dp", None),
        P("dp", None, None),
        P("dp", None),
        P("dp", None),
        P("dp", None),
        P("dp", None, None),
        P("dp", None),
        P(None, "dp"),
        P(None, "dp"),
        P("dp", None),
        P("dp", None),
        P("dp", None),
        P("dp", None, None),
        P("dp", None),
        P(None, "dp"),
        P(None, "dp"),
        P("dp", None),
        P("dp", None),
        P("dp", None),
        P("dp", None, None),
        P("dp", None),
        P(None, "dp"),
        P(None, "dp"),
    )
    out_specs = (
        P("dp", None, None),
        P("dp", None, None),
        P("dp", None),
        P("dp", None),
        P("dp", None),
        P("dp", None, None),
        P("dp", None),
        P(None, "dp"),
        P(None, "dp"),
        P("dp", None),
        P("dp", None),
        P("dp", None),
        P("dp", None, None),
        P("dp", None),
        P(None, "dp"),
        P(None, "dp"),
        P("dp", None),
        P("dp", None),
        P("dp", None),
        P("dp", None, None),
        P("dp", None),
        P(None, "dp"),
        P(None, "dp"),
        P("dp", None),
        P("dp", None),
        P("dp", None),
        P("dp", None, None),
        P("dp", None),
        P(None, "dp"),
        P(None, "dp"),
    )
    return jax.shard_map(
        per_device, mesh=mesh, in_specs=in_specs, out_specs=out_specs, check_vma=False
    )
```

```python
import jax
import jax.numpy as jnp
import numpy as np
from jax import lax
from jax.experimental import pallas as pl
from jax.experimental.layout import Layout, with_layout_constraint
from jax.experimental.pallas import tpu as pltpu
from jax.sharding import PartitionSpec as P

STEP = 3
norm_epsilon = 1e-06
beta_one = 0.9
beta_two = 0.999
learn_rate = 0.03
decay_coef = 0.1
adam_epsilon = 1e-08

DIMS = (4, 2, 2, 2)
BF = jnp.bfloat16


def shift_perm(axis, amount):
    pairs = []
    for place in range(int(np.prod(DIMS))):
        spot = list(np.unravel_index(place, DIMS))
        spot[axis] = (spot[axis] + amount) % DIMS[axis]
        pairs.append((place, int(np.ravel_multi_index(spot, DIMS))))
    return pairs


def shift(values, axis, amount):
    with jax.named_scope("zyxc"[axis] + str(amount % DIMS[axis])):
        return lax.ppermute(values, "dp", shift_perm(axis, amount))


def own_coords():
    place = lax.axis_index("dp")
    return place // 8, (place // 4) % 2, (place // 2) % 2, place % 2


def after(values, *others):
    return lax.optimization_barrier((values, others))[0]


def gather_along(block):
    return [block] + [shift(block, 0, -step) for step in (1, 2, 3)]


def gather_pair(near):
    first = jnp.stack([near[0], near[2]])
    second = jnp.stack([near[1], near[3]])
    return jnp.stack([first, shift(first, 2, 1)]), jnp.stack([second, shift(second, 1, 1)])


def gather_across(pair_a, pair_b):
    return [pair_a, shift(pair_a, 1, 1), pair_b, shift(pair_b, 2, 1)]


def gather_core(mine):
    return mine + [shift(piece, 3, 1) for piece in mine]


def wide(values):
    return values.astype(jnp.float32)


def swap_halves(core, low, high):
    return jnp.where(core == 0, high, low), jnp.where(core == 0, low, high)


def gather_plain(query_round, keyval_round, output_round, gateup_round, down_round, gains_round, headgain_round):
    gateup_full = lax.all_gather(gateup_round, "dp", axis=0, tiled=True)
    return (
        lax.all_gather(query_round, "dp", axis=0, tiled=True),
        lax.all_gather(keyval_round, "dp", axis=0, tiled=True),
        lax.all_gather(output_round, "dp", axis=0, tiled=True),
        gateup_full.reshape(gateup_full.shape[0], -1),
        lax.all_gather(down_round, "dp", axis=0, tiled=True),
        lax.all_gather(gains_round, "dp", axis=1, tiled=True).astype(jnp.float32),
        lax.all_gather(headgain_round, "dp", axis=1, tiled=True).astype(jnp.float32),
    )


def scatter_plain(grad_query, grad_keyval, grad_output, grad_gateup, grad_down, grad_gains, grad_heads):
    rows = grad_gateup.shape[0]
    return (
        lax.psum_scatter(grad_query, "dp", scatter_dimension=0, tiled=True),
        lax.psum_scatter(grad_keyval, "dp", scatter_dimension=0, tiled=True),
        lax.psum_scatter(grad_output, "dp", scatter_dimension=0, tiled=True),
        lax.psum_scatter(grad_gateup.reshape(rows, 2, -1), "dp", scatter_dimension=0, tiled=True),
        lax.psum_scatter(grad_down, "dp", scatter_dimension=0, tiled=True),
        lax.psum_scatter(grad_gains, "dp", scatter_dimension=1, tiled=True),
        lax.psum_scatter(grad_heads, "dp", scatter_dimension=1, tiled=True),
    )


BYTES = 1e6
COST = 1.0
HALF = 1024 // 2
SCALE = 256 ** (-0.5)
KEY_SPANS = ((0, 128), (0, 256), (0, 384), (128, 512))
TANH_SLOPE = (2.0 / np.pi) ** 0.5
TANH_CUBE = 0.044715


def dot(left, right):
    return jnp.dot(left, right, preferred_element_type=jnp.float32)


def dot_right_t(left, right):
    return lax.dot_general(left, right, (((1,), (1,)), ((), ())), preferred_element_type=jnp.float32)


def dot_left_t(left, right):
    return lax.dot_general(left, right, (((0,), (0,)), ((), ())), preferred_element_type=jnp.float32)


def inverse_rms(values):
    return lax.rsqrt(jnp.mean(values * values, axis=-1, keepdims=True) + norm_epsilon)


def pull_norm(values, gain_plus, grad):
    inverse = inverse_rms(values)
    unit = values * inverse
    scaled = grad * gain_plus
    return inverse * (scaled - unit * jnp.mean(scaled * unit, axis=-1, keepdims=True)), grad * unit


def fold_rows(values):
    rows, columns = values.shape
    return jnp.sum(values.reshape(rows // 8, 8, columns), axis=0)


def chunks(count, size, body, carry):
    for low in range(0, count, size):
        carry = body(slice(low, low + size), carry)
    return carry


def group_rows(piece_ref, low, high):
    return piece_ref[:, :, :, low:high].reshape(160, high - low)


def chip_at(coords_ref, gap):
    along = lax.rem(coords_ref[0] + gap[0], 4)
    upward = lax.rem(coords_ref[1] + gap[1], 2)
    sideways = lax.rem(coords_ref[2] + gap[2], 2)
    return (along * 2 + upward) * 2 + sideways


def gap_of(group, one, two):
    return (2 * two, group, one) if group < 2 else (1 + 2 * two, one, group - 2)


def slots(coords_ref):
    for far in range(2):
        core = lax.rem(coords_ref[3] + far, 2)
        for group in range(4):
            for one in range(2):
                for two in range(2):
                    yield far, group, one, two, 2 * chip_at(coords_ref, gap_of(group, one, two)) + core


def place_rows(out_ref, piece_refs, low, high):
    for group in range(4):
        for one in range(2):
            for two in range(2):
                row = 160 * group + 80 * one + 40 * two
                out_ref[row : row + 40, :] = piece_refs[group][one, two, :, low:high]


def project_forward(coords_ref, index_ref, tokens_ref, *refs):
    piece_refs, refs = refs[:8], refs[8:]
    (
        h1_ref, q_ref, kv_ref, qn_ref, kn_ref, vb_ref, wo_ref, gains_ref, perm_ref, own_ref, far_ref, plain_ref
    ) = refs
    for far, group, one, two, place in slots(coords_ref):
        wo_ref[place] = piece_refs[4 * far + group][one, two, 0:32, 768:1408]
    gains = jnp.zeros((8, 640), jnp.float32)
    for far in range(2):
        for group in range(4):
            for one in range(2):
                for two in range(2):
                    gains = gains + piece_refs[4 * far + group][one, two, 32:40, 768:1408].astype(jnp.float32)
    gains_ref[...] = gains
    core = coords_ref[3]

    def make_perm(rows, carry):
        place = lax.broadcasted_iota(jnp.int32, (64, 640), 0) + rows.start
        perm_ref[rows, :] = jnp.where(place == index_ref[...], 1.0, 0.0).astype(BF)
        return carry

    chunks(640, 64, make_perm, 0)
    gain_zero = 1.0 + gains_ref[0:1, :]

    def norm_in(rows, carry):
        values = tokens_ref[rows, :].astype(jnp.float32)
        plain_ref[rows, :] = (values * inverse_rms(values) * gain_zero).astype(BF)
        return carry

    chunks(512, 32, norm_in, 0)
    h1_ref[...] = dot(plain_ref[...], perm_ref[...]).astype(BF)
    for far, weight_ref in enumerate((own_ref, far_ref)):
        place_rows(weight_ref, piece_refs[4 * far : 4 * far + 4], 0, 768)
        side = lax.rem(core + far, 2)
        for part in range(3):
            total = dot(h1_ref[...], weight_ref[:, 256 * part : 256 * part + 256])
            if part < 2:
                q_ref[2 * side + part] = total
            else:
                kv_ref[side] = total
    query_gain, key_gain = 1.0 + gains_ref[4:5, 0:256], 1.0 + gains_ref[5:6, 0:256]

    def norm_heads(rows, carry):
        for head in range(4):
            values = q_ref[head, rows, :]
            qn_ref[head, rows, :] = (values * inverse_rms(values) * query_gain).astype(BF)
        values = kv_ref[0, rows, :]
        kn_ref[rows, :] = (values * inverse_rms(values) * key_gain).astype(BF)
        vb_ref[rows, :] = kv_ref[1, rows, :].astype(BF)
        return carry

    chunks(512, 64, norm_heads, 0)


def attention_forward(
    coords_ref, tokens_ref, segrow_ref, segcol_ref, qn_ref, kn_ref, vb_ref, wo_ref, gains_ref, perm_ref,
    prob_ref, o_ref, branch_ref, mid_ref, h3_ref, plain_ref, bias_ref, score_ref,
):
    for block, (low, high) in enumerate(KEY_SPANS):
        rows, span = slice(128 * block, 128 * block + 128), high - low
        row_at = lax.broadcasted_iota(jnp.int32, (128, span), 0) + 128 * block
        key_at = lax.broadcasted_iota(jnp.int32, (128, span), 1) + low
        allowed = (segcol_ref[rows, :] == segrow_ref[:, low:high]) & (key_at <= row_at)
        bias_ref[:, 0:span] = jnp.where(allowed, 0.0, -1e30)
        score_ref[:, 0:span] = dot_right_t(qn_ref[:, rows, :].reshape(512, 256), kn_ref[low:high, :])

        def soften(part, carry, block=block, span=span):
            near = slice(part.start % 128, part.start % 128 + 32)
            scores = score_ref[part, 0:span] * SCALE + bias_ref[near, 0:span]
            powers = jnp.exp(scores - jnp.max(scores, axis=-1, keepdims=True))
            inverse = 1.0 / jnp.sum(powers, axis=-1, keepdims=True)
            prob_ref[block, part, 0:span] = (powers * inverse).astype(BF)
            return carry

        chunks(512, 32, soften, 0)
        mixed = dot(prob_ref[block, :, 0:span], vb_ref[low:high, :])
        o_ref[:, rows, :] = mixed.astype(BF).reshape(4, 128, 256)
    total = jnp.zeros((512, 640), jnp.float32)
    for head in range(4):
        total = total + dot(o_ref[head], wo_ref[8 * head : 8 * head + 8].reshape(256, 640))
    branch_ref[...] = total
    gain_one, gain_two = 1.0 + gains_ref[1:2, :], 1.0 + gains_ref[2:3, :]

    def norm_mid(rows, carry):
        values = branch_ref[rows, :]
        middle = tokens_ref[rows, :].astype(jnp.float32) + values * inverse_rms(values) * gain_one
        mid_ref[rows, :] = middle
        plain_ref[rows, :] = (middle * inverse_rms(middle) * gain_two).astype(BF)
        return carry

    chunks(512, 32, norm_mid, 0)
    h3_ref[...] = dot(plain_ref[...], perm_ref[...]).astype(BF)


def gateup_own(coords_ref, h3_ref, *refs):
    piece_refs, (own_ref, weight_ref) = refs[:4], refs[4:]
    place_rows(weight_ref, piece_refs, 0, 2048)
    for block in range(4):
        low = 512 * block
        own_ref[:, low : low + 512] = dot(h3_ref[...], weight_ref[:, low : low + 512])


def gateup_forward(coords_ref, h3_ref, own_ref, *refs):
    piece_refs, (slope_ref, gelu_ref, hidden_ref, weight_ref, far_ref) = refs[:4], refs[4:]
    first = jnp.full((16, 512), coords_ref[3]) == 0
    place_rows(weight_ref, piece_refs, 0, 2048)
    for block in range(4):
        low = 512 * block
        spot = block % 2
        far_ref[spot] = dot(h3_ref[...], weight_ref[:, low : low + 512])

        def activate(rows, low=low, spot=spot):
            own, far = own_ref[rows, low : low + 512], far_ref[spot, rows, :]
            gate, up = jnp.where(first, own, far), jnp.where(first, far, own)
            square = gate * gate
            bend = jnp.tanh(gate * (TANH_SLOPE + (TANH_SLOPE * TANH_CUBE) * square))
            weight = 0.5 + 0.5 * bend
            rise = gate * (2.0 * TANH_SLOPE + (6.0 * TANH_SLOPE * TANH_CUBE) * square)
            gelu = gate * weight
            slope = weight + (weight * rise) * (1.0 - weight)
            slope_ref[rows, low : low + 512] = (slope * up).astype(BF)
            gelu_ref[rows, low : low + 512] = gelu.astype(BF)
            hidden_ref[rows, low : low + 512] = (gelu * up).astype(BF)

        for start in range(0, 512, 16):
            activate(slice(start, start + 16))


def plane_slots(coords_ref):
    for far in range(2):
        core = lax.rem(coords_ref[3] + far, 2)
        for step in range(4):
            for spot in range(4):
                yield far, step, spot, 2 * chip_at(coords_ref, (step, spot // 2, spot % 2)) + core


def down_both(coords_ref, hidden_ref, mid_ref, cot_ref, gains_ref, *refs):
    piece_refs, refs = refs[:8], refs[8:]
    (result_ref, dm_ref, gain_ref, wd_ref), refs = refs[:4], refs[4:]
    out_refs, (product_ref, natural_ref) = refs[:2], refs[2:]
    for far, group, one, two, place in slots(coords_ref):
        wd_ref[place] = piece_refs[4 * far + group][one, two]
    weights = wd_ref[...].reshape(2048, 640)
    for low in (0, 256):
        product_ref[low : low + 256, :] = dot(hidden_ref[low : low + 256, :], weights)
    gain_three = 1.0 + gains_ref[3:4, :]

    def finish(rows, carry):
        values = product_ref[rows, :]
        grad = cot_ref[rows, :].astype(jnp.float32)
        result_ref[rows, :] = (mid_ref[rows, :] + values * inverse_rms(values) * gain_three).astype(BF)
        pulled, term = pull_norm(values, gain_three, grad)
        dm_ref[rows, :] = pulled.astype(BF)
        return carry + fold_rows(term)

    gain_ref[...] = chunks(512, 32, finish, jnp.zeros((8, 640), jnp.float32))
    for block in range(8):
        grad = dot_left_t(hidden_ref[:, 256 * block : 256 * block + 256], dm_ref[...])
        natural_ref[4 * block : 4 * block + 4] = grad.astype(BF).reshape(4, 64, 640)
    for far, step, spot, place in plane_slots(coords_ref):
        out_refs[far][step, spot] = natural_ref[place]


def gateup_backward(coords_ref, dm_ref, wd_ref, slope_ref, gelu_ref, h3_ref, *refs):
    dgu_ref, out_refs, (dhid_ref, h3t_ref) = refs[0], refs[1:3], refs[3:]
    for block in range(4):
        low = 512 * block
        spot = block % 2
        dhid_ref[spot] = dot_right_t(dm_ref[...], wd_ref[8 * block : 8 * block + 8].reshape(512, 640))

        def spread(rows, low=low, spot=spot):
            grad = dhid_ref[spot, rows, :]
            dgu_ref[0, rows, low : low + 512] = (
                grad * slope_ref[rows, low : low + 512].astype(jnp.float32)
            ).astype(BF)
            dgu_ref[1, rows, low : low + 512] = (
                grad * gelu_ref[rows, low : low + 512].astype(jnp.float32)
            ).astype(BF)

        for start in range(0, 512, 16):
            spread(slice(start, start + 16))
    h3t_ref[...] = h3_ref[...].T
    for far in (1, 0):
        side = lax.rem(coords_ref[3] + far, 2)
        for block in range(4):
            low = 512 * block
            grad = dot(h3t_ref[...], dgu_ref[side, :, low : low + 512]).astype(BF)
            for spot in range(16):
                group, one, two = spot // 4, (spot // 2) % 2, spot % 2
                out_refs[far][group, one, two, :, low : low + 512] = grad[
                    40 * spot : 40 * spot + 40
                ]


def middle_backward(
    coords_ref, dgu_ref, mid_ref, branch_ref, cot_ref, gains_ref, perm_ref, own_ref, far_ref,
    dmid_ref, da_ref, gain_ref, rel_ref, plain_ref,
):
    core = coords_ref[3]
    for low in (0, 256):
        rows = slice(low, low + 256)
        total = dot_right_t(dgu_ref[core, rows, :], own_ref[...])
        total = total + dot_right_t(dgu_ref[1 - core, rows, :], far_ref[...])
        rel_ref[rows, :] = total.astype(BF)
    plain_ref[...] = dot_right_t(rel_ref[...], perm_ref[...])
    gain_one, gain_two = 1.0 + gains_ref[1:2, :], 1.0 + gains_ref[2:3, :]

    def pull(rows, carry):
        pulled, term_two = pull_norm(mid_ref[rows, :], gain_two, plain_ref[rows, :])
        grad = cot_ref[rows, :].astype(jnp.float32) + pulled
        dmid_ref[rows, :] = grad
        pulled, term_one = pull_norm(branch_ref[rows, :], gain_one, grad)
        da_ref[rows, :] = pulled.astype(BF)
        return carry[0] + fold_rows(term_one), carry[1] + fold_rows(term_two)

    zero = jnp.zeros((8, 640), jnp.float32)
    gain_ref[0], gain_ref[1] = chunks(512, 32, pull, (zero, zero))


def attention_backward(
    coords_ref, da_ref, wo_ref, o_ref, prob_ref, qn_ref, kn_ref, vb_ref, q_ref, kv_ref, gains_ref,
    dqkv_ref, gain_ref, dwo_ref, do_ref, dqn_ref, dkn_ref, dv_ref, ds_ref, lifted_ref,
):
    for head in range(4):
        block = wo_ref[8 * head : 8 * head + 8].reshape(256, 640)
        do_ref[head] = dot_right_t(da_ref[...], block).astype(BF)
        grad = dot_left_t(o_ref[head], da_ref[...])
        dwo_ref[8 * head : 8 * head + 8] = grad.astype(BF).reshape(8, 32, 640)
    dkn_ref[...] = jnp.zeros_like(dkn_ref)
    dv_ref[...] = jnp.zeros_like(dv_ref)
    for block, (low, high) in enumerate(KEY_SPANS):
        rows, span = slice(128 * block, 128 * block + 128), high - low
        lifted_ref[:, 0:span] = dot_right_t(do_ref[:, rows, :].reshape(512, 256), vb_ref[low:high, :])

        def soften(part, carry, block=block, span=span):
            head, near = part.start // 128, 128 * block + part.start % 128
            near = slice(near, near + 32)
            delta = jnp.sum(
                do_ref[head, near, :].astype(jnp.float32) * o_ref[head, near, :].astype(jnp.float32),
                axis=-1,
                keepdims=True,
            )
            soft = prob_ref[block, part, 0:span].astype(jnp.float32)
            ds_ref[part, 0:span] = (soft * (lifted_ref[part, 0:span] - delta) * SCALE).astype(BF)
            return carry

        chunks(512, 32, soften, 0)
        all_ds = ds_ref[:, 0:span]
        all_rows = qn_ref[:, rows, :].reshape(512, 256)
        dqn_ref[:, rows, :] = dot(all_ds, kn_ref[low:high, :]).reshape(4, 128, 256)
        dkn_ref[low:high, :] += dot_left_t(all_ds, all_rows)
        dv_ref[low:high, :] += dot_left_t(
            prob_ref[block, :, 0:span], do_ref[:, rows, :].reshape(512, 256)
        )
    query_gain, key_gain = 1.0 + gains_ref[4:5, 0:256], 1.0 + gains_ref[5:6, 0:256]

    def pull(rows, carry):
        query_sum, key_sum = carry
        for head in range(4):
            pulled, term = pull_norm(q_ref[head, rows, :], query_gain, dqn_ref[head, rows, :])
            dqkv_ref[head // 2, rows, 256 * (head % 2) : 256 * (head % 2) + 256] = pulled.astype(BF)
            query_sum = query_sum + fold_rows(term)
        pulled, term = pull_norm(kv_ref[0, rows, :], key_gain, dkn_ref[rows, :])
        dqkv_ref[0, rows, 512:768] = pulled.astype(BF)
        dqkv_ref[1, rows, 512:768] = dv_ref[rows, :].astype(BF)
        return query_sum, key_sum + fold_rows(term)

    zero = jnp.zeros((8, 256), jnp.float32)
    gain_ref[0], gain_ref[1] = chunks(512, 32, pull, (zero, zero))


def input_backward(
    coords_ref, dqkv_ref, h1_ref, dwo_ref, tokens_ref, dmid_ref, perm_ref, gains_ref, gain_mid_ref,
    gain_head_ref, gain_down_ref, own_ref, far_ref, input_ref, *refs
):
    out_refs, (rel_ref, plain_ref, h1t_ref) = refs[:2], refs[2:]
    core = coords_ref[3]
    total = dot_right_t(dqkv_ref[core], own_ref[...]) + dot_right_t(dqkv_ref[1 - core], far_ref[...])
    rel_ref[...] = total.astype(BF)
    h1t_ref[...] = h1_ref[...].T
    plain_ref[...] = dot_right_t(rel_ref[...], perm_ref[...])
    gain_zero = 1.0 + gains_ref[0:1, :]

    def pull(rows, carry):
        pulled, term = pull_norm(tokens_ref[rows, :].astype(jnp.float32), gain_zero, plain_ref[rows, :])
        input_ref[rows, :] = dmid_ref[rows, :] + pulled
        return carry + fold_rows(term)

    sums = [chunks(512, 32, pull, jnp.zeros((8, 640), jnp.float32))]
    sums += [gain_mid_ref[0], gain_mid_ref[1], gain_down_ref[...]]
    lines = [jnp.sum(part, axis=0, keepdims=True) for part in sums]
    for part in range(2):
        line = jnp.sum(gain_head_ref[part], axis=0, keepdims=True)
        lines.append(jnp.concatenate([line, jnp.zeros((1, 384), jnp.float32)], axis=1))
    lines.append(jnp.zeros((2, 640), jnp.float32))
    gain_block = jnp.concatenate(lines, axis=0).astype(BF)
    for far, group, one, two, place in slots(coords_ref):
        out_refs[far][group, one, two, 0:32, 768:1408] = dwo_ref[place]
        out_refs[far][group, one, two, 32:40, 768:1408] = gain_block
    for far in range(2):
        side = lax.rem(core + far, 2)
        for part in range(3):
            low = 256 * part
            grad = dot(h1t_ref[...], dqkv_ref[side, :, low : low + 256]).astype(BF)
            for spot in range(16):
                group, one, two = spot // 4, (spot // 2) % 2, spot % 2
                out_refs[far][group, one, two, :, low : low + 256] = grad[
                    40 * spot : 40 * spot + 40
                ]


def call(kernel, coords, inputs, outs, scratch=(), megabytes=32, cost=(1, 1), anys=0):
    whole = pl.BlockSpec(memory_space=pltpu.VMEM)
    return pl.pallas_call(
        kernel,
        out_shape=outs,
        in_specs=[pl.BlockSpec(memory_space=pltpu.SMEM)] + [whole] * len(inputs),
        out_specs=jax.tree.map(lambda _: whole, outs),
        scratch_shapes=list(scratch),
        cost_estimate=pl.CostEstimate(
            flops=int(cost[0] * COST * 1e9), bytes_accessed=int(cost[1] * BYTES), transcendentals=0
        ),
        compiler_params=pltpu.CompilerParams(vmem_limit_bytes=megabytes * 1024 * 1024),
    )(coords, *inputs)


def rel_table():
    table = np.zeros((32, 1, 640), np.int32)
    for place in range(32):
        z, y, x, _ = np.unravel_index(place, DIMS)
        for group in range(4):
            for one in range(2):
                for two in range(2):
                    gap = gap_of(group, one, two)
                    chip = (((z + gap[0]) % 4) * 2 + (y + gap[1]) % 2) * 2 + (x + gap[2]) % 2
                    low = 160 * group + 80 * one + 40 * two
                    table[place, 0, low : low + 40] = 40 * chip + np.arange(40)
    return table


def shape(*sizes, kind=BF):
    return jax.ShapeDtypeStruct(sizes, kind)


def join(*values):
    return lax.optimization_barrier(values)


def narrow(left, right):
    return (wide(left) + wide(right)).astype(BF)


def diagonal(values):
    pairs = []
    for place in range(int(np.prod(DIMS))):
        spot = list(np.unravel_index(place, DIMS))
        spot[1], spot[2] = (spot[1] + 1) % DIMS[1], (spot[2] + 1) % DIMS[2]
        pairs.append((place, int(np.ravel_multi_index(spot, DIMS))))
    with jax.named_scope("xy"):
        return lax.ppermute(values, "dp", pairs)


def scatter_across(keep, got):
    return shift(narrow(keep[1], got[1]), 1, 1), shift(narrow(keep[3], got[3]), 2, 1)


def scatter_sums(keep, got, far_a, far_b):
    sum_a = wide(keep[0]) + wide(got[0]) + wide(far_a)
    sum_b = wide(keep[2]) + wide(got[2]) + wide(far_b)
    return sum_a[0], sum_b[0], sum_a[1].astype(BF), sum_b[1].astype(BF)


def scatter_pair(keep, got, far_a, far_b):
    first, second, side_a, side_b = scatter_sums(keep, got, far_a, far_b)
    return first, second, shift(side_a, 2, 1), shift(side_b, 1, 1)


def scatter_along(sum_a, sum_b, side_a, side_b):
    last_a = sum_a + wide(side_a)
    last_b = sum_b + wide(side_b)
    return last_a[0], [last_b[0].astype(BF), last_a[1].astype(BF), last_b[1].astype(BF)]


def scatter_end(own, *others):
    for other in others:
        own = own + wide(other)
    return own


def block_fast(tokens, segment_ids, cotangent, weights, update_gateup):
    query_round, keyval_round, output_round, gateup_round, down_round, gains, heads = weights
    f32 = jnp.float32
    along, upward, sideways, core = own_coords()
    place = lax.axis_index("dp")
    coords = jnp.stack([along, upward, sideways, core]).astype(jnp.int32)
    index = lax.dynamic_index_in_dim(jnp.asarray(rel_table()), place, keepdims=False)
    tokens, cotangent = tokens.reshape(512, 640), cotangent.reshape(512, 640)
    segcol = segment_ids.reshape(512, 1)

    low = jnp.concatenate([query_round[:, :512], keyval_round[:, :256], gateup_round[:, 0]], axis=1)
    high = jnp.concatenate([query_round[:, 512:], keyval_round[:, 256:], gateup_round[:, 1]], axis=1)
    away, keep = swap_halves(core, low, high)
    got = shift(away, 3, 1)
    both = jnp.concatenate([jnp.where(core == 0, keep, got), jnp.where(core == 0, got, keep)], axis=0)
    spread = jnp.zeros((8, 640), BF)
    spread = lax.dynamic_update_slice(spread, gains, (0, place * gains.shape[1]))
    spread = lax.dynamic_update_slice(spread, heads, (4, place * heads.shape[1]))
    block_a = jnp.concatenate([both[:, :768], jnp.concatenate([output_round, spread], axis=0)], axis=1)
    block_g = both[:, 768:]

    near_a = gather_along(block_a)
    near_a, block_w, block_g = join(near_a, down_round, block_g)
    first, second = jnp.stack([near_a[0], near_a[2]]), jnp.stack([near_a[1], near_a[3]])
    first, second, block_w, block_g = join(first, second, block_w, block_g)
    pairs_a = [jnp.stack([first, shift(first, 2, 1)]), jnp.stack([second, shift(second, 1, 1)])]
    near_w = gather_along(block_w)
    pairs_a, near_w, block_g = join(pairs_a, near_w, block_g)
    mine_a = gather_across(*pairs_a)
    near_g = gather_along(block_g)
    pairs_w = gather_pair(near_w)
    mine_a, near_g = join(mine_a, near_g)
    pieces_a = gather_core(mine_a)
    pairs_g = gather_pair(near_g)
    pairs_g, pairs_w = join(pairs_g, pairs_w)
    mine_g = gather_across(*pairs_g)
    early_g = [shift(pair, 3, 1) for pair in pairs_g]
    h1, q, kv, qn, kn, vb, wo, gains_full, perm, own_qkv, far_qkv = call(
        project_forward,
        coords,
        [index, tokens, *pieces_a],
        [
            shape(512, 640), shape(4, 512, 256, kind=f32), shape(2, 512, 256, kind=f32),
            shape(4, 512, 256), shape(512, 256), shape(512, 256),
            shape(32, 32, 640), shape(8, 640, kind=f32), shape(640, 640), shape(640, 768), shape(640, 768),
        ],
        [pltpu.VMEM((512, 640), BF)],
        12,
        (5, 20),
    )
    qn, pairs_w = join(qn, pairs_w)
    mine_w = gather_across(*pairs_w)
    early_w = [shift(pair, 3, 1) for pair in pairs_w]
    prob, o, branch, mid, h3 = call(
        attention_forward,
        coords,
        [tokens, segment_ids, segcol, qn, kn, vb, wo, gains_full, perm],
        [
            shape(4, 512, 384), shape(4, 512, 256), shape(512, 640, kind=f32),
            shape(512, 640, kind=f32), shape(512, 640),
        ],
        [pltpu.VMEM((512, 640), BF), pltpu.VMEM((128, 384), f32), pltpu.VMEM((512, 384), f32)],
        12,
        (5, 20),
    )
    mine_g, h3, early_g = join(mine_g, h3, early_g)
    far_g = [early_g[0], shift(mine_g[1], 3, 1), early_g[1], shift(mine_g[3], 3, 1)]
    own, own_gu = call(
        gateup_own,
        coords,
        [h3, *mine_g],
        [shape(512, 2048, kind=f32), shape(640, 2048)],
        [],
        12,
        (6, 20),
    )
    far_g, own = join(far_g, own)
    slope, gelu, hidden, far_gu = call(
        gateup_forward,
        coords,
        [h3, own, *far_g],
        [shape(512, 2048)] * 3 + [shape(640, 2048)],
        [pltpu.VMEM((2, 512, 512), f32)],
        12,
        (3, 10),
    )
    hidden, mine_w = join(hidden, mine_w)
    pieces_w = mine_w + [early_w[0], shift(mine_w[1], 3, 1), early_w[1], shift(mine_w[3], 3, 1)]
    result, dm, gain_down, wd, keep_w, send_w = call(
        down_both,
        coords,
        [hidden, mid, cotangent, gains_full, *pieces_w],
        [shape(512, 640), shape(512, 640), shape(8, 640, kind=f32), shape(32, 64, 640)]
        + [shape(4, 4, 64, 640)] * 2,
        [pltpu.VMEM((512, 640), f32), pltpu.VMEM((32, 64, 640), BF)],
        12,
        (6, 20),
    )
    got_w = shift(send_w, 3, 1)
    dgu, keep_g, send_g = call(
        gateup_backward,
        coords,
        [dm, wd, slope, gelu, h3],
        [shape(2, 512, 2048)] + [shape(4, 2, 2, 40, 2048)] * 2,
        [pltpu.VMEM((2, 512, 512), f32), pltpu.VMEM((640, 512), BF)],
        12,
        (8, 20),
    )
    dgu, got_w, send_g = join(dgu, got_w, send_g)
    near_w, far_w, across_w = [narrow(keep_w[step], got_w[step]) for step in (1, 3, 2)]
    near_w = shift(near_w, 0, 1)
    got_g = shift(send_g, 3, 1)
    dmid, da, gain_mid = call(
        middle_backward,
        coords,
        [dgu, mid, branch, cotangent, gains_full, perm, own_gu, far_gu],
        [shape(512, 640, kind=f32), shape(512, 640), shape(2, 8, 640, kind=f32)],
        [pltpu.VMEM((512, 640), BF), pltpu.VMEM((512, 640), f32)],
        12,
        (8, 20),
    )
    da, got_g, near_w, far_w = join(da, got_g, near_w, far_w)
    far_g = scatter_across(keep_g, got_g)
    far_w = shift(far_w, 0, 3)
    dqkv, gain_head, dwo = call(
        attention_backward,
        coords,
        [da, wo, o, prob, qn, kn, vb, q, kv, gains_full],
        [shape(2, 512, 768), shape(2, 8, 256, kind=f32), shape(32, 32, 640)],
        [
            pltpu.VMEM((4, 512, 256), BF),
            pltpu.VMEM((4, 512, 256), f32), pltpu.VMEM((512, 256), f32), pltpu.VMEM((512, 256), f32),
            pltpu.VMEM((512, 384), BF), pltpu.VMEM((512, 384), f32),
        ],
        12,
        (6, 20),
    )
    dqkv, far_w, across_w = join(dqkv, far_w, across_w)
    across_w = shift(across_w, 0, 2)
    input_grad, keep_a, send_a = call(
        input_backward,
        coords,
        [dqkv, h1, dwo, tokens, dmid, perm, gains_full, gain_mid, gain_head, gain_down, own_qkv, far_qkv],
        [shape(512, 640, kind=f32)] + [shape(4, 2, 2, 40, 1408)] * 2,
        [pltpu.VMEM((512, 640), BF), pltpu.VMEM((512, 640), f32), pltpu.VMEM((640, 512), BF)],
        12,
        (6, 20),
    )
    send_a, far_g = join(send_a, far_g)
    got_a = shift(send_a, 3, 1)
    side_g = scatter_pair(keep_g, got_g, *far_g)
    got_a, side_g = join(got_a, side_g)
    first, second = narrow(keep_a[1], got_a[1]), narrow(keep_a[3], got_a[3])
    first, second, side_g = join(first, second, side_g)
    far_a = shift(first, 1, 1), shift(second, 2, 1)
    own_g, along_g = scatter_along(*side_g)
    ends_g = [shift(along_g[0], 0, 1), shift(along_g[2], 0, 3)]
    far_a, ends_g, across_g, across_w = join(far_a, ends_g, along_g[1], across_w)
    first, second, *side_a = scatter_sums(keep_a, got_a, *far_a)
    side_a, across_g = join(side_a, across_g)
    side_a = shift(side_a[0], 2, 1), shift(side_a[1], 1, 1)
    across_g = shift(across_g, 0, 2)
    plane = scatter_end(wide(keep_w[0]) + wide(got_w[0]), near_w, far_w, across_w)
    sent = plane.astype(BF)
    plane_w = [shift(sent[1], 2, 1), shift(sent[2], 1, 1), diagonal(sent[3])]
    side_a, across_g = join(side_a, across_g)
    own_a, along_a = scatter_along(first, second, *side_a)
    along_a = [shift(part, 0, step + 1) for step, part in enumerate(along_a)]
    gateup_sum = scatter_end(own_g, across_g, *ends_g)

    def own_rows(both):
        away, keep = swap_halves(core, both[:20], both[20:])
        got = shift(away, 3, 1)
        return jnp.where(core == 0, keep, got), jnp.where(core == 0, got, keep)

    low, high = own_rows(gateup_sum)
    gateup_grad = with_layout_constraint(jnp.stack([low, high], axis=1), Layout((0, 1, 2)))
    gateup_done = (gateup_grad, *update_gateup(gateup_grad))
    along_a, gateup_done, plane_w = join(along_a, gateup_done, plane_w)
    down_grad = scatter_end(plane[0], *plane_w)
    rest = scatter_end(own_a, *along_a)
    output_grad = rest[:32, 768:]
    norm_grad = lax.dynamic_slice(rest[32:36, 768:], (0, place * 20), (4, 20))
    qknorm_grad = lax.dynamic_slice(rest[36:38, 768:], (0, place * 8), (2, 8))

    low, high = own_rows(rest[:, :768])
    query_grad = jnp.concatenate([low[:, :512], high[:, :512]], axis=1)
    keyval_grad = jnp.concatenate([low[:, 512:], high[:, 512:]], axis=1)
    grads = (query_grad, keyval_grad, output_grad, gateup_done[0], down_grad, norm_grad, qknorm_grad)
    return result[None], input_grad[None], grads, gateup_done[1:]


def norm_apply(values, gain_vector):
    inverse = lax.rsqrt(jnp.mean(values * values, axis=-1, keepdims=True) + norm_epsilon)
    return values * inverse * (1.0 + gain_vector)


def gelu_product(gate_part, up_part):
    return jax.nn.gelu(gate_part, approximate=True) * up_part


def block_scores(query_normed, key_normed, segments, row_start, row_stop, score_scale):
    positions = jnp.arange(row_stop)
    same_doc = segments[row_start:row_stop, None] == segments[None, :row_stop]
    causal = positions[None, :] <= positions[row_start:row_stop, None]
    allowed = (same_doc & causal)[None]
    scores = (
        jnp.einsum("qhd,kd->hqk", query_normed, key_normed, preferred_element_type=jnp.float32)
        * score_scale
    )
    return (jnp.where(allowed, scores, -1e30), allowed)


def attend_forward(query_normed, key_normed, value_round, segments, score_scale):
    length = query_normed.shape[0]
    block_rows = min(512, length)
    masked, allowed = block_scores(query_normed, key_normed, segments, 0, block_rows, score_scale)
    row_max = jnp.max(masked, axis=-1, keepdims=True)
    row_total = jnp.sum(jnp.where(allowed, jnp.exp(masked - row_max), 0.0), axis=-1, keepdims=True)
    log_total = row_max + jnp.log(row_total)
    soft_round = jnp.where(allowed, jnp.exp(masked - log_total), 0.0).astype(jnp.bfloat16)
    attended_block = jnp.einsum(
        "hqk,kd->qhd", soft_round, value_round, preferred_element_type=jnp.float32
    )
    attended_parts = attended_block.astype(jnp.bfloat16)
    total_parts = log_total[:, :, 0]
    return (attended_parts, total_parts)


def attend_backward(
    query_normed,
    key_normed,
    value_round,
    segments,
    log_totals,
    attended,
    grad_attended,
    score_scale,
):
    length = query_normed.shape[0]
    head_dim = key_normed.shape[1]
    block_rows = min(512, length)
    row_delta = jnp.sum(grad_attended.astype(jnp.float32) * attended.astype(jnp.float32), axis=-1)
    grad_key_sum = jnp.zeros((length, head_dim), jnp.float32)
    grad_value_sum = jnp.zeros((length, head_dim), jnp.float32)
    masked, allowed = block_scores(query_normed, key_normed, segments, 0, block_rows, score_scale)
    soft_weights = jnp.where(allowed, jnp.exp(masked - log_totals[:, 0:block_rows, None]), 0.0)
    soft_round = soft_weights.astype(jnp.bfloat16)
    grad_value_sum = grad_value_sum.at[:block_rows].add(
        jnp.einsum("hqk,qhd->kd", soft_round, grad_attended, preferred_element_type=jnp.float32)
    )
    grad_soft = jnp.einsum(
        "qhd,kd->hqk", grad_attended, value_round, preferred_element_type=jnp.float32
    )
    delta_block = row_delta.T[:, :, None]
    grad_scores = (soft_weights * (grad_soft - delta_block) * score_scale).astype(jnp.bfloat16)
    grad_query_parts = jnp.einsum(
        "hqk,kd->qhd", grad_scores, key_normed, preferred_element_type=jnp.float32
    )
    grad_key_sum = grad_key_sum.at[:block_rows].add(
        jnp.einsum("hqk,qhd->kd", grad_scores, query_normed, preferred_element_type=jnp.float32)
    )
    return (grad_query_parts, grad_key_sum, grad_value_sum)


def adam_update(parameter, gradient, first_moment, second_moment, decay_value):
    first_new = beta_one * first_moment + (1.0 - beta_one) * gradient
    second_new = beta_two * second_moment + (1.0 - beta_two) * gradient * gradient
    first_hat = first_new / (1.0 - beta_one**STEP)
    second_hat = second_new / (1.0 - beta_two**STEP)
    parameter_new = (
        parameter
        - learn_rate * first_hat / (jnp.sqrt(second_hat) + adam_epsilon)
        - learn_rate * decay_value * parameter
    )
    return (parameter_new, first_new, second_new)


def block_plain(tokens, segment_ids, cotangent, weights, update_gateup):
    query_full, keyval_full, output_full, gateup_full, down_full, main_gains, head_gains = gather_plain(*weights)
    seq_count, length, model_width = tokens.shape
    row_count = seq_count * length
    head_dim = head_gains.shape[1]
    head_count = query_full.shape[1] // head_dim
    hidden_units = gateup_full.shape[1] // 2
    score_scale = head_dim ** (-0.5)
    inputs = tokens.reshape(row_count, model_width).astype(jnp.float32)
    normed_in = norm_apply(inputs, main_gains[0]).astype(jnp.bfloat16)
    queries = jnp.dot(normed_in, query_full, preferred_element_type=jnp.float32).reshape(
        row_count, head_count, head_dim
    )
    keyvals = jnp.dot(normed_in, keyval_full, preferred_element_type=jnp.float32)
    key_rows = keyvals[:, :head_dim]
    value_rows = keyvals[:, head_dim:]
    query_normed = norm_apply(queries, head_gains[0]).astype(jnp.bfloat16)
    key_normed = norm_apply(key_rows, head_gains[1]).astype(jnp.bfloat16)
    value_round = value_rows.astype(jnp.bfloat16)
    seq_index = 0
    attended_seq, totals_seq = attend_forward(
        query_normed, key_normed, value_round, segment_ids[seq_index], score_scale
    )
    total_parts = [totals_seq]
    attended_flat = attended_seq.reshape(row_count, head_count * head_dim)
    branch = jnp.dot(attended_flat, output_full, preferred_element_type=jnp.float32)
    middle = inputs + norm_apply(branch, main_gains[1])
    normed_mid = norm_apply(middle, main_gains[2]).astype(jnp.bfloat16)
    gate_up = jnp.dot(
        normed_mid,
        gateup_full,
        preferred_element_type=jnp.float32,
    )
    gate_part = gate_up[:, :hidden_units]
    up_part = gate_up[:, hidden_units:]
    hidden = gelu_product(gate_part, up_part).astype(jnp.bfloat16)
    down_out = jnp.dot(hidden, down_full, preferred_element_type=jnp.float32)
    result = (middle + norm_apply(down_out, main_gains[3])).astype(jnp.bfloat16)
    query_back, keyval_back, output_back, gateup_back, down_back = (
        query_full,
        keyval_full,
        output_full,
        gateup_full,
        down_full,
    )
    gateup_flat = gateup_back
    grad_out = cotangent.reshape(row_count, model_width).astype(jnp.float32)
    _, pull_back = jax.vjp(norm_apply, down_out, main_gains[3])
    grad_down_out, grad_gain_three = pull_back(grad_out)
    grad_down_round = grad_down_out.astype(jnp.bfloat16)
    grad_down = jnp.dot(hidden.T, grad_down_round, preferred_element_type=jnp.float32)
    grad_hidden = jnp.dot(grad_down_round, down_back.T, preferred_element_type=jnp.float32)
    _, pull_back = jax.vjp(gelu_product, gate_part, up_part)
    grad_gate, grad_up = pull_back(grad_hidden)
    grad_gate_up = jnp.concatenate([grad_gate, grad_up], axis=1).astype(jnp.bfloat16)
    grad_gateup = jnp.dot(normed_mid.T, grad_gate_up, preferred_element_type=jnp.float32)
    grad_normed_mid = jnp.dot(grad_gate_up, gateup_flat.T, preferred_element_type=jnp.float32)
    _, pull_back = jax.vjp(norm_apply, middle, main_gains[2])
    grad_mid_norm, grad_gain_two = pull_back(grad_normed_mid)
    grad_middle = grad_out + grad_mid_norm
    _, pull_back = jax.vjp(norm_apply, branch, main_gains[1])
    grad_branch, grad_gain_one = pull_back(grad_middle)
    grad_branch_round = grad_branch.astype(jnp.bfloat16)
    grad_output = jnp.dot(attended_flat.T, grad_branch_round, preferred_element_type=jnp.float32)
    grad_attended = (
        jnp.dot(grad_branch_round, output_back.T, preferred_element_type=jnp.float32)
        .reshape(row_count, head_count, head_dim)
        .astype(jnp.bfloat16)
    )
    seq_index = 0
    grad_query_seq, grad_key_seq, grad_value_seq = attend_backward(
        query_normed,
        key_normed,
        value_round,
        segment_ids[seq_index],
        total_parts[seq_index],
        attended_seq,
        grad_attended,
        score_scale,
    )
    _, pull_back = jax.vjp(norm_apply, queries, head_gains[0])
    grad_queries, grad_head_zero = pull_back(grad_query_seq)
    _, pull_back = jax.vjp(norm_apply, key_rows, head_gains[1])
    grad_keys, grad_head_one = pull_back(grad_key_seq)
    grad_query_round = grad_queries.reshape(row_count, head_count * head_dim).astype(jnp.bfloat16)
    grad_keyval_round = jnp.concatenate([grad_keys, grad_value_seq], axis=1).astype(jnp.bfloat16)
    grad_query = jnp.dot(normed_in.T, grad_query_round, preferred_element_type=jnp.float32)
    grad_keyval = jnp.dot(normed_in.T, grad_keyval_round, preferred_element_type=jnp.float32)
    grad_normed_in = jnp.dot(
        grad_query_round, query_back.T, preferred_element_type=jnp.float32
    ) + jnp.dot(grad_keyval_round, keyval_back.T, preferred_element_type=jnp.float32)
    _, pull_back = jax.vjp(norm_apply, inputs, main_gains[0])
    grad_in_norm, grad_gain_zero = pull_back(grad_normed_in)
    input_grad = grad_middle + grad_in_norm
    grad_gains = jnp.stack([grad_gain_zero, grad_gain_one, grad_gain_two, grad_gain_three])
    grad_heads = jnp.stack([grad_head_zero, grad_head_one])
    gradients = scatter_plain(
        grad_query, grad_keyval, grad_output, grad_gateup, grad_down, grad_gains, grad_heads
    )
    result_out = result.reshape(seq_count, length, model_width)
    input_out = input_grad.reshape(seq_count, length, model_width)
    return result_out, input_out, gradients, update_gateup(gradients[3])


def per_device(
    tokens,
    segment_ids,
    cotangent,
    query_weight,
    keyval_weight,
    output_weight,
    gateup_weight,
    down_weight,
    norm_gains,
    qknorm_gains,
    query_mean,
    keyval_mean,
    output_mean,
    gateup_mean,
    down_mean,
    norm_mean,
    qknorm_mean,
    query_square,
    keyval_square,
    output_square,
    gateup_square,
    down_square,
    norm_square,
    qknorm_square,
):
    query_round = query_weight.astype(jnp.bfloat16)
    keyval_round = keyval_weight.astype(jnp.bfloat16)
    output_round = output_weight.astype(jnp.bfloat16)
    gateup_round = gateup_weight.astype(jnp.bfloat16)
    down_round = down_weight.astype(jnp.bfloat16)
    gains_round = norm_gains.astype(jnp.bfloat16)
    headgain_round = qknorm_gains.astype(jnp.bfloat16)
    weights = (
        query_round, keyval_round, output_round, gateup_round, down_round, gains_round, headgain_round
    )

    def update_gateup(gradient):
        return adam_update(gateup_weight, gradient, gateup_mean, gateup_square, decay_coef)

    block = block_fast if lax.axis_size("dp") == 32 else block_plain
    result_out, input_out, gradients, gateup_done = block(
        tokens, segment_ids, cotangent, weights, update_gateup
    )
    parameters = (
        query_weight,
        keyval_weight,
        output_weight,
        gateup_weight,
        down_weight,
        norm_gains,
        qknorm_gains,
    )
    firsts = (query_mean, keyval_mean, output_mean, gateup_mean, down_mean, norm_mean, qknorm_mean)
    seconds = (
        query_square,
        keyval_square,
        output_square,
        gateup_square,
        down_square,
        norm_square,
        qknorm_square,
    )
    decays = (decay_coef, decay_coef, decay_coef, decay_coef, decay_coef, 0.0, 0.0)
    updates = [
        adam_update(
            parameters[place], gradients[place], firsts[place], seconds[place], decays[place]
        )
        if place != 3
        else gateup_done
        for place in range(7)
    ]
    news = tuple((update[0] for update in updates))
    first_news = tuple((update[1] for update in updates))
    second_news = tuple((update[2] for update in updates))
    return (result_out, input_out) + gradients + news + first_news + second_news


def solution(mesh):
    in_specs = (
        P("dp", None, None),
        P("dp", None),
        P("dp", None, None),
        P("dp", None),
        P("dp", None),
        P("dp", None),
        P("dp", None, None),
        P("dp", None),
        P(None, "dp"),
        P(None, "dp"),
        P("dp", None),
        P("dp", None),
        P("dp", None),
        P("dp", None, None),
        P("dp", None),
        P(None, "dp"),
        P(None, "dp"),
        P("dp", None),
        P("dp", None),
        P("dp", None),
        P("dp", None, None),
        P("dp", None),
        P(None, "dp"),
        P(None, "dp"),
    )
    out_specs = (
        P("dp", None, None),
        P("dp", None, None),
        P("dp", None),
        P("dp", None),
        P("dp", None),
        P("dp", None, None),
        P("dp", None),
        P(None, "dp"),
        P(None, "dp"),
        P("dp", None),
        P("dp", None),
        P("dp", None),
        P("dp", None, None),
        P("dp", None),
        P(None, "dp"),
        P(None, "dp"),
        P("dp", None),
        P("dp", None),
        P("dp", None),
        P("dp", None, None),
        P("dp", None),
        P(None, "dp"),
        P(None, "dp"),
        P("dp", None),
        P("dp", None),
        P("dp", None),
        P("dp", None, None),
        P("dp", None),
        P(None, "dp"),
        P(None, "dp"),
    )
    return jax.shard_map(
        per_device, mesh=mesh, in_specs=in_specs, out_specs=out_specs, check_vma=False
    )
```

```python
import jax
import jax.numpy as jnp
import numpy as np
from jax import lax
from jax.experimental import pallas as pl
from jax.experimental.layout import Layout, with_layout_constraint
from jax.experimental.pallas import tpu as pltpu
from jax.sharding import PartitionSpec as P

STEP = 3
norm_epsilon = 1e-06
beta_one = 0.9
beta_two = 0.999
learn_rate = 0.03
decay_coef = 0.1
adam_epsilon = 1e-08

DIMS = (4, 2, 2, 2)
BF = jnp.bfloat16


def shift_perm(axis, amount):
    pairs = []
    for place in range(int(np.prod(DIMS))):
        spot = list(np.unravel_index(place, DIMS))
        spot[axis] = (spot[axis] + amount) % DIMS[axis]
        pairs.append((place, int(np.ravel_multi_index(spot, DIMS))))
    return pairs


def shift(values, axis, amount):
    with jax.named_scope("zyxc"[axis] + str(amount % DIMS[axis])):
        return lax.ppermute(values, "dp", shift_perm(axis, amount))


def own_coords():
    place = lax.axis_index("dp")
    return place // 8, (place // 4) % 2, (place // 2) % 2, place % 2


def after(values, *others):
    return lax.optimization_barrier((values, others))[0]


def gather_along(block):
    return [block] + [shift(block, 0, -step) for step in (1, 2, 3)]


def gather_pair(near):
    first = jnp.stack([near[0], near[2]])
    second = jnp.stack([near[1], near[3]])
    return jnp.stack([first, shift(first, 2, 1)]), jnp.stack([second, shift(second, 1, 1)])


def gather_across(pair_a, pair_b):
    return [pair_a, shift(pair_a, 1, 1), pair_b, shift(pair_b, 2, 1)]


def gather_core(mine):
    return mine + [shift(piece, 3, 1) for piece in mine]


def wide(values):
    return values.astype(jnp.float32)


def swap_halves(core, low, high):
    return jnp.where(core == 0, high, low), jnp.where(core == 0, low, high)


def gather_plain(query_round, keyval_round, output_round, gateup_round, down_round, gains_round, headgain_round):
    gateup_full = lax.all_gather(gateup_round, "dp", axis=0, tiled=True)
    return (
        lax.all_gather(query_round, "dp", axis=0, tiled=True),
        lax.all_gather(keyval_round, "dp", axis=0, tiled=True),
        lax.all_gather(output_round, "dp", axis=0, tiled=True),
        gateup_full.reshape(gateup_full.shape[0], -1),
        lax.all_gather(down_round, "dp", axis=0, tiled=True),
        lax.all_gather(gains_round, "dp", axis=1, tiled=True).astype(jnp.float32),
        lax.all_gather(headgain_round, "dp", axis=1, tiled=True).astype(jnp.float32),
    )


def scatter_plain(grad_query, grad_keyval, grad_output, grad_gateup, grad_down, grad_gains, grad_heads):
    rows = grad_gateup.shape[0]
    return (
        lax.psum_scatter(grad_query, "dp", scatter_dimension=0, tiled=True),
        lax.psum_scatter(grad_keyval, "dp", scatter_dimension=0, tiled=True),
        lax.psum_scatter(grad_output, "dp", scatter_dimension=0, tiled=True),
        lax.psum_scatter(grad_gateup.reshape(rows, 2, -1), "dp", scatter_dimension=0, tiled=True),
        lax.psum_scatter(grad_down, "dp", scatter_dimension=0, tiled=True),
        lax.psum_scatter(grad_gains, "dp", scatter_dimension=1, tiled=True),
        lax.psum_scatter(grad_heads, "dp", scatter_dimension=1, tiled=True),
    )


BYTES = 1e6
COST = 1.0
HALF = 1024 // 2
SCALE = 256 ** (-0.5)
KEY_SPANS = ((0, 128), (0, 256), (0, 384), (128, 512))
TANH_SLOPE = (2.0 / np.pi) ** 0.5
TANH_CUBE = 0.044715


def dot(left, right):
    return jnp.dot(left, right, preferred_element_type=jnp.float32)


def dot_right_t(left, right):
    return lax.dot_general(left, right, (((1,), (1,)), ((), ())), preferred_element_type=jnp.float32)


def dot_left_t(left, right):
    return lax.dot_general(left, right, (((0,), (0,)), ((), ())), preferred_element_type=jnp.float32)


def inverse_rms(values):
    return lax.rsqrt(jnp.mean(values * values, axis=-1, keepdims=True) + norm_epsilon)


def pull_norm(values, gain_plus, grad):
    inverse = inverse_rms(values)
    unit = values * inverse
    scaled = grad * gain_plus
    return inverse * (scaled - unit * jnp.mean(scaled * unit, axis=-1, keepdims=True)), grad * unit


def fold_rows(values):
    rows, columns = values.shape
    return jnp.sum(values.reshape(rows // 8, 8, columns), axis=0)


def chunks(count, size, body, carry):
    for low in range(0, count, size):
        carry = body(slice(low, low + size), carry)
    return carry


def group_rows(piece_ref, low, high):
    return piece_ref[:, :, :, low:high].reshape(160, high - low)


def chip_at(coords_ref, gap):
    along = lax.rem(coords_ref[0] + gap[0], 4)
    upward = lax.rem(coords_ref[1] + gap[1], 2)
    sideways = lax.rem(coords_ref[2] + gap[2], 2)
    return (along * 2 + upward) * 2 + sideways


def gap_of(group, one, two):
    return (2 * two, group, one) if group < 2 else (1 + 2 * two, one, group - 2)


def slots(coords_ref):
    for far in range(2):
        core = lax.rem(coords_ref[3] + far, 2)
        for group in range(4):
            for one in range(2):
                for two in range(2):
                    yield far, group, one, two, 2 * chip_at(coords_ref, gap_of(group, one, two)) + core


def place_rows(out_ref, piece_refs, low, high):
    for group in range(4):
        for one in range(2):
            for two in range(2):
                row = 160 * group + 80 * one + 40 * two
                out_ref[row : row + 40, :] = piece_refs[group][one, two, :, low:high]


def project_forward(coords_ref, index_ref, tokens_ref, *refs):
    piece_refs, refs = refs[:8], refs[8:]
    (
        h1_ref, q_ref, kv_ref, qn_ref, kn_ref, vb_ref, wo_ref, gains_ref, perm_ref, own_ref, far_ref, plain_ref
    ) = refs
    for far, group, one, two, place in slots(coords_ref):
        wo_ref[place] = piece_refs[4 * far + group][one, two, 0:32, 768:1408]
    gains = jnp.zeros((8, 640), jnp.float32)
    for far in range(2):
        for group in range(4):
            for one in range(2):
                for two in range(2):
                    gains = gains + piece_refs[4 * far + group][one, two, 32:40, 768:1408].astype(jnp.float32)
    gains_ref[...] = gains
    core = coords_ref[3]

    def make_perm(rows, carry):
        place = lax.broadcasted_iota(jnp.int32, (64, 640), 0) + rows.start
        perm_ref[rows, :] = jnp.where(place == index_ref[...], 1.0, 0.0).astype(BF)
        return carry

    chunks(640, 64, make_perm, 0)
    gain_zero = 1.0 + gains_ref[0:1, :]

    def norm_in(rows, carry):
        values = tokens_ref[rows, :].astype(jnp.float32)
        plain_ref[rows, :] = (values * inverse_rms(values) * gain_zero).astype(BF)
        return carry

    chunks(512, 32, norm_in, 0)
    h1_ref[...] = dot(plain_ref[...], perm_ref[...]).astype(BF)
    for far, weight_ref in enumerate((own_ref, far_ref)):
        place_rows(weight_ref, piece_refs[4 * far : 4 * far + 4], 0, 768)
        side = lax.rem(core + far, 2)
        for part in range(3):
            total = dot(h1_ref[...], weight_ref[:, 256 * part : 256 * part + 256])
            if part < 2:
                q_ref[2 * side + part] = total
            else:
                kv_ref[side] = total
    query_gain, key_gain = 1.0 + gains_ref[4:5, 0:256], 1.0 + gains_ref[5:6, 0:256]

    def norm_heads(rows, carry):
        for head in range(4):
            values = q_ref[head, rows, :]
            qn_ref[head, rows, :] = (values * inverse_rms(values) * query_gain).astype(BF)
        values = kv_ref[0, rows, :]
        kn_ref[rows, :] = (values * inverse_rms(values) * key_gain).astype(BF)
        vb_ref[rows, :] = kv_ref[1, rows, :].astype(BF)
        return carry

    chunks(512, 64, norm_heads, 0)


def attention_forward(
    coords_ref, tokens_ref, segrow_ref, segcol_ref, qn_ref, kn_ref, vb_ref, wo_ref, gains_ref, perm_ref,
    prob_ref, o_ref, branch_ref, mid_ref, h3_ref, plain_ref, bias_ref, score_ref,
):
    for block, (low, high) in enumerate(KEY_SPANS):
        rows, span = slice(128 * block, 128 * block + 128), high - low
        row_at = lax.broadcasted_iota(jnp.int32, (128, span), 0) + 128 * block
        key_at = lax.broadcasted_iota(jnp.int32, (128, span), 1) + low
        allowed = (segcol_ref[rows, :] == segrow_ref[:, low:high]) & (key_at <= row_at)
        bias_ref[:, 0:span] = jnp.where(allowed, 0.0, -1e30)
        score_ref[:, 0:span] = dot_right_t(qn_ref[:, rows, :].reshape(512, 256), kn_ref[low:high, :])

        def soften(part, carry, block=block, span=span):
            near = slice(part.start % 128, part.start % 128 + 32)
            scores = score_ref[part, 0:span] * SCALE + bias_ref[near, 0:span]
            powers = jnp.exp(scores - jnp.max(scores, axis=-1, keepdims=True))
            inverse = 1.0 / jnp.sum(powers, axis=-1, keepdims=True)
            prob_ref[block, part, 0:span] = (powers * inverse).astype(BF)
            return carry

        chunks(512, 32, soften, 0)
        mixed = dot(prob_ref[block, :, 0:span], vb_ref[low:high, :])
        o_ref[:, rows, :] = mixed.astype(BF).reshape(4, 128, 256)
    total = jnp.zeros((512, 640), jnp.float32)
    for head in range(4):
        total = total + dot(o_ref[head], wo_ref[8 * head : 8 * head + 8].reshape(256, 640))
    branch_ref[...] = total
    gain_one, gain_two = 1.0 + gains_ref[1:2, :], 1.0 + gains_ref[2:3, :]

    def norm_mid(rows, carry):
        values = branch_ref[rows, :]
        middle = tokens_ref[rows, :].astype(jnp.float32) + values * inverse_rms(values) * gain_one
        mid_ref[rows, :] = middle
        plain_ref[rows, :] = (middle * inverse_rms(middle) * gain_two).astype(BF)
        return carry

    chunks(512, 32, norm_mid, 0)
    h3_ref[...] = dot(plain_ref[...], perm_ref[...]).astype(BF)


def gateup_own(coords_ref, h3_ref, *refs):
    piece_refs, (own_ref, weight_ref) = refs[:4], refs[4:]
    place_rows(weight_ref, piece_refs, 0, 2048)
    for block in range(4):
        low = 512 * block
        own_ref[:, low : low + 512] = dot(h3_ref[...], weight_ref[:, low : low + 512])


def gateup_forward(coords_ref, h3_ref, own_ref, *refs):
    piece_refs, (slope_ref, gelu_ref, hidden_ref, weight_ref, far_ref) = refs[:4], refs[4:]
    first = jnp.full((16, 512), coords_ref[3]) == 0
    place_rows(weight_ref, piece_refs, 0, 2048)
    for block in range(4):
        low = 512 * block
        spot = block % 2
        far_ref[spot] = dot(h3_ref[...], weight_ref[:, low : low + 512])

        def activate(rows, low=low, spot=spot):
            own, far = own_ref[rows, low : low + 512], far_ref[spot, rows, :]
            gate, up = jnp.where(first, own, far), jnp.where(first, far, own)
            square = gate * gate
            bend = jnp.tanh(gate * (TANH_SLOPE + (TANH_SLOPE * TANH_CUBE) * square))
            weight = 0.5 + 0.5 * bend
            rise = gate * (2.0 * TANH_SLOPE + (6.0 * TANH_SLOPE * TANH_CUBE) * square)
            gelu = gate * weight
            slope = weight + (weight * rise) * (1.0 - weight)
            slope_ref[rows, low : low + 512] = (slope * up).astype(BF)
            gelu_ref[rows, low : low + 512] = gelu.astype(BF)
            hidden_ref[rows, low : low + 512] = (gelu * up).astype(BF)

        for start in range(0, 512, 16):
            activate(slice(start, start + 16))


def plane_slots(coords_ref):
    for far in range(2):
        core = lax.rem(coords_ref[3] + far, 2)
        for step in range(4):
            for spot in range(4):
                yield far, step, spot, 2 * chip_at(coords_ref, (step, spot // 2, spot % 2)) + core


def down_both(coords_ref, hidden_ref, mid_ref, cot_ref, gains_ref, *refs):
    piece_refs, refs = refs[:8], refs[8:]
    (result_ref, dm_ref, gain_ref, wd_ref), refs = refs[:4], refs[4:]
    out_refs, (product_ref, natural_ref) = refs[:2], refs[2:]
    for far, group, one, two, place in slots(coords_ref):
        wd_ref[place] = piece_refs[4 * far + group][one, two]
    weights = wd_ref[...].reshape(2048, 640)
    for low in (0, 256):
        product_ref[low : low + 256, :] = dot(hidden_ref[low : low + 256, :], weights)
    gain_three = 1.0 + gains_ref[3:4, :]

    def finish(rows, carry):
        values = product_ref[rows, :]
        grad = cot_ref[rows, :].astype(jnp.float32)
        result_ref[rows, :] = (mid_ref[rows, :] + values * inverse_rms(values) * gain_three).astype(BF)
        pulled, term = pull_norm(values, gain_three, grad)
        dm_ref[rows, :] = pulled.astype(BF)
        return carry + fold_rows(term)

    gain_ref[...] = chunks(512, 16, finish, jnp.zeros((8, 640), jnp.float32))
    for block in range(8):
        grad = dot_left_t(hidden_ref[:, 256 * block : 256 * block + 256], dm_ref[...])
        natural_ref[4 * block : 4 * block + 4] = grad.astype(BF).reshape(4, 64, 640)
    for far, step, spot, place in plane_slots(coords_ref):
        out_refs[far][step, spot] = natural_ref[place]


def gateup_backward(coords_ref, dm_ref, wd_ref, slope_ref, gelu_ref, h3_ref, *refs):
    dgu_ref, out_refs, (dhid_ref, h3t_ref) = refs[0], refs[1:3], refs[3:]
    for block in range(4):
        low = 512 * block
        spot = block % 2
        dhid_ref[spot] = dot_right_t(dm_ref[...], wd_ref[8 * block : 8 * block + 8].reshape(512, 640))

        def spread(rows, low=low, spot=spot):
            grad = dhid_ref[spot, rows, :]
            dgu_ref[0, rows, low : low + 512] = (
                grad * slope_ref[rows, low : low + 512].astype(jnp.float32)
            ).astype(BF)
            dgu_ref[1, rows, low : low + 512] = (
                grad * gelu_ref[rows, low : low + 512].astype(jnp.float32)
            ).astype(BF)

        for start in range(0, 512, 16):
            spread(slice(start, start + 16))
    h3t_ref[...] = h3_ref[...].T
    for far in (1, 0):
        side = lax.rem(coords_ref[3] + far, 2)
        for block in range(4):
            low = 512 * block
            grad = dot(h3t_ref[...], dgu_ref[side, :, low : low + 512]).astype(BF)
            for spot in range(16):
                group, one, two = spot // 4, (spot // 2) % 2, spot % 2
                out_refs[far][group, one, two, :, low : low + 512] = grad[
                    40 * spot : 40 * spot + 40
                ]


def middle_backward(
    coords_ref, dgu_ref, mid_ref, branch_ref, cot_ref, gains_ref, perm_ref, own_ref, far_ref,
    dmid_ref, da_ref, gain_ref, rel_ref, plain_ref,
):
    core = coords_ref[3]
    for low in (0, 256):
        rows = slice(low, low + 256)
        total = dot_right_t(dgu_ref[core, rows, :], own_ref[...])
        total = total + dot_right_t(dgu_ref[1 - core, rows, :], far_ref[...])
        rel_ref[rows, :] = total.astype(BF)
    plain_ref[...] = dot_right_t(rel_ref[...], perm_ref[...])
    gain_one, gain_two = 1.0 + gains_ref[1:2, :], 1.0 + gains_ref[2:3, :]

    def pull(rows, carry):
        pulled, term_two = pull_norm(mid_ref[rows, :], gain_two, plain_ref[rows, :])
        grad = cot_ref[rows, :].astype(jnp.float32) + pulled
        dmid_ref[rows, :] = grad
        pulled, term_one = pull_norm(branch_ref[rows, :], gain_one, grad)
        da_ref[rows, :] = pulled.astype(BF)
        return carry[0] + fold_rows(term_one), carry[1] + fold_rows(term_two)

    zero = jnp.zeros((8, 640), jnp.float32)
    gain_ref[0], gain_ref[1] = chunks(512, 16, pull, (zero, zero))


def attention_backward(
    coords_ref, da_ref, wo_ref, o_ref, prob_ref, qn_ref, kn_ref, vb_ref, q_ref, kv_ref, gains_ref,
    dqkv_ref, gain_ref, dwo_ref, do_ref, dqn_ref, dkn_ref, dv_ref, ds_ref, lifted_ref,
):
    for head in range(4):
        block = wo_ref[8 * head : 8 * head + 8].reshape(256, 640)
        do_ref[head] = dot_right_t(da_ref[...], block).astype(BF)
        grad = dot_left_t(o_ref[head], da_ref[...])
        dwo_ref[8 * head : 8 * head + 8] = grad.astype(BF).reshape(8, 32, 640)
    dkn_ref[...] = jnp.zeros_like(dkn_ref)
    dv_ref[...] = jnp.zeros_like(dv_ref)
    for block, (low, high) in enumerate(KEY_SPANS):
        rows, span = slice(128 * block, 128 * block + 128), high - low
        lifted_ref[:, 0:span] = dot_right_t(do_ref[:, rows, :].reshape(512, 256), vb_ref[low:high, :])

        def soften(part, carry, block=block, span=span):
            head, near = part.start // 128, 128 * block + part.start % 128
            near = slice(near, near + 32)
            delta = jnp.sum(
                do_ref[head, near, :].astype(jnp.float32) * o_ref[head, near, :].astype(jnp.float32),
                axis=-1,
                keepdims=True,
            )
            soft = prob_ref[block, part, 0:span].astype(jnp.float32)
            ds_ref[part, 0:span] = (soft * (lifted_ref[part, 0:span] - delta) * SCALE).astype(BF)
            return carry

        chunks(512, 32, soften, 0)
        all_ds = ds_ref[:, 0:span]
        all_rows = qn_ref[:, rows, :].reshape(512, 256)
        dqn_ref[:, rows, :] = dot(all_ds, kn_ref[low:high, :]).reshape(4, 128, 256)
        dkn_ref[low:high, :] += dot_left_t(all_ds, all_rows)
        dv_ref[low:high, :] += dot_left_t(
            prob_ref[block, :, 0:span], do_ref[:, rows, :].reshape(512, 256)
        )
    query_gain, key_gain = 1.0 + gains_ref[4:5, 0:256], 1.0 + gains_ref[5:6, 0:256]

    def pull(rows, carry):
        query_sum, key_sum = carry
        for head in range(4):
            pulled, term = pull_norm(q_ref[head, rows, :], query_gain, dqn_ref[head, rows, :])
            dqkv_ref[head // 2, rows, 256 * (head % 2) : 256 * (head % 2) + 256] = pulled.astype(BF)
            query_sum = query_sum + fold_rows(term)
        pulled, term = pull_norm(kv_ref[0, rows, :], key_gain, dkn_ref[rows, :])
        dqkv_ref[0, rows, 512:768] = pulled.astype(BF)
        dqkv_ref[1, rows, 512:768] = dv_ref[rows, :].astype(BF)
        return query_sum, key_sum + fold_rows(term)

    zero = jnp.zeros((8, 256), jnp.float32)
    gain_ref[0], gain_ref[1] = chunks(512, 16, pull, (zero, zero))


def input_backward(
    coords_ref, dqkv_ref, h1_ref, dwo_ref, tokens_ref, dmid_ref, perm_ref, gains_ref, gain_mid_ref,
    gain_head_ref, gain_down_ref, own_ref, far_ref, input_ref, *refs
):
    out_refs, (rel_ref, plain_ref, h1t_ref) = refs[:2], refs[2:]
    core = coords_ref[3]
    total = dot_right_t(dqkv_ref[core], own_ref[...]) + dot_right_t(dqkv_ref[1 - core], far_ref[...])
    rel_ref[...] = total.astype(BF)
    h1t_ref[...] = h1_ref[...].T
    plain_ref[...] = dot_right_t(rel_ref[...], perm_ref[...])
    gain_zero = 1.0 + gains_ref[0:1, :]

    def pull(rows, carry):
        pulled, term = pull_norm(tokens_ref[rows, :].astype(jnp.float32), gain_zero, plain_ref[rows, :])
        input_ref[rows, :] = dmid_ref[rows, :] + pulled
        return carry + fold_rows(term)

    sums = [chunks(512, 32, pull, jnp.zeros((8, 640), jnp.float32))]
    sums += [gain_mid_ref[0], gain_mid_ref[1], gain_down_ref[...]]
    lines = [jnp.sum(part, axis=0, keepdims=True) for part in sums]
    for part in range(2):
        line = jnp.sum(gain_head_ref[part], axis=0, keepdims=True)
        lines.append(jnp.concatenate([line, jnp.zeros((1, 384), jnp.float32)], axis=1))
    lines.append(jnp.zeros((2, 640), jnp.float32))
    gain_block = jnp.concatenate(lines, axis=0).astype(BF)
    for far, group, one, two, place in slots(coords_ref):
        out_refs[far][group, one, two, 0:32, 768:1408] = dwo_ref[place]
        out_refs[far][group, one, two, 32:40, 768:1408] = gain_block
    for far in range(2):
        side = lax.rem(core + far, 2)
        for part in range(3):
            low = 256 * part
            grad = dot(h1t_ref[...], dqkv_ref[side, :, low : low + 256]).astype(BF)
            for spot in range(16):
                group, one, two = spot // 4, (spot // 2) % 2, spot % 2
                out_refs[far][group, one, two, :, low : low + 256] = grad[
                    40 * spot : 40 * spot + 40
                ]


def call(kernel, coords, inputs, outs, scratch=(), megabytes=32, cost=(1, 1), anys=0):
    whole = pl.BlockSpec(memory_space=pltpu.VMEM)
    return pl.pallas_call(
        kernel,
        out_shape=outs,
        in_specs=[pl.BlockSpec(memory_space=pltpu.SMEM)] + [whole] * len(inputs),
        out_specs=jax.tree.map(lambda _: whole, outs),
        scratch_shapes=list(scratch),
        cost_estimate=pl.CostEstimate(
            flops=int(cost[0] * COST * 1e9), bytes_accessed=int(cost[1] * BYTES), transcendentals=0
        ),
        compiler_params=pltpu.CompilerParams(vmem_limit_bytes=megabytes * 1024 * 1024),
    )(coords, *inputs)


def rel_table():
    table = np.zeros((32, 1, 640), np.int32)
    for place in range(32):
        z, y, x, _ = np.unravel_index(place, DIMS)
        for group in range(4):
            for one in range(2):
                for two in range(2):
                    gap = gap_of(group, one, two)
                    chip = (((z + gap[0]) % 4) * 2 + (y + gap[1]) % 2) * 2 + (x + gap[2]) % 2
                    low = 160 * group + 80 * one + 40 * two
                    table[place, 0, low : low + 40] = 40 * chip + np.arange(40)
    return table


def shape(*sizes, kind=BF):
    return jax.ShapeDtypeStruct(sizes, kind)


def join(*values):
    return lax.optimization_barrier(values)


def narrow(left, right):
    return (wide(left) + wide(right)).astype(BF)


def diagonal(values):
    pairs = []
    for place in range(int(np.prod(DIMS))):
        spot = list(np.unravel_index(place, DIMS))
        spot[1], spot[2] = (spot[1] + 1) % DIMS[1], (spot[2] + 1) % DIMS[2]
        pairs.append((place, int(np.ravel_multi_index(spot, DIMS))))
    with jax.named_scope("xy"):
        return lax.ppermute(values, "dp", pairs)


def scatter_across(keep, got):
    return shift(narrow(keep[1], got[1]), 1, 1), shift(narrow(keep[3], got[3]), 2, 1)


def scatter_sums(keep, got, far_a, far_b):
    sum_a = wide(keep[0]) + wide(got[0]) + wide(far_a)
    sum_b = wide(keep[2]) + wide(got[2]) + wide(far_b)
    return sum_a[0], sum_b[0], sum_a[1].astype(BF), sum_b[1].astype(BF)


def scatter_pair(keep, got, far_a, far_b):
    first, second, side_a, side_b = scatter_sums(keep, got, far_a, far_b)
    return first, second, shift(side_a, 2, 1), shift(side_b, 1, 1)


def scatter_along(sum_a, sum_b, side_a, side_b):
    last_a = sum_a + wide(side_a)
    last_b = sum_b + wide(side_b)
    return last_a[0], [last_b[0].astype(BF), last_a[1].astype(BF), last_b[1].astype(BF)]


def scatter_end(own, *others):
    for other in others:
        own = own + wide(other)
    return own


def block_fast(tokens, segment_ids, cotangent, weights, update_gateup):
    query_round, keyval_round, output_round, gateup_round, down_round, gains, heads = weights
    f32 = jnp.float32
    along, upward, sideways, core = own_coords()
    place = lax.axis_index("dp")
    coords = jnp.stack([along, upward, sideways, core]).astype(jnp.int32)
    index = lax.dynamic_index_in_dim(jnp.asarray(rel_table()), place, keepdims=False)
    tokens, cotangent = tokens.reshape(512, 640), cotangent.reshape(512, 640)
    segcol = segment_ids.reshape(512, 1)

    low = jnp.concatenate([query_round[:, :512], keyval_round[:, :256], gateup_round[:, 0]], axis=1)
    high = jnp.concatenate([query_round[:, 512:], keyval_round[:, 256:], gateup_round[:, 1]], axis=1)
    away, keep = swap_halves(core, low, high)
    got = shift(away, 3, 1)
    both = jnp.concatenate([jnp.where(core == 0, keep, got), jnp.where(core == 0, got, keep)], axis=0)
    spread = jnp.zeros((8, 640), BF)
    spread = lax.dynamic_update_slice(spread, gains, (0, place * gains.shape[1]))
    spread = lax.dynamic_update_slice(spread, heads, (4, place * heads.shape[1]))
    block_a = jnp.concatenate([both[:, :768], jnp.concatenate([output_round, spread], axis=0)], axis=1)
    block_g = both[:, 768:]

    near_a = gather_along(block_a)
    near_a, block_w, block_g = join(near_a, down_round, block_g)
    first, second = jnp.stack([near_a[0], near_a[2]]), jnp.stack([near_a[1], near_a[3]])
    first, second, block_w, block_g = join(first, second, block_w, block_g)
    pairs_a = [jnp.stack([first, shift(first, 2, 1)]), jnp.stack([second, shift(second, 1, 1)])]
    near_w = gather_along(block_w)
    pairs_a, near_w, block_g = join(pairs_a, near_w, block_g)
    mine_a = gather_across(*pairs_a)
    near_g = gather_along(block_g)
    pairs_w = gather_pair(near_w)
    mine_a, near_g = join(mine_a, near_g)
    pieces_a = gather_core(mine_a)
    pairs_g = gather_pair(near_g)
    pairs_g, pairs_w = join(pairs_g, pairs_w)
    mine_g = gather_across(*pairs_g)
    early_g = [shift(pair, 3, 1) for pair in pairs_g]
    h1, q, kv, qn, kn, vb, wo, gains_full, perm, own_qkv, far_qkv = call(
        project_forward,
        coords,
        [index, tokens, *pieces_a],
        [
            shape(512, 640), shape(4, 512, 256, kind=f32), shape(2, 512, 256, kind=f32),
            shape(4, 512, 256), shape(512, 256), shape(512, 256),
            shape(32, 32, 640), shape(8, 640, kind=f32), shape(640, 640), shape(640, 768), shape(640, 768),
        ],
        [pltpu.VMEM((512, 640), BF)],
        12,
        (5, 20),
    )
    qn, pairs_w = join(qn, pairs_w)
    mine_w = gather_across(*pairs_w)
    early_w = [shift(pair, 3, 1) for pair in pairs_w]
    prob, o, branch, mid, h3 = call(
        attention_forward,
        coords,
        [tokens, segment_ids, segcol, qn, kn, vb, wo, gains_full, perm],
        [
            shape(4, 512, 384), shape(4, 512, 256), shape(512, 640, kind=f32),
            shape(512, 640, kind=f32), shape(512, 640),
        ],
        [pltpu.VMEM((512, 640), BF), pltpu.VMEM((128, 384), f32), pltpu.VMEM((512, 384), f32)],
        12,
        (5, 20),
    )
    mine_g, h3, early_g = join(mine_g, h3, early_g)
    far_g = [early_g[0], shift(mine_g[1], 3, 1), early_g[1], shift(mine_g[3], 3, 1)]
    own, own_gu = call(
        gateup_own,
        coords,
        [h3, *mine_g],
        [shape(512, 2048, kind=f32), shape(640, 2048)],
        [],
        12,
        (6, 20),
    )
    far_g, own = join(far_g, own)
    slope, gelu, hidden, far_gu = call(
        gateup_forward,
        coords,
        [h3, own, *far_g],
        [shape(512, 2048)] * 3 + [shape(640, 2048)],
        [pltpu.VMEM((2, 512, 512), f32)],
        12,
        (3, 10),
    )
    hidden, mine_w = join(hidden, mine_w)
    pieces_w = mine_w + [early_w[0], shift(mine_w[1], 3, 1), early_w[1], shift(mine_w[3], 3, 1)]
    result, dm, gain_down, wd, keep_w, send_w = call(
        down_both,
        coords,
        [hidden, mid, cotangent, gains_full, *pieces_w],
        [shape(512, 640), shape(512, 640), shape(8, 640, kind=f32), shape(32, 64, 640)]
        + [shape(4, 4, 64, 640)] * 2,
        [pltpu.VMEM((512, 640), f32), pltpu.VMEM((32, 64, 640), BF)],
        12,
        (6, 20),
    )
    got_w = shift(send_w, 3, 1)
    dgu, keep_g, send_g = call(
        gateup_backward,
        coords,
        [dm, wd, slope, gelu, h3],
        [shape(2, 512, 2048)] + [shape(4, 2, 2, 40, 2048)] * 2,
        [pltpu.VMEM((2, 512, 512), f32), pltpu.VMEM((640, 512), BF)],
        12,
        (8, 20),
    )
    dgu, got_w, send_g = join(dgu, got_w, send_g)
    near_w, far_w, across_w = [narrow(keep_w[step], got_w[step]) for step in (1, 3, 2)]
    near_w = shift(near_w, 0, 1)
    got_g = shift(send_g, 3, 1)
    dmid, da, gain_mid = call(
        middle_backward,
        coords,
        [dgu, mid, branch, cotangent, gains_full, perm, own_gu, far_gu],
        [shape(512, 640, kind=f32), shape(512, 640), shape(2, 8, 640, kind=f32)],
        [pltpu.VMEM((512, 640), BF), pltpu.VMEM((512, 640), f32)],
        12,
        (8, 20),
    )
    da, got_g, near_w, far_w = join(da, got_g, near_w, far_w)
    far_g = scatter_across(keep_g, got_g)
    far_w = shift(far_w, 0, 3)
    dqkv, gain_head, dwo = call(
        attention_backward,
        coords,
        [da, wo, o, prob, qn, kn, vb, q, kv, gains_full],
        [shape(2, 512, 768), shape(2, 8, 256, kind=f32), shape(32, 32, 640)],
        [
            pltpu.VMEM((4, 512, 256), BF),
            pltpu.VMEM((4, 512, 256), f32), pltpu.VMEM((512, 256), f32), pltpu.VMEM((512, 256), f32),
            pltpu.VMEM((512, 384), BF), pltpu.VMEM((512, 384), f32),
        ],
        12,
        (6, 20),
    )
    dqkv, far_w, across_w = join(dqkv, far_w, across_w)
    across_w = shift(across_w, 0, 2)
    input_grad, keep_a, send_a = call(
        input_backward,
        coords,
        [dqkv, h1, dwo, tokens, dmid, perm, gains_full, gain_mid, gain_head, gain_down, own_qkv, far_qkv],
        [shape(512, 640, kind=f32)] + [shape(4, 2, 2, 40, 1408)] * 2,
        [pltpu.VMEM((512, 640), BF), pltpu.VMEM((512, 640), f32), pltpu.VMEM((640, 512), BF)],
        12,
        (6, 20),
    )
    send_a, far_g = join(send_a, far_g)
    got_a = shift(send_a, 3, 1)
    side_g = scatter_pair(keep_g, got_g, *far_g)
    got_a, side_g = join(got_a, side_g)
    first, second = narrow(keep_a[1], got_a[1]), narrow(keep_a[3], got_a[3])
    first, second, side_g = join(first, second, side_g)
    far_a = shift(first, 1, 1), shift(second, 2, 1)
    own_g, along_g = scatter_along(*side_g)
    ends_g = [shift(along_g[0], 0, 1), shift(along_g[2], 0, 3)]
    far_a, ends_g, across_g, across_w = join(far_a, ends_g, along_g[1], across_w)
    first, second, *side_a = scatter_sums(keep_a, got_a, *far_a)
    side_a, across_g = join(side_a, across_g)
    side_a = shift(side_a[0], 2, 1), shift(side_a[1], 1, 1)
    across_g = shift(across_g, 0, 2)
    plane = scatter_end(wide(keep_w[0]) + wide(got_w[0]), near_w, far_w, across_w)
    sent = plane.astype(BF)
    plane_w = [shift(sent[1], 2, 1), shift(sent[2], 1, 1), diagonal(sent[3])]
    side_a, across_g = join(side_a, across_g)
    own_a, along_a = scatter_along(first, second, *side_a)
    along_a = [shift(part, 0, step + 1) for step, part in enumerate(along_a)]
    gateup_sum = scatter_end(own_g, across_g, *ends_g)

    def own_rows(both):
        away, keep = swap_halves(core, both[:20], both[20:])
        got = shift(away, 3, 1)
        return jnp.where(core == 0, keep, got), jnp.where(core == 0, got, keep)

    low, high = own_rows(gateup_sum)
    gateup_grad = with_layout_constraint(jnp.stack([low, high], axis=1), Layout((0, 1, 2)))
    gateup_done = (gateup_grad, *update_gateup(gateup_grad))
    along_a, gateup_done, plane_w = join(along_a, gateup_done, plane_w)
    down_grad = scatter_end(plane[0], *plane_w)
    rest = scatter_end(own_a, *along_a)
    output_grad = rest[:32, 768:]
    norm_grad = lax.dynamic_slice(rest[32:36, 768:], (0, place * 20), (4, 20))
    qknorm_grad = lax.dynamic_slice(rest[36:38, 768:], (0, place * 8), (2, 8))

    low, high = own_rows(rest[:, :768])
    query_grad = jnp.concatenate([low[:, :512], high[:, :512]], axis=1)
    keyval_grad = jnp.concatenate([low[:, 512:], high[:, 512:]], axis=1)
    grads = (query_grad, keyval_grad, output_grad, gateup_done[0], down_grad, norm_grad, qknorm_grad)
    return result[None], input_grad[None], grads, gateup_done[1:]


def norm_apply(values, gain_vector):
    inverse = lax.rsqrt(jnp.mean(values * values, axis=-1, keepdims=True) + norm_epsilon)
    return values * inverse * (1.0 + gain_vector)


def gelu_product(gate_part, up_part):
    return jax.nn.gelu(gate_part, approximate=True) * up_part


def block_scores(query_normed, key_normed, segments, row_start, row_stop, score_scale):
    positions = jnp.arange(row_stop)
    same_doc = segments[row_start:row_stop, None] == segments[None, :row_stop]
    causal = positions[None, :] <= positions[row_start:row_stop, None]
    allowed = (same_doc & causal)[None]
    scores = (
        jnp.einsum("qhd,kd->hqk", query_normed, key_normed, preferred_element_type=jnp.float32)
        * score_scale
    )
    return (jnp.where(allowed, scores, -1e30), allowed)


def attend_forward(query_normed, key_normed, value_round, segments, score_scale):
    length = query_normed.shape[0]
    block_rows = min(512, length)
    masked, allowed = block_scores(query_normed, key_normed, segments, 0, block_rows, score_scale)
    row_max = jnp.max(masked, axis=-1, keepdims=True)
    row_total = jnp.sum(jnp.where(allowed, jnp.exp(masked - row_max), 0.0), axis=-1, keepdims=True)
    log_total = row_max + jnp.log(row_total)
    soft_round = jnp.where(allowed, jnp.exp(masked - log_total), 0.0).astype(jnp.bfloat16)
    attended_block = jnp.einsum(
        "hqk,kd->qhd", soft_round, value_round, preferred_element_type=jnp.float32
    )
    attended_parts = attended_block.astype(jnp.bfloat16)
    total_parts = log_total[:, :, 0]
    return (attended_parts, total_parts)


def attend_backward(
    query_normed,
    key_normed,
    value_round,
    segments,
    log_totals,
    attended,
    grad_attended,
    score_scale,
):
    length = query_normed.shape[0]
    head_dim = key_normed.shape[1]
    block_rows = min(512, length)
    row_delta = jnp.sum(grad_attended.astype(jnp.float32) * attended.astype(jnp.float32), axis=-1)
    grad_key_sum = jnp.zeros((length, head_dim), jnp.float32)
    grad_value_sum = jnp.zeros((length, head_dim), jnp.float32)
    masked, allowed = block_scores(query_normed, key_normed, segments, 0, block_rows, score_scale)
    soft_weights = jnp.where(allowed, jnp.exp(masked - log_totals[:, 0:block_rows, None]), 0.0)
    soft_round = soft_weights.astype(jnp.bfloat16)
    grad_value_sum = grad_value_sum.at[:block_rows].add(
        jnp.einsum("hqk,qhd->kd", soft_round, grad_attended, preferred_element_type=jnp.float32)
    )
    grad_soft = jnp.einsum(
        "qhd,kd->hqk", grad_attended, value_round, preferred_element_type=jnp.float32
    )
    delta_block = row_delta.T[:, :, None]
    grad_scores = (soft_weights * (grad_soft - delta_block) * score_scale).astype(jnp.bfloat16)
    grad_query_parts = jnp.einsum(
        "hqk,kd->qhd", grad_scores, key_normed, preferred_element_type=jnp.float32
    )
    grad_key_sum = grad_key_sum.at[:block_rows].add(
        jnp.einsum("hqk,qhd->kd", grad_scores, query_normed, preferred_element_type=jnp.float32)
    )
    return (grad_query_parts, grad_key_sum, grad_value_sum)


def adam_update(parameter, gradient, first_moment, second_moment, decay_value):
    first_new = beta_one * first_moment + (1.0 - beta_one) * gradient
    second_new = beta_two * second_moment + (1.0 - beta_two) * gradient * gradient
    first_hat = first_new / (1.0 - beta_one**STEP)
    second_hat = second_new / (1.0 - beta_two**STEP)
    parameter_new = (
        parameter
        - learn_rate * first_hat / (jnp.sqrt(second_hat) + adam_epsilon)
        - learn_rate * decay_value * parameter
    )
    return (parameter_new, first_new, second_new)


def block_plain(tokens, segment_ids, cotangent, weights, update_gateup):
    query_full, keyval_full, output_full, gateup_full, down_full, main_gains, head_gains = gather_plain(*weights)
    seq_count, length, model_width = tokens.shape
    row_count = seq_count * length
    head_dim = head_gains.shape[1]
    head_count = query_full.shape[1] // head_dim
    hidden_units = gateup_full.shape[1] // 2
    score_scale = head_dim ** (-0.5)
    inputs = tokens.reshape(row_count, model_width).astype(jnp.float32)
    normed_in = norm_apply(inputs, main_gains[0]).astype(jnp.bfloat16)
    queries = jnp.dot(normed_in, query_full, preferred_element_type=jnp.float32).reshape(
        row_count, head_count, head_dim
    )
    keyvals = jnp.dot(normed_in, keyval_full, preferred_element_type=jnp.float32)
    key_rows = keyvals[:, :head_dim]
    value_rows = keyvals[:, head_dim:]
    query_normed = norm_apply(queries, head_gains[0]).astype(jnp.bfloat16)
    key_normed = norm_apply(key_rows, head_gains[1]).astype(jnp.bfloat16)
    value_round = value_rows.astype(jnp.bfloat16)
    seq_index = 0
    attended_seq, totals_seq = attend_forward(
        query_normed, key_normed, value_round, segment_ids[seq_index], score_scale
    )
    total_parts = [totals_seq]
    attended_flat = attended_seq.reshape(row_count, head_count * head_dim)
    branch = jnp.dot(attended_flat, output_full, preferred_element_type=jnp.float32)
    middle = inputs + norm_apply(branch, main_gains[1])
    normed_mid = norm_apply(middle, main_gains[2]).astype(jnp.bfloat16)
    gate_up = jnp.dot(
        normed_mid,
        gateup_full,
        preferred_element_type=jnp.float32,
    )
    gate_part = gate_up[:, :hidden_units]
    up_part = gate_up[:, hidden_units:]
    hidden = gelu_product(gate_part, up_part).astype(jnp.bfloat16)
    down_out = jnp.dot(hidden, down_full, preferred_element_type=jnp.float32)
    result = (middle + norm_apply(down_out, main_gains[3])).astype(jnp.bfloat16)
    query_back, keyval_back, output_back, gateup_back, down_back = (
        query_full,
        keyval_full,
        output_full,
        gateup_full,
        down_full,
    )
    gateup_flat = gateup_back
    grad_out = cotangent.reshape(row_count, model_width).astype(jnp.float32)
    _, pull_back = jax.vjp(norm_apply, down_out, main_gains[3])
    grad_down_out, grad_gain_three = pull_back(grad_out)
    grad_down_round = grad_down_out.astype(jnp.bfloat16)
    grad_down = jnp.dot(hidden.T, grad_down_round, preferred_element_type=jnp.float32)
    grad_hidden = jnp.dot(grad_down_round, down_back.T, preferred_element_type=jnp.float32)
    _, pull_back = jax.vjp(gelu_product, gate_part, up_part)
    grad_gate, grad_up = pull_back(grad_hidden)
    grad_gate_up = jnp.concatenate([grad_gate, grad_up], axis=1).astype(jnp.bfloat16)
    grad_gateup = jnp.dot(normed_mid.T, grad_gate_up, preferred_element_type=jnp.float32)
    grad_normed_mid = jnp.dot(grad_gate_up, gateup_flat.T, preferred_element_type=jnp.float32)
    _, pull_back = jax.vjp(norm_apply, middle, main_gains[2])
    grad_mid_norm, grad_gain_two = pull_back(grad_normed_mid)
    grad_middle = grad_out + grad_mid_norm
    _, pull_back = jax.vjp(norm_apply, branch, main_gains[1])
    grad_branch, grad_gain_one = pull_back(grad_middle)
    grad_branch_round = grad_branch.astype(jnp.bfloat16)
    grad_output = jnp.dot(attended_flat.T, grad_branch_round, preferred_element_type=jnp.float32)
    grad_attended = (
        jnp.dot(grad_branch_round, output_back.T, preferred_element_type=jnp.float32)
        .reshape(row_count, head_count, head_dim)
        .astype(jnp.bfloat16)
    )
    seq_index = 0
    grad_query_seq, grad_key_seq, grad_value_seq = attend_backward(
        query_normed,
        key_normed,
        value_round,
        segment_ids[seq_index],
        total_parts[seq_index],
        attended_seq,
        grad_attended,
        score_scale,
    )
    _, pull_back = jax.vjp(norm_apply, queries, head_gains[0])
    grad_queries, grad_head_zero = pull_back(grad_query_seq)
    _, pull_back = jax.vjp(norm_apply, key_rows, head_gains[1])
    grad_keys, grad_head_one = pull_back(grad_key_seq)
    grad_query_round = grad_queries.reshape(row_count, head_count * head_dim).astype(jnp.bfloat16)
    grad_keyval_round = jnp.concatenate([grad_keys, grad_value_seq], axis=1).astype(jnp.bfloat16)
    grad_query = jnp.dot(normed_in.T, grad_query_round, preferred_element_type=jnp.float32)
    grad_keyval = jnp.dot(normed_in.T, grad_keyval_round, preferred_element_type=jnp.float32)
    grad_normed_in = jnp.dot(
        grad_query_round, query_back.T, preferred_element_type=jnp.float32
    ) + jnp.dot(grad_keyval_round, keyval_back.T, preferred_element_type=jnp.float32)
    _, pull_back = jax.vjp(norm_apply, inputs, main_gains[0])
    grad_in_norm, grad_gain_zero = pull_back(grad_normed_in)
    input_grad = grad_middle + grad_in_norm
    grad_gains = jnp.stack([grad_gain_zero, grad_gain_one, grad_gain_two, grad_gain_three])
    grad_heads = jnp.stack([grad_head_zero, grad_head_one])
    gradients = scatter_plain(
        grad_query, grad_keyval, grad_output, grad_gateup, grad_down, grad_gains, grad_heads
    )
    result_out = result.reshape(seq_count, length, model_width)
    input_out = input_grad.reshape(seq_count, length, model_width)
    return result_out, input_out, gradients, update_gateup(gradients[3])


def per_device(
    tokens,
    segment_ids,
    cotangent,
    query_weight,
    keyval_weight,
    output_weight,
    gateup_weight,
    down_weight,
    norm_gains,
    qknorm_gains,
    query_mean,
    keyval_mean,
    output_mean,
    gateup_mean,
    down_mean,
    norm_mean,
    qknorm_mean,
    query_square,
    keyval_square,
    output_square,
    gateup_square,
    down_square,
    norm_square,
    qknorm_square,
):
    query_round = query_weight.astype(jnp.bfloat16)
    keyval_round = keyval_weight.astype(jnp.bfloat16)
    output_round = output_weight.astype(jnp.bfloat16)
    gateup_round = gateup_weight.astype(jnp.bfloat16)
    down_round = down_weight.astype(jnp.bfloat16)
    gains_round = norm_gains.astype(jnp.bfloat16)
    headgain_round = qknorm_gains.astype(jnp.bfloat16)
    weights = (
        query_round, keyval_round, output_round, gateup_round, down_round, gains_round, headgain_round
    )

    def update_gateup(gradient):
        return adam_update(gateup_weight, gradient, gateup_mean, gateup_square, decay_coef)

    block = block_fast if lax.axis_size("dp") == 32 else block_plain
    result_out, input_out, gradients, gateup_done = block(
        tokens, segment_ids, cotangent, weights, update_gateup
    )
    parameters = (
        query_weight,
        keyval_weight,
        output_weight,
        gateup_weight,
        down_weight,
        norm_gains,
        qknorm_gains,
    )
    firsts = (query_mean, keyval_mean, output_mean, gateup_mean, down_mean, norm_mean, qknorm_mean)
    seconds = (
        query_square,
        keyval_square,
        output_square,
        gateup_square,
        down_square,
        norm_square,
        qknorm_square,
    )
    decays = (decay_coef, decay_coef, decay_coef, decay_coef, decay_coef, 0.0, 0.0)
    updates = [
        adam_update(
            parameters[place], gradients[place], firsts[place], seconds[place], decays[place]
        )
        if place != 3
        else gateup_done
        for place in range(7)
    ]
    news = tuple((update[0] for update in updates))
    first_news = tuple((update[1] for update in updates))
    second_news = tuple((update[2] for update in updates))
    return (result_out, input_out) + gradients + news + first_news + second_news


def solution(mesh):
    in_specs = (
        P("dp", None, None),
        P("dp", None),
        P("dp", None, None),
        P("dp", None),
        P("dp", None),
        P("dp", None),
        P("dp", None, None),
        P("dp", None),
        P(None, "dp"),
        P(None, "dp"),
        P("dp", None),
        P("dp", None),
        P("dp", None),
        P("dp", None, None),
        P("dp", None),
        P(None, "dp"),
        P(None, "dp"),
        P("dp", None),
        P("dp", None),
        P("dp", None),
        P("dp", None, None),
        P("dp", None),
        P(None, "dp"),
        P(None, "dp"),
    )
    out_specs = (
        P("dp", None, None),
        P("dp", None, None),
        P("dp", None),
        P("dp", None),
        P("dp", None),
        P("dp", None, None),
        P("dp", None),
        P(None, "dp"),
        P(None, "dp"),
        P("dp", None),
        P("dp", None),
        P("dp", None),
        P("dp", None, None),
        P("dp", None),
        P(None, "dp"),
        P(None, "dp"),
        P("dp", None),
        P("dp", None),
        P("dp", None),
        P("dp", None, None),
        P("dp", None),
        P(None, "dp"),
        P(None, "dp"),
        P("dp", None),
        P("dp", None),
        P("dp", None),
        P("dp", None, None),
        P("dp", None),
        P(None, "dp"),
        P(None, "dp"),
    )
    return jax.shard_map(
        per_device, mesh=mesh, in_specs=in_specs, out_specs=out_specs, check_vma=False
    )
```
